128 devices in a mesh: fsdp: 16 (over x, z_lo, core), ctx: 4 (over y), tp: 2 (over z_hi).
Axes of the slice: x: 4, y: 4, z: 4 (z_hi: 2, z_lo: 2; z = z_hi * 2 + z_lo), core: 2. Of those that a mesh axis runs over, the one named last changes fastest.
Arguments:
- tokens_in: bfloat16 [8192, 2048], P(('fsdp', 'ctx')), may hold values from -16 to 16
- documents: int32 [16, 512], P('fsdp'), may hold values from 0 to 126, as said below
- routes: int32 [8192, 6], P(('fsdp', 'ctx')), may hold values from 0 to 63, all different within a row; in each aligned block of 128 rows (0 to 127, 128 to 255, ...) at most 16 rows name the same one
- attn_gain: bfloat16 [2048], P(('fsdp', 'ctx')), may hold values from 0.5 to 1.5
- query_weight: bfloat16 [2048, 3072], P(('fsdp', 'ctx'), 'tp'), may hold values from -0.125 to 0.125
- latent_down: bfloat16 [2048, 576], P(('fsdp', 'ctx')), may hold values from -0.125 to 0.125
- latent_gain: bfloat16 [512], P(('fsdp', 'ctx')), may hold values from 0.5 to 1.5
- latent_up: bfloat16 [512, 4096], P(('fsdp', 'ctx'), 'tp'), may hold values from -0.25 to 0.25
- output_weight: bfloat16 [2048, 2048], P('tp', ('fsdp', 'ctx')), may hold values from -1.5 to 1.5
- ffn_gain: bfloat16 [2048], P(('fsdp', 'ctx')), may hold values from 0.5 to 1.5
- router: bfloat16 [2048, 64], P(('fsdp', 'ctx')), may hold values from -0.0625 to 0.0625
- shared_gate: bfloat16 [2048, 2816], P(('fsdp', 'ctx'), 'tp'), may hold values from -0.125 to 0.125
- shared_up: bfloat16 [2048, 2816], P(('fsdp', 'ctx'), 'tp'), may hold values from -0.125 to 0.125
- shared_down: bfloat16 [2816, 2048], P('tp', ('fsdp', 'ctx')), may hold values from -0.109375 to 0.109375
- expert_gate: bfloat16 [64, 2048, 1408], P(('fsdp', 'ctx'), None, 'tp'), may hold values from -0.125 to 0.125
- expert_up: bfloat16 [64, 2048, 1408], P(('fsdp', 'ctx'), None, 'tp'), may hold values from -0.125 to 0.125
- expert_down: bfloat16 [64, 1408, 2048], P(('fsdp', 'ctx'), 'tp'), may hold values from -4 to 4
- cotangent: bfloat16 [8192, 2048], P(('fsdp', 'ctx')), may hold values from -16 to 16
Outputs:
- layer_out: bfloat16 [8192, 2048], P(('fsdp', 'ctx'))
- input_grad: float32 [8192, 2048], P(('fsdp', 'ctx'))
- attn_gain_grad: float32 [2048], P(('fsdp', 'ctx'))
- query_weight_grad: float32 [2048, 3072], P(('fsdp', 'ctx'), 'tp')
- latent_down_grad: float32 [2048, 576], P(('fsdp', 'ctx'))
- latent_gain_grad: float32 [512], P(('fsdp', 'ctx'))
- latent_up_grad: float32 [512, 4096], P(('fsdp', 'ctx'), 'tp')
- output_weight_grad: float32 [2048, 2048], P('tp', ('fsdp', 'ctx'))
- ffn_gain_grad: float32 [2048], P(('fsdp', 'ctx'))
- router_grad: float32 [2048, 64], P(('fsdp', 'ctx'))
- shared_gate_grad: float32 [2048, 2816], P(('fsdp', 'ctx'), 'tp')
- shared_up_grad: float32 [2048, 2816], P(('fsdp', 'ctx'), 'tp')
- shared_down_grad: float32 [2816, 2048], P('tp', ('fsdp', 'ctx'))
- expert_gate_grad: float32 [64, 2048, 1408], P(('fsdp', 'ctx'), None, 'tp')
- expert_up_grad: float32 [64, 2048, 1408], P(('fsdp', 'ctx'), None, 'tp')
- expert_down_grad: float32 [64, 1408, 2048], P(('fsdp', 'ctx'), 'tp')
The draws below stay inside these ranges and needn't reach their ends.
Inputs may be any that keep to these rules, and one draw needn't show every extreme that they name: `routes`: each row names 6 different experts; within each aligned block of 128 rows (the rows of one device) no expert is named more than 16 times, and in some block an expert is named exactly 16 times. `documents`: document numbers start at 0 in each row and never fall along it; each row has one document of 386 positions that begins before position 127, and every other position is a document of its own.
All inputs are finite; a program needn't handle non-finite values.
Results may differ from the reference program's by a relative error of at most 0.02.
Values may be sent and summed in bfloat16 or wider, within the bound.
No kernel may reach another device: no remote copies, remote signals or barrier semaphores. Data moves between devices by JAX's collectives and lax.ppermute only.
A program may use at most 256 MiB of HBM per device.

```python
import math
from functools import reduce
import jax
import jax.numpy as jnp
import numpy as np
from jax import lax

D = 2048
HEADS = 16
NOPE = 128
ROPE = 64
VDIM = 128
LATENT = 512
EXPERT_FF = 1408
SHARED_FF = 2816
TOP = 6
TOK = 128
LENGTH = 512
TOKENS = 8192
EXPERTS = 64
CAP = 16
EXPERT_ROWS = 1024
N_FSDP = 16
N_CTX = 4
N_TP = 2


def draw_documents(key, part):
    key = jax.random.fold_in(key, 11)
    key_start = jax.random.fold_in(key, 0)
    begin_at = jax.random.randint(key_start, (N_FSDP, 1), 0, TOK - 1)
    finish = begin_at + LENGTH - TOK + 2
    places = jnp.arange(LENGTH, dtype=jnp.int32)[None, :]
    in_long = (places >= begin_at) & (places < finish)
    starting = (jnp.logical_not(in_long) | (places == begin_at)) & (places > 0)
    return jnp.cumsum(starting.astype(jnp.int32), axis=1).astype(jnp.int32)


def strengthened(drawn, rng, source, target, blocks, factor):
    owner, partner = [(jnp.arange(drawn.shape[dim]) // (drawn.shape[dim] // blocks)).reshape([-1 if axis == dim else 1 for axis in range(drawn.ndim)]) for dim in (source, target)]
    chosen = jax.random.permutation(rng, blocks)[partner]
    strong = (owner == chosen) | (owner == (partner + blocks // 2) % blocks)
    return jnp.where(strong, factor * drawn, drawn)


def steps_of(stream_key, shape, cuts, smallest, largest):
    def one(dim, parts):
        steps = jax.random.uniform(jax.random.fold_in(jax.random.fold_in(stream_key, 6), dim), (parts,), jnp.float32, smallest / len(cuts), largest / len(cuts))
        return jnp.repeat(jnp.exp(steps), shape[dim] // parts).reshape((-1,) + (1,) * (len(shape) - dim - 1))

    factor_of = one(*cuts[0])
    for cut in cuts[1:]:
        factor_of = factor_of * one(*cut)
    return factor_of


def deal_out(rng, own, number, rows, number_of, top, most, slope):
    order = jax.random.permutation(rng, number_of)
    heavy_load, usual = portions_of(number_of, rows * top, most, slope, True), portions_of(number_of, rows * top, most, slope, False)
    places = jnp.arange(number_of)

    def named(sizes, turn):
        used = int((sizes > 0).sum())
        fixed = max(1, used // 4)
        passed = fixed + (places - fixed + turn * (used - fixed)) % max(1, number_of - fixed)
        return jnp.zeros((number_of,), jnp.int32).at[order[jnp.where(places < fixed, places, passed)]].set(jnp.asarray(sizes, jnp.int32))

    sizes = jnp.where(number % 4 == 0, named(heavy_load, number // 4), named(usual, number - number // 4 - 1))
    mixed = jax.random.permutation(jax.random.fold_in(own, 3), number_of)
    donor, sink = mixed[0:number_of // 2 * 2:2], mixed[1:number_of // 2 * 2:2]
    slack = jnp.minimum(sizes[donor] - 1, most - sizes[sink]) // 2
    slack = jnp.where((donor == order[0]) | (sink == order[0]) | (sizes[sink] == 0), 0, jnp.maximum(slack, 0))
    passed = jax.random.randint(jax.random.fold_in(own, 4), (number_of // 2,), 0, 1 << 20) % (slack + 1)
    sizes = sizes.at[donor].add(-passed).at[sink].add(passed)
    labels = jnp.searchsorted(jnp.cumsum(sizes), jnp.arange(rows * top), side="right").astype(jnp.int32)
    listing = labels.reshape(top, rows).T
    listing = listing[jax.random.permutation(jax.random.fold_in(own, 1), rows)]
    turn = jax.random.randint(jax.random.fold_in(own, 2), (rows, 1), 0, top)
    return jnp.take_along_axis(listing, (jnp.arange(top)[None, :] + turn) % top, axis=1)


def portions_of(amount, total, reach, lean, full):
    weights = [(1 << 20) // math.isqrt(grade ** lean) + 1 for grade in range(1, amount + 1)]
    largest = reach if full else min(reach, max(-(-total // amount), total * weights[0] // sum(weights)))
    least = 1 if total - largest >= amount - 1 else 0
    given, rest = [largest] + [least] * (amount - 1), total - largest - least * (amount - 1)
    while rest > 0:
        movable = [i for i in range(1, amount) if given[i] < largest] or [i for i in range(1, amount) if given[i] < reach]
        mass, budget = sum([weights[i] for i in movable]), rest
        for i in movable:
            more = min(reach - given[i], max(1, budget * weights[i] // mass), rest)
            given[i] = given[i] + more
            rest = rest - more
    return np.array(given)


def bell_draw(own_key, extent, scale, reach, cuts=(), kind=jnp.bfloat16):
    result = jax.random.normal(own_key, extent, jnp.float32) * scale
    if len(cuts) > 0:
        result = steps_of(own_key, extent, cuts, -0.22, 0.18) * result
    return jnp.clip(result, min=-reach, max=reach).astype(kind)


def heavy_noise(stream_key, dims, spread, limit, cuts, heavy, kind=jnp.bfloat16):
    values = spread * jax.random.normal(stream_key, dims, jnp.float32)
    if cuts:
        values = values * steps_of(stream_key, dims, cuts, -0.22, 0.18)
    return jnp.clip(strengthened(values, jax.random.fold_in(stream_key, 3), *heavy), -limit, limit).astype(kind)


def setup_inputs(seed: int = 0) -> dict:
    arg_keys = jax.random.split(jax.random.key(seed), 19)
    tokens_in = heavy_noise(arg_keys[0], (TOKENS, D), 1.0, 16.0, ((0, 64),), (0, 1, 64, 4.0))
    documents = draw_documents(jax.random.fold_in(arg_keys[18], 71), 0)
    routes_keys = jax.random.split(jax.random.fold_in(arg_keys[2], 1), TOKENS // TOK)
    routes_turns = jax.random.permutation(jax.random.fold_in(arg_keys[2], 3), TOKENS // TOK)
    routes = jax.vmap(lambda own, number: deal_out(jax.random.fold_in(arg_keys[2], 2), own, number, TOK, EXPERTS, TOP, CAP, 2))(routes_keys, routes_turns).reshape((TOKENS, TOP))
    attn_gain = jnp.clip(1.0 + 0.1 * jax.random.normal(arg_keys[3], (D,), jnp.float32), 0.5, 1.5).astype(jnp.bfloat16)
    query_weight = bell_draw(arg_keys[4], (D, HEADS * (NOPE + ROPE)), D ** -0.5, 0.125, ((0, 64), (1, 2)))
    latent_down = bell_draw(arg_keys[5], (D, LATENT + ROPE), D ** -0.5, 0.125, ((0, 64),))
    latent_gain = jnp.clip(1.0 + 0.1 * jax.random.normal(arg_keys[6], (LATENT,), jnp.float32), 0.5, 1.5).astype(jnp.bfloat16)
    latent_up = bell_draw(arg_keys[7], (LATENT, HEADS * (NOPE + VDIM)), LATENT ** -0.5, 0.25, ((0, 64), (1, 2)))
    output_weight = heavy_noise(arg_keys[8], (HEADS * VDIM, D), (HEADS * VDIM // 16) ** -0.5, 1.5, ((0, 2), (1, 64)), (0, 1, 64, 4.0))
    ffn_gain = jnp.clip(1.0 + 0.1 * jax.random.normal(arg_keys[9], (D,), jnp.float32), 0.5, 1.5).astype(jnp.bfloat16)
    router = bell_draw(arg_keys[10], (D, EXPERTS), (4 * D) ** -0.5, 0.0625, ((0, 64),))
    shared_gate = bell_draw(arg_keys[11], (D, SHARED_FF), D ** -0.5, 0.125, ((0, 64), (1, 2)))
    shared_up = bell_draw(arg_keys[12], (D, SHARED_FF), D ** -0.5, 0.125, ((0, 64), (1, 2)))
    shared_down = bell_draw(arg_keys[13], (SHARED_FF, D), SHARED_FF ** -0.5, 0.109375, ((0, 2), (1, 64)))
    expert_gate = bell_draw(arg_keys[14], (EXPERTS, D, EXPERT_FF), D ** -0.5, 0.125, ((0, 64), (2, 2)))
    expert_up = bell_draw(arg_keys[15], (EXPERTS, D, EXPERT_FF), D ** -0.5, 0.125, ((0, 64), (2, 2)))
    expert_down = bell_draw(arg_keys[16], (EXPERTS, EXPERT_FF, D), (max(1, EXPERT_FF // 512)) ** -0.5, 4.0, ((0, 64), (1, 2)))
    cotangent = heavy_noise(arg_keys[17], (TOKENS, D), 1.0, 16.0, ((0, 64),), (0, 1, 64, 4.0))
    return dict(tokens_in=tokens_in, documents=documents, routes=routes, attn_gain=attn_gain, query_weight=query_weight, latent_down=latent_down, latent_gain=latent_gain, latent_up=latent_up, output_weight=output_weight, ffn_gain=ffn_gain, router=router, shared_gate=shared_gate, shared_up=shared_up, shared_down=shared_down, expert_gate=expert_gate, expert_up=expert_up, expert_down=expert_down, cotangent=cotangent)


@jax.custom_vjp
def low(v):
    return lax.optimization_barrier(v.astype(jnp.bfloat16)).astype(jnp.float32)

@jax.custom_vjp
def low_back(v):
    return v

def low_keep(v):
    return (low(v), None)

def low_pass(kept, grad):
    return (grad,)

def back_keep(v):
    return (v, None)

def back_low(kept, grad):
    return (low(grad),)
low.defvjp(low_keep, low_pass)
low_back.defvjp(back_keep, back_low)
epsilon = 1e-06
precise = lax.Precision.HIGHEST

def product(left, right):
    return jnp.dot(left, right, precision=precise, preferred_element_type=jnp.float32)

def rope_tables(positions, half_width):
    freq_steps = jnp.arange(half_width, dtype=jnp.float32)
    inverse = 10000.0 ** (-freq_steps / half_width)
    angles = positions.astype(jnp.float32)[:, None] * inverse[None, :]
    return (jnp.cos(angles), jnp.sin(angles))

def rotate(values, cosine_table, sine_table):
    half_width = values.shape[-1] // 2
    leading = values[..., :half_width]
    trailing = values[..., half_width:]
    return jnp.concatenate([leading * cosine_table - trailing * sine_table, trailing * cosine_table + leading * sine_table], axis=-1)

def doc_positions(doc_row):
    places = jnp.arange(doc_row.shape[0], dtype=jnp.int32)
    starts = jnp.concatenate([jnp.ones((1,), bool), doc_row[1:] != doc_row[:-1]])
    begins = lax.cummax(jnp.where(starts, places, 0), axis=0)
    return places - begins

def attention_row(tokens_row, doc_row, one_gain, query_mat, down_mat, lat_gain, up_mat, out_mat):
    length = tokens_row.shape[0]
    head_width = NOPE + ROPE
    cosine_table, sine_table = rope_tables(doc_positions(doc_row), ROPE // 2)
    inverse_one = lax.rsqrt(lax.optimization_barrier(jnp.mean(tokens_row * tokens_row, axis=1, keepdims=True)) + epsilon)
    attn_in = low(tokens_row * inverse_one * one_gain)
    query_lin = low_back(product(attn_in, query_mat)).reshape(length, HEADS, head_width)
    query_rot = jnp.concatenate([query_lin[..., :NOPE], rotate(query_lin[..., NOPE:], cosine_table[:, None], sine_table[:, None])], axis=-1)
    query = low_back(low(query_rot))
    compressed = low_back(product(attn_in, down_mat))
    latent = compressed[:, :LATENT]
    inverse_lat = lax.rsqrt(lax.optimization_barrier(jnp.mean(latent * latent, axis=1, keepdims=True)) + epsilon)
    latent_in = low(latent * inverse_lat * lat_gain)
    key_rope = low(rotate(compressed[:, LATENT:], cosine_table, sine_table))
    group_count = N_TP * N_CTX
    rope_groups = low_back(jnp.broadcast_to(key_rope[:, None, :], (length, group_count, ROPE)))
    rope_heads = jnp.repeat(rope_groups, HEADS // group_count, axis=1)
    keys_values = low_back(low(product(latent_in, up_mat))).reshape(length, HEADS, NOPE + VDIM)
    key_heads = jnp.concatenate([keys_values[..., :NOPE], rope_heads], axis=-1)
    value_heads = keys_values[..., NOPE:]
    places = jnp.arange(length, dtype=jnp.int32)
    same_doc = (doc_row[:, None] == doc_row[None, :]) & (places[None, :] <= places[:, None])
    raw_scores = low_back(jnp.einsum('qhd,khd->hqk', query, key_heads, precision=precise))
    scores = jnp.where(same_doc[None], raw_scores * head_width ** (-0.5), -1e+30)
    row_max = lax.optimization_barrier(jnp.max(scores, axis=2, keepdims=True))
    log_total = row_max + jnp.log(lax.optimization_barrier(jnp.sum(jnp.exp(scores - row_max), axis=2, keepdims=True)))
    attn_probs = jnp.exp(scores - log_total)
    attended = low_back(low(jnp.einsum('hqk,khd->qhd', low(attn_probs), value_heads, precision=precise)))
    attn_out = low_back(product(attended.reshape(length, HEADS * VDIM), out_mat))
    return tokens_row + attn_out

def expert_block(operands):
    rows_in, gate_mat, upper_mat, lower_mat = operands
    width = EXPERT_FF // N_TP
    pieces = []
    for part_index in range(N_TP):
        piece_in = low_back(rows_in)
        gate_lin = low_back(product(piece_in, gate_mat[:, part_index * width:(part_index + 1) * width]))
        up_lin = low_back(product(piece_in, upper_mat[:, part_index * width:(part_index + 1) * width]))
        hidden_act = low(jax.nn.silu(gate_lin) * up_lin)
        pieces.append(low_back(low(product(hidden_act, lower_mat[part_index * width:(part_index + 1) * width]))))
    return reduce(lambda left, right: left + right, pieces)

def reference(tokens_in, documents, routes, attn_gain, query_weight, latent_down, latent_gain, latent_up, output_weight, ffn_gain, router, shared_gate, shared_up, shared_down, expert_gate, expert_up, expert_down, cotangent):
    blocks_count = TOKENS // TOK
    pair_expert = routes.reshape(blocks_count, TOK * TOP)
    onehot = (pair_expert[:, :, None] == jnp.arange(EXPERTS, dtype=jnp.int32)[None, None, :]).astype(jnp.int32)
    slot_index = lax.optimization_barrier(jnp.sum(jnp.cumsum(onehot, axis=1) * onehot, axis=2)) - 1
    block_ids = jnp.arange(blocks_count, dtype=jnp.int32)[:, None]
    destination = (pair_expert * EXPERT_ROWS + block_ids * CAP + slot_index).reshape(-1).astype(jnp.int32)
    pair_ids = jnp.arange(TOKENS * TOP, dtype=jnp.int32)
    source = jnp.zeros((EXPERTS * EXPERT_ROWS,), jnp.int32).at[destination].set(pair_ids // TOP)
    pair_of_slot = jnp.zeros((EXPERTS * EXPERT_ROWS,), jnp.int32).at[destination].set(pair_ids)
    filled = jnp.zeros((EXPERTS * EXPERT_ROWS,), jnp.float32).at[destination].set(1.0)

    def layer(tokens, one_gain, query_mat, down_mat, lat_gain, up_mat, out_mat, two_gain, route_mat, sgate_mat, supper_mat, sdown_mat, egate_mat, eupper_mat, edown_mat):

        def row_step(pair):
            return attention_row(pair[0], pair[1], one_gain, query_mat, down_mat, lat_gain, up_mat, out_mat)
        resid = lax.map(jax.checkpoint(row_step), (tokens.reshape(N_FSDP, LENGTH, D), documents)).reshape(TOKENS, D)
        inverse_two = lax.rsqrt(lax.optimization_barrier(jnp.mean(resid * resid, axis=1, keepdims=True)) + epsilon)
        ffn_in = low(resid * inverse_two * two_gain)
        router_probs = jax.nn.softmax(low_back(product(ffn_in, route_mat)), axis=1)
        gates = jnp.take_along_axis(router_probs, routes, axis=1)
        shared_act = low(jax.nn.silu(low_back(product(ffn_in, sgate_mat))) * low_back(product(ffn_in, supper_mat)))
        shared_out = product(shared_act, sdown_mat)
        buffer = (ffn_in[source] * filled[:, None]).reshape(EXPERTS, EXPERT_ROWS, D)
        expert_out = lax.map(jax.checkpoint(expert_block), (buffer, egate_mat, eupper_mat, edown_mat)).reshape(EXPERTS * EXPERT_ROWS, D)
        slot_gate = gates.reshape(-1)[pair_of_slot] * filled
        routed = jax.ops.segment_sum(expert_out * slot_gate[:, None], source, num_segments=TOKENS)
        return resid + shared_out + routed
    layer_out, pullback = jax.vjp(layer, tokens_in.astype(jnp.float32), attn_gain.astype(jnp.float32), query_weight.astype(jnp.float32), latent_down.astype(jnp.float32), latent_gain.astype(jnp.float32), latent_up.astype(jnp.float32), output_weight.astype(jnp.float32), ffn_gain.astype(jnp.float32), router.astype(jnp.float32), shared_gate.astype(jnp.float32), shared_up.astype(jnp.float32), shared_down.astype(jnp.float32), expert_gate.astype(jnp.float32), expert_up.astype(jnp.float32), expert_down.astype(jnp.float32))
    grads = pullback(cotangent.astype(jnp.float32))
    return (layer_out.astype(jnp.bfloat16), grads[0], grads[1], grads[2], grads[3], grads[4], grads[5], grads[6], grads[7], grads[8], grads[9], grads[10], grads[11], grads[12], grads[13], grads[14])
```

```python
import jax
import jax.numpy as jnp
from jax import lax
from jax.experimental import pallas as pl
from jax.experimental.pallas import tpu as pltpu
from jax.sharding import Mesh
from jax.sharding import PartitionSpec as P

NOPE = 128
ROPE = 64
VDIM = 128
LATENT = 512
HEAD = NOPE + ROPE
EPS = 1e-06
SCALE = HEAD ** (-0.5)
F32 = jnp.float32
BF16 = jnp.bfloat16


def dot(left, right, left_dim=1, right_dim=0):
    return lax.dot_general(
        left, right, (((left_dim,), (right_dim,)), ((), ())), preferred_element_type=F32
    )


def shift(values, axis, step):
    size = lax.axis_size(axis)
    return lax.ppermute(values, axis, [(j, (j + step) % size) for j in range(size)])


def put(buffer, piece, index, offset=0):
    start = (index, offset) + (0,) * (piece.ndim - 1)
    return lax.dynamic_update_slice(buffer, piece[None], start)


def pick(buffer, index):
    return lax.dynamic_index_in_dim(buffer, index, 0, keepdims=False)


def ring_gather(block, axis):
    me = lax.axis_index(axis)
    from_left = shift(block, axis, 1)
    from_right = shift(block, axis, -1)
    half = block.shape[0] // 2
    far_low = shift(from_left[:half], axis, 1)
    far_high = shift(from_right[half:], axis, -1)
    out = jnp.zeros((4,) + block.shape, block.dtype)
    out = put(out, block, me)
    out = put(out, from_left, (me + 3) % 4)
    out = put(out, from_right, (me + 1) % 4)
    out = put(out, far_low, (me + 2) % 4)
    return put(out, far_high, (me + 2) % 4, half)


def ring_scatter(parts, axis):
    me = lax.axis_index(axis)
    kind = parts.dtype
    far = pick(parts, (me + 2) % 4)
    right = pick(parts, (me + 1) % 4)
    left = pick(parts, (me + 3) % 4)
    half = far.shape[0] // 2
    low = shift(far[:half], axis, 1)
    high = shift(far[half:], axis, -1)
    right = jnp.concatenate(
        [(right[:half].astype(F32) + low.astype(F32)).astype(kind), right[half:]], axis=0
    )
    left = jnp.concatenate(
        [left[:half], (left[half:].astype(F32) + high.astype(F32)).astype(kind)], axis=0
    )
    got_left = shift(right, axis, 1)
    got_right = shift(left, axis, -1)
    total = pick(parts, me).astype(F32) + got_left.astype(F32) + got_right.astype(F32)
    return total.astype(kind)


def in_order(own, other, index):
    first = jnp.where(index == 0, own, other)
    second = jnp.where(index == 0, other, own)
    return jnp.stack([first, second])


def pair_gather(block, axis):
    return in_order(block, shift(block, axis, 1), lax.axis_index(axis))


def pair_scatter(parts, axis):
    me = lax.axis_index(axis)
    got = shift(pick(parts, 1 - me), axis, 1)
    return pick(parts, me).astype(F32) + got.astype(F32)


def gather_rows(halves):
    mine = lax.all_to_all(halves, "c", split_axis=0, concat_axis=0, tiled=True)
    pair = pair_gather(mine, "z")
    one = ring_gather(ring_gather(pair[:, 0], "x"), "y")
    two = ring_gather(ring_gather(pair[:, 1], "y"), "x")
    both = jnp.stack([one.transpose(1, 2, 0, 3, 4), two.transpose(0, 2, 1, 3, 4)], axis=2)
    return both.reshape(-1, halves.shape[-1])


def scatter_rows(partial):
    blocks = partial.reshape(4, 2, 2, 4, -1, partial.shape[-1])
    one, two = blocks[:, :, 0], blocks[:, :, 1]
    one = ring_scatter(ring_scatter(one.transpose(2, 0, 1, 3, 4), "y"), "x")
    two = ring_scatter(ring_scatter(two.transpose(0, 2, 1, 3, 4), "x"), "y")
    mine = pair_scatter(jnp.stack([one, two], axis=1), "z")
    return lax.all_to_all(mine, "c", split_axis=0, concat_axis=0, tiled=True)


def exchange(parts, axis):
    me = lax.axis_index(axis)
    out = jnp.zeros_like(parts)
    out = put(out, pick(parts, me), me)
    for step in (1, 2, 3):
        got = shift(pick(parts, (me + step) % 4), axis, step)
        out = put(out, got, (me + 4 - step) % 4)
    return out


def both_cores(block):
    pair = pair_gather(block, "c")
    return pair.reshape((-1,) + block.shape[1:])


def core_sum(partial):
    return pair_scatter_low(partial.reshape(2, -1, partial.shape[-1]))


def pair_scatter_low(parts):
    me = lax.axis_index("c")
    got = shift(pick(parts, 1 - me).astype(BF16), "c", 1)
    return pick(parts, me) + got.astype(F32)


def half_sum(partial):
    low = partial.astype(BF16)
    return low.astype(F32) + shift(low, "t", 1).astype(F32)


MSG = 1024
QR = 256
KV = 384
KR = 896


def head_lanes(rows, head):
    lane = lax.broadcasted_iota(jnp.int32, (rows, 128), 1)
    return jnp.where(((lane >> 5) & 1) == head, 1.0, 0.0).astype(F32)


def head_keys(msg_ref, head):
    rotated = msg_ref[:, :, KR:].reshape(512, 128).astype(F32) * head_lanes(512, head)
    plain = msg_ref[:, :, KV + head * 256 : KV + head * 256 + 128].reshape(512, 128)
    return jnp.concatenate([plain, rotated.astype(BF16)], axis=1)


def head_values(msg_ref, head):
    return msg_ref[:, :, KV + head * 256 + 128 : KV + head * 256 + 256].reshape(512, 128)


def block_probs(query, keys, row_ref, col_ref, block):
    count = (block + 1) * 128
    scores = dot(query, keys[:count], 1, 1) * SCALE
    rows = lax.broadcasted_iota(jnp.int32, (128, count), 0) + block * 128
    cols = lax.broadcasted_iota(jnp.int32, (128, count), 1)
    same = col_ref[block * 128 : count, :] == row_ref[:, :count]
    scores = jnp.where(same & (cols <= rows), scores, -1e30)
    powers = jnp.exp(scores - jnp.max(scores, axis=1, keepdims=True))
    return powers / jnp.sum(powers, axis=1, keepdims=True)


def block_query(msg_ref, head, block):
    return jnp.concatenate(
        [msg_ref[block, :, head * 128 : head * 128 + 128], msg_ref[block, :, QR:KV]], axis=1
    )


def forward_kernel(msg_ref, row_ref, col_ref, out_ref):
    for head in range(2):
        keys = head_keys(msg_ref, head)
        values = head_values(msg_ref, head)
        for block in range(4):
            query = block_query(msg_ref, head, block)
            probs = block_probs(query, keys, row_ref, col_ref, block)
            mixed = dot(probs.astype(BF16), values[: (block + 1) * 128])
            out_ref[block, :, head * 128 : head * 128 + 128] = mixed.astype(BF16)


def backward_kernel(msg_ref, grad_ref, row_ref, col_ref, out_ref, key_acc, value_acc):
    for head in range(2):
        keys = head_keys(msg_ref, head)
        values = head_values(msg_ref, head)
        key_acc[...] = jnp.zeros_like(key_acc)
        value_acc[...] = jnp.zeros_like(value_acc)
        lanes = head_lanes(128, head)
        for block in range(4):
            count = (block + 1) * 128
            query = block_query(msg_ref, head, block)
            probs = block_probs(query, keys, row_ref, col_ref, block)
            grad = grad_ref[block, :, head * 128 : head * 128 + 128]
            probs_grad = dot(grad, values[:count], 1, 1)
            inner = jnp.sum(probs * probs_grad, axis=1, keepdims=True)
            score_grad = (probs * (probs_grad - inner) * SCALE).astype(BF16)
            query_grad = dot(score_grad, keys[:count])
            out_ref[block, :, head * 128 : head * 128 + 128] = query_grad[:, :128].astype(BF16)
            turned = query_grad[:, 128:]
            if head == 1:
                turned = turned + out_ref[block, :, QR:KV].astype(F32)
            out_ref[block, :, QR:KV] = turned.astype(BF16)
            key_acc[:count] += dot(score_grad, query, 0, 0)
            value_acc[:count] += dot(probs.astype(BF16), grad, 0, 0)
        base = KV + head * 256
        for block in range(4):
            span = slice(block * 128, block * 128 + 128)
            out_ref[block, :, base : base + 128] = key_acc[span, :128].astype(BF16)
            out_ref[block, :, base + 128 : base + 256] = value_acc[span, :].astype(BF16)
            turned = key_acc[span, 128:] * lanes
            if head == 1:
                turned = turned + out_ref[block, :, KR:].astype(F32)
            out_ref[block, :, KR:] = turned.astype(BF16)


def vmem():
    return pl.BlockSpec(memory_space=pltpu.VMEM)


def attention_forward(msg, row, col):
    return pl.pallas_call(
        forward_kernel,
        out_shape=jax.ShapeDtypeStruct((4, 128, 256), BF16),
        in_specs=[vmem()] * 3,
        out_specs=vmem(),
        compiler_params=pltpu.CompilerParams(vmem_limit_bytes=32 * 1024 * 1024),
        cost_estimate=pl.CostEstimate(
            flops=400_000_000, bytes_accessed=1_400_000, transcendentals=400_000
        ),
    )(msg, row, col)


def attention_backward(msg, grad, row, col):
    return pl.pallas_call(
        backward_kernel,
        out_shape=jax.ShapeDtypeStruct((4, 128, MSG), BF16),
        in_specs=[vmem()] * 4,
        out_specs=vmem(),
        scratch_shapes=[pltpu.VMEM((512, 256), F32), pltpu.VMEM((512, 128), F32)],
        compiler_params=pltpu.CompilerParams(vmem_limit_bytes=32 * 1024 * 1024),
        cost_estimate=pl.CostEstimate(
            flops=1_000_000_000, bytes_accessed=2_600_000, transcendentals=400_000
        ),
    )(msg, grad, row, col)


def doc_positions(doc_row):
    places = jnp.arange(doc_row.shape[0], dtype=jnp.int32)
    starts = jnp.concatenate([jnp.ones((1,), bool), doc_row[1:] != doc_row[:-1]])
    begins = lax.cummax(jnp.where(starts, places, 0), axis=0)
    return places - begins


def swap_halves(values):
    rows, lanes = values.shape
    parts = values.reshape(rows, lanes // 128, 2, 64)
    return parts[:, :, ::-1].reshape(rows, lanes)


def rotate(values, cosine, sine):
    count = values.shape[1] // 128
    cosine = jnp.tile(cosine, (1, count))
    sine = jnp.tile(sine, (1, count))
    return values * cosine + swap_halves(values) * sine


def norm_back(scaled, normed, inverse):
    return inverse * (scaled - normed * jnp.mean(scaled * normed, axis=1, keepdims=True))


def silu_parts(lin):
    sig = jax.nn.sigmoid(lin)
    return lin * sig, sig * (1.0 + lin * (1.0 - sig))


def rms(values):
    return lax.rsqrt(jnp.mean(values * values, axis=1, keepdims=True) + EPS)


def shards(
    tokens_in,
    documents,
    routes,
    attn_gain,
    query_weight,
    latent_down,
    latent_gain,
    latent_up,
    output_weight,
    ffn_gain,
    router,
    shared_gate,
    shared_up,
    shared_down,
    expert_gate,
    expert_up,
    expert_down,
    cotangent,
):
    core = lax.axis_index("c")
    spot = lax.axis_index("y")
    expert = (lax.axis_index("x") * 4 + lax.axis_index("z") * 2 + core) * 4 + spot
    rows = tokens_in.shape[0]
    width = tokens_in.shape[1]
    experts_count = router.shape[1]
    capacity = 16
    every = ("x", "z", "c", "y")

    gain_col = attn_gain.astype(F32)[:, None]
    heads = query_weight.reshape(32, 2, 2, 2, HEAD)
    query_plain = heads[..., :NOPE].reshape(32, 2, 512)
    query_turn = (
        heads[..., NOPE:].reshape(32, 2, 2, 2, 2, 32).transpose(0, 1, 2, 4, 3, 5).reshape(32, 2, 256)
    )
    query_pack = jnp.concatenate([query_plain, query_turn], axis=2).transpose(1, 0, 2)
    up_pack = latent_up.reshape(8, 2, 4, 256).transpose(1, 0, 2, 3)
    up_scaled = (up_pack.astype(F32) * latent_gain.astype(F32)[None, :, None, None]).astype(BF16)
    out_pack = output_weight.reshape(2, 512, 32).transpose(0, 2, 1)
    gain_pad = jnp.pad(ffn_gain[:, None], ((0, 0), (0, 63)))
    attn_pack = jnp.concatenate(
        [
            (query_pack.astype(F32) * gain_col).astype(BF16),
            jnp.broadcast_to((latent_down.astype(F32) * gain_col).astype(BF16), (2, 32, 576)),
            jnp.broadcast_to(gain_pad, (2, 32, 64)),
            out_pack,
            up_scaled.reshape(2, 32, 256),
        ],
        axis=2,
    )
    attn_all = gather_rows(attn_pack)

    shared_pack = jnp.concatenate(
        [
            shared_gate.reshape(32, 2, 704),
            shared_up.reshape(32, 2, 704),
            shared_down.reshape(2, 704, 32).transpose(2, 0, 1),
            jnp.broadcast_to(router[:, None], (32, 2, 64)),
        ],
        axis=2,
    ).transpose(1, 0, 2)
    shared_pack, attn_all = lax.optimization_barrier((shared_pack, attn_all))
    shared_all = gather_rows(shared_pack)

    in_all = attn_all[:, :1408]
    out_all = attn_all[:, 1408:1920]
    up_all = attn_all[:, 1920:].reshape(LATENT, 1024)

    docs = both_cores(documents)
    positions = jax.vmap(doc_positions)(docs)
    local_pos = lax.dynamic_slice_in_dim(positions, spot * rows, rows, axis=1).reshape(-1)
    steps = jnp.arange(ROPE // 2, dtype=F32)
    angles = local_pos.astype(F32)[:, None] * (10000.0 ** (-steps / (ROPE // 2)))[None, :]
    cosine = jnp.tile(jnp.cos(angles), (1, 4))
    sine = jnp.sin(angles)
    sine = jnp.concatenate([-sine, -sine, sine, sine], axis=1)

    tokens_f = tokens_in.astype(F32)
    tokens_two = both_cores(tokens_in).astype(F32)
    normed_low = (tokens_two * rms(tokens_two)).astype(BF16)
    lin = dot(normed_low, in_all)
    query_turned = rotate(lin[:, 512:768], cosine, sine)
    latent = lin[:, 768:1280]
    inverse_lat = rms(latent)
    latent_normed = latent * inverse_lat
    latent_low = latent_normed.astype(BF16)
    key_u, key_w = lin[:, 1280:1312], lin[:, 1312:1344]
    key_turned = rotate(jnp.concatenate([key_u, key_u, key_w, key_w], axis=1), cosine, sine)
    keys_values = dot(latent_low, up_all)

    def messages(pair):
        span = slice(pair * 256, pair * 256 + 256)
        return jnp.concatenate(
            [
                lin[:, span],
                query_turned[:, pair * 128 : pair * 128 + 128],
                keys_values[:, pair * 512 : pair * 512 + 512],
                key_turned,
            ],
            axis=1,
        ).astype(BF16)

    sent = jnp.stack([messages(0), messages(1)]).reshape(2, 2, rows, MSG)
    sent = sent.transpose(1, 0, 2, 3).reshape(4, rows, MSG)
    msg = exchange(sent, "y")
    doc = pick(docs, spot // 2)
    doc_row, doc_col = doc[None, :], doc[:, None]
    mixed = attention_forward(msg, doc_row, doc_col)
    mixed_back = exchange(mixed, "y")
    attended = mixed_back.reshape(2, 2, rows, 256).transpose(0, 2, 1, 3).reshape(2 * rows, 512)
    resid = tokens_f + half_sum(core_sum(dot(attended, out_all, 1, 1)))

    gain_two = dot(
        (jnp.arange(64)[None, :] == 0).astype(BF16) * jnp.ones((8, 1), BF16),
        attn_all[:, 1344:1408],
        1,
        1,
    )[:1]
    inverse_two = rms(resid)
    normed_two = resid * inverse_two
    ffn_in = (normed_two * gain_two).astype(BF16)

    named = jnp.any(
        routes.T[None, :, :] == jnp.arange(experts_count, dtype=jnp.int32)[:, None, None], axis=1
    )
    before = jnp.arange(rows)[:, None] < jnp.arange(rows)[None, :]
    place = dot(named.astype(BF16), before.astype(BF16))
    slots = (
        named[:, None, :] & (place[:, None, :] == jnp.arange(capacity, dtype=F32)[None, :, None])
    ).astype(BF16)
    slots = slots.reshape(experts_count * capacity, rows)

    def to_experts(values):
        sent = dot(slots, values).astype(BF16).reshape(experts_count, capacity, width)
        got = lax.all_to_all(sent, every, split_axis=0, concat_axis=0, tiled=True)
        return got.reshape(-1, width)

    def from_experts(values):
        sent = values.reshape(experts_count, capacity, width)
        got = lax.all_to_all(sent, every, split_axis=0, concat_axis=0, tiled=True)
        return dot(slots, got.reshape(-1, width), 0, 0)

    gate_w, up_w, down_w = expert_gate[0], expert_up[0], expert_down[0]
    cot_sent, _ = lax.optimization_barrier((cotangent, attn_all))
    expert_cot = to_experts(cot_sent)
    expert_rows = to_experts(ffn_in)
    router_all = shared_all[:, 2112:]
    probs = jax.nn.softmax(dot(expert_rows, router_all), axis=1)
    own = (jnp.arange(experts_count, dtype=jnp.int32) == expert)[None, :].astype(F32)
    gate = jnp.sum(probs * own, axis=1, keepdims=True)
    plain_grad = dot(expert_cot, down_w, 1, 1)
    gate_lin = dot(expert_rows, gate_w)
    up_lin = dot(expert_rows, up_w)
    silu, slope = silu_parts(gate_lin)
    act = silu * up_lin
    act_low = (gate * act).astype(BF16)
    inner = jnp.sum(act * plain_grad, axis=1, keepdims=True)
    act_grad = gate * plain_grad
    gate_grad = (act_grad * up_lin * slope).astype(BF16)
    up_grad = (act_grad * silu).astype(BF16)
    logit_grad = (inner * gate * (own - probs)).astype(BF16)
    row_grad = (
        dot(gate_grad, gate_w, 1, 1) + dot(up_grad, up_w, 1, 1) + dot(logit_grad, router_all, 1, 1)
    ).astype(BF16)
    routed_back = from_experts(row_grad)
    piece = dot(act_low, down_w).astype(BF16)
    piece, _ = lax.optimization_barrier((piece, routed_back))
    routed_out = from_experts(piece)
    expert_down_grad = dot(act_low, expert_cot, 0, 0)[None]
    expert_gate_grad = dot(expert_rows, gate_grad, 0, 0)[None]
    expert_up_grad = dot(expert_rows, up_grad, 0, 0)[None]
    router_grad = dot(expert_rows, logit_grad, 0, 0)

    ffn_two = both_cores(ffn_in)
    cot_two = both_cores(cotangent)
    gate_up_all = shared_all[:, :1408]
    down_all = shared_all[:, 1408:2112]
    shared_lin = dot(ffn_two, gate_up_all)
    shared_up_lin = shared_lin[:, 704:]
    shared_silu, shared_slope = silu_parts(shared_lin[:, :704])
    shared_act = (shared_silu * shared_up_lin).astype(BF16)
    shared_dact = dot(cot_two, down_all)
    shared_dlin = jnp.concatenate(
        [shared_dact * shared_up_lin * shared_slope, shared_dact * shared_silu], axis=1
    ).astype(BF16)
    shared_out = core_sum(dot(shared_act, down_all, 1, 1))
    shared_back = core_sum(dot(shared_dlin, gate_up_all, 1, 1))
    gate_up_grad = dot(ffn_two, shared_dlin, 0, 0)
    shared_down_grad = dot(cot_two, shared_act, 0, 0)
    shared_sum = scatter_rows(
        jnp.concatenate([gate_up_grad, shared_down_grad, router_grad], axis=1).astype(BF16)
    )

    cot_f = cotangent.astype(F32)
    layer_out = (resid + half_sum(shared_out + routed_out)).astype(BF16)
    ffn_grad = half_sum(shared_back + routed_back)
    resid_grad = cot_f + norm_back(ffn_grad * gain_two, normed_two, inverse_two)
    first_lane = jnp.broadcast_to(jnp.arange(64)[None, :] == 0, (rows, 64)).astype(BF16)
    ffn_gain_part = dot((ffn_grad * normed_two).astype(BF16), first_lane, 0, 0)

    resid_two = both_cores(resid_grad.astype(BF16))
    out_grad = dot(resid_two, attended, 0, 0)
    heads_grad = dot(resid_two, out_all).astype(BF16)
    heads_sent = heads_grad.reshape(2, rows, 2, 256).transpose(0, 2, 1, 3).reshape(4, rows, 256)
    heads_got = exchange(heads_sent, "y")
    back = exchange(attention_backward(msg, heads_got, doc_row, doc_col), "y")
    back = back.reshape(2, 2, rows, MSG)

    def columns(low, high):
        part = back[..., low:high].transpose(0, 2, 1, 3)
        return part.reshape(2 * rows, 2 * (high - low))

    turned = rotate(columns(QR, KV).astype(F32), cosine, -sine)
    kv_grad = columns(KV, KR)
    key_back = jnp.sum(back[..., KR:].astype(F32), axis=1).reshape(2 * rows, 128)
    key_back = rotate(key_back, cosine, -sine)
    key_back = jnp.concatenate(
        [key_back[:, :32] + key_back[:, 32:64], key_back[:, 64:96] + key_back[:, 96:]], axis=1
    )
    latent_grad = norm_back(dot(kv_grad, up_all, 1, 1), latent_normed, inverse_lat)
    lin_grad = jnp.concatenate(
        [columns(0, QR), turned.astype(BF16), latent_grad.astype(BF16), key_back.astype(BF16)],
        axis=1,
    )
    normed_grad = dot(lin_grad, in_all[:, :1344], 1, 1)
    attn_in_grad = half_sum(core_sum(normed_grad))
    inverse_one = rms(tokens_f)
    input_grad = resid_grad + norm_back(attn_in_grad, tokens_f * inverse_one, inverse_one)
    in_grad = dot(normed_low, lin_grad, 0, 0)
    up_grad_part = dot(latent_low, kv_grad, 0, 0).reshape(width, 256)
    attn_sum = scatter_rows(
        jnp.concatenate([in_grad, ffn_gain_part, out_grad, up_grad_part], axis=1).astype(BF16)
    )

    query_sum = attn_sum[..., :768]
    up_sum = attn_sum[..., 1920:]
    down_sum = attn_sum[0, :, 768:1344] + attn_sum[1, :, 768:1344]
    attn_gain_part = jnp.sum(query_pack.astype(F32) * query_sum, axis=(0, 2)) + jnp.sum(
        latent_down.astype(F32) * down_sum, axis=1
    )
    latent_gain_part = jnp.sum(up_pack.reshape(2, 32, 256).astype(F32) * up_sum, axis=(0, 2))
    router_sum = shared_sum[0, :, 2112:] + shared_sum[1, :, 2112:]
    small = jnp.concatenate(
        [down_sum, router_sum, attn_gain_part[:, None], latent_gain_part[:, None]], axis=1
    )
    small = small + shift(small, "t", 1)
    attn_gain_grad = small[:, 640]
    latent_gain_grad = jnp.sum(small[:, 641].reshape(8, 4), axis=1)
    latent_down_grad = gain_col * small[:, :576]
    router_out = small[:, 576:640]
    query_plain = query_sum[..., :512].reshape(2, 32, 2, 2, NOPE)
    query_turn = query_sum[..., 512:].reshape(2, 32, 2, 2, 2, 32).transpose(0, 1, 2, 4, 3, 5)
    query_turn = query_turn.reshape(2, 32, 2, 2, ROPE)
    query_out = jnp.concatenate([query_plain, query_turn], axis=4).transpose(1, 0, 2, 3, 4)
    query_out = gain_col * query_out.reshape(32, 2 * 4 * HEAD)
    up_out = up_sum.reshape(2, 8, 4, 256).transpose(1, 0, 2, 3).reshape(8, 2048)
    up_out = latent_gain.astype(F32)[:, None] * up_out
    out_out = attn_sum[..., 1408:1920].transpose(0, 2, 1).reshape(1024, 32)
    ffn_gain_grad = attn_sum[0, :, 1344] + attn_sum[1, :, 1344]
    shared_rows = shared_sum.transpose(1, 0, 2)
    return (
        layer_out,
        input_grad,
        attn_gain_grad,
        query_out,
        latent_down_grad,
        latent_gain_grad,
        up_out,
        out_out,
        ffn_gain_grad,
        router_out,
        shared_rows[..., :704].reshape(32, 1408),
        shared_rows[..., 704:1408].reshape(32, 1408),
        shared_sum[..., 1408:2112].transpose(0, 2, 1).reshape(1408, 32),
        expert_gate_grad,
        expert_up_grad,
        expert_down_grad,
    )


def solution(mesh):
    fine = Mesh(mesh.devices.reshape(4, 2, 2, 4, 2), ("x", "z", "c", "y", "t"))
    fsdp = ("x", "z", "c")
    every = ("x", "z", "c", "y")
    in_specs = (
        P(every, None),
        P(fsdp, None),
        P(every, None),
        P(every),
        P(every, "t"),
        P(every, None),
        P(every),
        P(every, "t"),
        P("t", every),
        P(every),
        P(every, None),
        P(every, "t"),
        P(every, "t"),
        P("t", every),
        P(every, None, "t"),
        P(every, None, "t"),
        P(every, "t", None),
        P(every, None),
    )
    out_specs = (
        P(every, None),
        P(every, None),
        P(every),
        P(every, "t"),
        P(every, None),
        P(every),
        P(every, "t"),
        P("t", every),
        P(every),
        P(every, None),
        P(every, "t"),
        P(every, "t"),
        P("t", every),
        P(every, None, "t"),
        P(every, None, "t"),
        P(every, "t", None),
    )
    return jax.shard_map(shards, mesh=fine, in_specs=in_specs, out_specs=out_specs, check_vma=False)
```

```python
import functools

import jax
import jax.numpy as jnp
import numpy as np
from jax import lax
from jax.experimental import pallas as pl
from jax.experimental.pallas import tpu as pltpu
from jax.sharding import Mesh
from jax.sharding import PartitionSpec as P

NOPE = 128
ROPE = 64
VDIM = 128
LATENT = 512
HEAD = NOPE + ROPE
EPS = 1e-06
SCALE = HEAD ** (-0.5)
F32 = jnp.float32
BF16 = jnp.bfloat16


def dot(left, right, left_dim=1, right_dim=0):
    return lax.dot_general(
        left, right, (((left_dim,), (right_dim,)), ((), ())), preferred_element_type=F32
    )


def shift(values, axis, step):
    size = lax.axis_size(axis)
    return lax.ppermute(values, axis, [(j, (j + step) % size) for j in range(size)])


def diagonal(values):
    return lax.ppermute(values, ("z", "c"), [(0, 3), (1, 2), (2, 1), (3, 0)])


def pick(buffer, index):
    return lax.dynamic_index_in_dim(buffer, index, 0, keepdims=False)


def in_order(own, other, index):
    return jnp.stack([jnp.where(index == 0, own, other), jnp.where(index == 0, other, own)])


def gather_rows(halves, at):
    x, z, core, y = (lax.axis_index(name) for name in ("x", "z", "c", "y"))
    lanes = halves.shape[-1]
    keep, send = pick(halves, core), pick(halves, 1 - core)
    across, beside, corner = shift(send, "c", 1), shift(keep, "z", 1), diagonal(send)
    final = jnp.zeros((4, 2, 2, 4, 32, lanes), halves.dtype)

    def put_one(buffer, piece, level, place):
        start = (0, level, core, place % 4, 0, 0)
        return lax.dynamic_update_slice(buffer, piece.reshape(4, 1, 1, 1, 32, lanes), start)

    def put_two(buffer, piece, level, place):
        start = (place % 4, level, 1 - core, 0, 0, 0)
        return lax.dynamic_update_slice(buffer, piece.reshape(1, 1, 1, 4, 32, lanes), start)

    first = [line_up(at, 0, keep, "x"), line_up(at, 0, beside, "x")]
    second = [line_up(at, 3, across, "y"), line_up(at, 3, corner, "y")]
    levels = (z, 1 - z)
    for put, lines, axis, place in ((put_one, first, "y", y), (put_two, second, "x", x)):
        for line, level in zip(lines, levels, strict=True):
            final = put(final, line, level, place)
    near = {}
    for name, lines, axis in (("one", first, "y"), ("two", second, "x")):
        near[name] = [(shift(line, axis, 1), shift(line, axis, -1)) for line in lines]
    far = {}
    for name, axis in (("one", "y"), ("two", "x")):
        far[name] = (shift(near[name][0][0], axis, 1), shift(near[name][1][1], axis, -1))
    for name, put, place in (("one", put_one, y), ("two", put_two, x)):
        for (left, right), level in zip(near[name], levels, strict=True):
            final = put(put(final, left, level, place + 3), right, level, place + 1)
    for name, put, place in (("one", put_one, y), ("two", put_two, x)):
        for piece, level in zip(far[name], levels, strict=True):
            final = put(final, piece, level, place + 2)
    return final.reshape(-1, lanes)


def line_kernel(index, at, *refs):
    for step in range(4):
        refs[4][lax.rem(at[index] + 4 - step, 4)] = refs[step][...]


def line_up(at, index, block, axis):
    blocks = [block] + [shift(block, axis, step) for step in (1, 2, 3)]
    return call(
        functools.partial(line_kernel, index), (4,) + block.shape, BF16, at, *blocks
    )


def ring_sum(parts, axis):
    low = shift(parts[2][0], axis, 1)
    high = shift(parts[2][1], axis, -1)
    right_high = shift(parts[1][1], axis, 1)
    left_low = shift(parts[3][0], axis, -1)
    right_low = shift(add_low(parts[1][0], low), axis, 1)
    left_high = shift(add_low(parts[3][1], high), axis, -1)
    return [add_low(parts[0][0], left_low, right_low), add_low(parts[0][1], right_high, left_high)]


def add_low(*values):
    return sum(value.astype(F32) for value in values).astype(BF16)


def direct_sum(line, axis):
    me = lax.axis_index(axis)
    got = [shift(pick(line, (me + step) % 4), axis, step) for step in (1, 2, 3)]
    return add_low(pick(line, me), *got)


def scatter_rows(one, two):
    one = [direct_sum(line, "x") for line in ring_sum(one, "y")]
    two = [direct_sum(line, "y") for line in ring_sum(two, "x")]
    beside, across, corner = shift(one[1], "z", 1), shift(two[0], "c", 1), diagonal(two[1])
    own = one[0].astype(F32) + beside.astype(F32)
    other = across.astype(F32) + corner.astype(F32)
    return in_order(own, other, lax.axis_index("c"))


def to_ring(pieces):
    return [pieces[0]] + [shift(pieces[step], "y", step) for step in (1, 2, 3)]


def half_sum(partial):
    low = partial.astype(BF16)
    return low.astype(F32) + shift(low, "t", 1).astype(F32)


def core_sum(own, other):
    return own + shift(other, "c", 1).astype(F32)


def call(kernel, shapes, dtypes, at, *operands, scratch=(), flops=1_000_000, many=False):
    if not many:
        shapes, dtypes = [shapes], [dtypes]
    out_shape = [jax.ShapeDtypeStruct(s, d) for s, d in zip(shapes, dtypes, strict=True)]
    moved = sum(o.size * o.dtype.itemsize for o in operands)
    moved += sum(int(np.prod(s)) * jnp.dtype(d).itemsize for s, d in zip(shapes, dtypes, strict=True))
    outs = pl.pallas_call(
        kernel,
        out_shape=out_shape,
        in_specs=[pl.BlockSpec(memory_space=pltpu.SMEM)]
        + [pl.BlockSpec(memory_space=pltpu.VMEM)] * len(operands),
        out_specs=[pl.BlockSpec(memory_space=pltpu.VMEM)] * len(out_shape),
        scratch_shapes=scratch,
        compiler_params=pltpu.CompilerParams(vmem_limit_bytes=56 * 1024 * 1024),
        cost_estimate=pl.CostEstimate(flops=flops, bytes_accessed=moved, transcendentals=0),
    )(at, *operands)
    return outs if many else outs[0]


MSG = 1024
QR = 256
KV = 384
KR = 896


def rows_at(index):
    return pl.ds(pl.multiple_of(index * 128, 128), 128)


def lanes_at(index, size, base=0):
    return pl.ds(pl.multiple_of(base + index * size, 128), size)


def owner(at, place):
    return jnp.bitwise_xor(lax.shift_right_logical(place, 1), at[2]), jnp.bitwise_and(place, 1)


def ahead(at, step):
    return lax.rem(at[3] + step, 4)


def behind(at, step):
    return lax.rem(at[3] + 4 - step, 4)


def turn(values, cosine, sine):
    return values * cosine + pltpu.roll(values, 64, 1) * sine


def project_kernel(
    at, own, other, weights, up, cosine, sine, m0, m1, m2, m3, normed, low, plain, inverse, query, keys, key
):
    for index, block in enumerate((own, other)):
        values = block[...].astype(F32)
        scale = lax.rsqrt(jnp.mean(values * values, axis=1, keepdims=True) + EPS)
        normed[index * 128 : index * 128 + 128] = (values * scale).astype(BF16)
    lin = dot(normed[...], weights[...])
    cos, sin = cosine[...], sine[...]
    query[:, :512] = lin[:, :512].astype(BF16)
    for pair in range(2):
        span = slice(512 + pair * 128, 640 + pair * 128)
        query[:, span] = turn(lin[:, span], cos, sin).astype(BF16)
    key[...] = turn(lin[:, 1280:], cos, sin).astype(BF16)
    latent = lin[:, 768:1280]
    scale = lax.rsqrt(jnp.mean(latent * latent, axis=1, keepdims=True) + EPS)
    latent = latent * scale
    plain[...] = latent
    low[...] = latent.astype(BF16)
    inverse[...] = jnp.broadcast_to(scale, inverse.shape)
    keys[...] = dot(low[...], up[...]).astype(BF16)
    for step, out in enumerate((m0, m1, m2, m3)):
        block, pair = owner(at, ahead(at, step))
        rows = rows_at(block)
        out[:, :QR] = query[rows, lanes_at(pair, 256)]
        out[:, QR:KV] = query[rows, lanes_at(pair, 128, 512)]
        out[:, KV:KR] = keys[rows, lanes_at(pair, 512)]
        out[:, KR:] = key[rows, :]


def head_lanes(rows, head):
    lane = lax.broadcasted_iota(jnp.int32, (rows, 128), 1)
    return jnp.where(((lane >> 5) & 1) == head, 1.0, 0.0).astype(F32)


def head_keys(msg_ref, head):
    rotated = msg_ref[:, :, KR:].reshape(512, 128).astype(F32) * head_lanes(512, head)
    plain = msg_ref[:, :, KV + head * 256 : KV + head * 256 + 128].reshape(512, 128)
    return jnp.concatenate([plain, rotated.astype(BF16)], axis=1)


def head_values(msg_ref, head):
    return msg_ref[:, :, KV + head * 256 + 128 : KV + head * 256 + 256].reshape(512, 128)


def block_probs(query, keys, row_ref, col_ref, block):
    count = (block + 1) * 128
    scores = dot(query, keys[:count], 1, 1) * SCALE
    rows = lax.broadcasted_iota(jnp.int32, (128, count), 0) + block * 128
    cols = lax.broadcasted_iota(jnp.int32, (128, count), 1)
    same = col_ref[block * 128 : count, :] == row_ref[:, :count]
    scores = jnp.where(same & (cols <= rows), scores, -1e30)
    powers = jnp.exp(scores - jnp.max(scores, axis=1, keepdims=True))
    return powers / jnp.sum(powers, axis=1, keepdims=True)


def block_query(msg_ref, head, block):
    return jnp.concatenate(
        [msg_ref[block, :, head * 128 : head * 128 + 128], msg_ref[block, :, QR:KV]], axis=1
    )


def forward_kernel(at, m0, m1, m2, m3, row_ref, col_ref, msg_ref, o0, o1, o2, o3, mixed):
    for step, piece in enumerate((m0, m1, m2, m3)):
        msg_ref[behind(at, step)] = piece[...]
    for head in range(2):
        keys = head_keys(msg_ref, head)
        values = head_values(msg_ref, head)
        for block in range(4):
            query = block_query(msg_ref, head, block)
            probs = block_probs(query, keys, row_ref, col_ref, block)
            part = dot(probs.astype(BF16), values[: (block + 1) * 128])
            mixed[block, :, head * 128 : head * 128 + 128] = part.astype(BF16)
    for step, out in enumerate((o0, o1, o2, o3)):
        out[...] = mixed[ahead(at, step)]


def output_kernel(at, p0, p1, p2, p3, weights, attended, own, other):
    for step, piece in enumerate((p0, p1, p2, p3)):
        block, pair = owner(at, behind(at, step))
        attended[rows_at(block), lanes_at(pair, 256)] = piece[...]
    own[...] = dot(attended[:128], weights[...], 1, 1)
    other[...] = dot(attended[128:], weights[...], 1, 1).astype(BF16)


def heads_kernel(at, own, other, weights, h0, h1, h2, h3, grad):
    grad[:128] = dot(own[...], weights[...]).astype(BF16)
    grad[128:] = dot(other[...], weights[...]).astype(BF16)
    for step, out in enumerate((h0, h1, h2, h3)):
        block, pair = owner(at, ahead(at, step))
        out[...] = grad[rows_at(block), lanes_at(pair, 256)]


def backward_kernel(
    at, msg_ref, g0, g1, g2, g3, row_ref, col_ref, o0, o1, o2, o3, grad_ref, out_ref, key_acc, value_acc
):
    for step, piece in enumerate((g0, g1, g2, g3)):
        grad_ref[behind(at, step)] = piece[...]
    for head in range(2):
        keys = head_keys(msg_ref, head)
        values = head_values(msg_ref, head)
        key_acc[...] = jnp.zeros_like(key_acc)
        value_acc[...] = jnp.zeros_like(value_acc)
        lanes = head_lanes(128, head)
        for block in range(4):
            count = (block + 1) * 128
            query = block_query(msg_ref, head, block)
            probs = block_probs(query, keys, row_ref, col_ref, block)
            grad = grad_ref[block, :, head * 128 : head * 128 + 128]
            probs_grad = dot(grad, values[:count], 1, 1)
            inner = jnp.sum(probs * probs_grad, axis=1, keepdims=True)
            score_grad = (probs * (probs_grad - inner) * SCALE).astype(BF16)
            query_grad = dot(score_grad, keys[:count])
            out_ref[block, :, head * 128 : head * 128 + 128] = query_grad[:, :128].astype(BF16)
            turned = query_grad[:, 128:]
            if head == 1:
                turned = turned + out_ref[block, :, QR:KV].astype(F32)
            out_ref[block, :, QR:KV] = turned.astype(BF16)
            key_acc[:count] += dot(score_grad, query, 0, 0)
            value_acc[:count] += dot(probs.astype(BF16), grad, 0, 0)
        base = KV + head * 256
        for block in range(4):
            span = slice(block * 128, block * 128 + 128)
            out_ref[block, :, base : base + 128] = key_acc[span, :128].astype(BF16)
            out_ref[block, :, base + 128 : base + 256] = value_acc[span, :].astype(BF16)
            turned = key_acc[span, 128:] * lanes
            if head == 1:
                turned = turned + out_ref[block, :, KR:].astype(F32)
            out_ref[block, :, KR:] = turned.astype(BF16)
    for step, out in enumerate((o0, o1, o2, o3)):
        out[...] = out_ref[ahead(at, step)]


def return_kernel(
    at, b0, b1, b2, b3, weights, up, cosine, sine, plain, inverse, lin_grad, kv_grad, own, other, key
):
    for step, piece in enumerate((b0, b1, b2, b3)):
        block, pair = owner(at, behind(at, step))
        rows = rows_at(block)
        lin_grad[rows, lanes_at(pair, 256)] = piece[:, :QR]
        turned = turn(piece[:, QR:KV].astype(F32), cosine[rows, :], -sine[rows, :])
        lin_grad[rows, lanes_at(pair, 128, 512)] = turned.astype(BF16)
        kv_grad[rows, lanes_at(pair, 512)] = piece[:, KV:KR]
        key[rows_at(block + 2 * pair), :] = piece[:, KR:].astype(F32)
    turned = turn(key[:256] + key[256:], cosine[...], -sine[...])
    lin_grad[:, 1280:] = turned.astype(BF16)
    grad = dot(kv_grad[...], up[...], 1, 1)
    latent = plain[...]
    grad = inverse[:, :1] * (grad - latent * jnp.mean(grad * latent, axis=1, keepdims=True))
    lin_grad[:, 768:1280] = grad.astype(BF16)
    own[...] = dot(lin_grad[:128], weights[...], 1, 1)
    other[...] = dot(lin_grad[128:], weights[...], 1, 1).astype(BF16)


def grads_kernel(at, normed, lin_grad, own, other, attended, up, tail, *refs):
    one, two, rows = refs[:8], refs[8:16], refs[16]
    for step in range(4):
        column = lax.rem(at[0] + step, 4)
        for side in range(2):
            level = at[1] if side == 0 else 1 - at[1]
            start = pl.multiple_of((column * 2 + level) * 256, 256)
            span = pl.ds(start, 256)
            part = dot(normed[:, span], lin_grad[...], 0, 0).astype(BF16)
            rows[:, :, :1408] = part.reshape(8, 32, 1408)
            part = dot(own[:, span], attended[:128], 0, 0) + dot(other[:, span], attended[128:], 0, 0)
            rows[:, :, 1408:1920] = part.astype(BF16).reshape(8, 32, 512)
            rows[:, :, 1920:2176] = up[span, :].reshape(8, 32, 256)
            rows[:, :, 2176:] = tail[span, :].reshape(8, 32, 128)
            for place in range(4):
                one[place * 2 + side][column] = rows[at[2] * 4 + ahead(at, place)]
            two[step * 2 + side][...] = rows[pl.ds((1 - at[2]) * 4, 4)]


def shared_grads_kernel(at, own, other, lin_grad, cot, cot_other, act, out):
    for block in range(8):
        span = slice(block * 256, block * 256 + 256)
        part = dot(own[:, span], lin_grad[:128], 0, 0) + dot(other[:, span], lin_grad[128:], 0, 0)
        part = part.astype(BF16).reshape(2, 4, 32, 1408)
        for core in range(2):
            out[block, :, core, :, :1408] = part[core]
        part = dot(cot[:, span], act[:128], 0, 0) + dot(cot_other[:, span], act[128:], 0, 0)
        part = part.astype(BF16).reshape(2, 4, 32, 704)
        for core in range(2):
            out[block, :, core, :, 1408:] = part[core]


def doc_positions(doc_row):
    places = jnp.arange(doc_row.shape[0], dtype=jnp.int32)
    starts = jnp.concatenate([jnp.ones((1,), bool), doc_row[1:] != doc_row[:-1]])
    begins = lax.cummax(jnp.where(starts, places, 0), axis=0)
    return places - begins


def norm_back(scaled, normed, inverse):
    return inverse * (scaled - normed * jnp.mean(scaled * normed, axis=1, keepdims=True))


def silu_parts(lin):
    sig = jax.nn.sigmoid(lin)
    return lin * sig, sig * (1.0 + lin * (1.0 - sig))


def rms(values):
    return lax.rsqrt(jnp.mean(values * values, axis=1, keepdims=True) + EPS)


def shards(
    tokens_in,
    documents,
    routes,
    attn_gain,
    query_weight,
    latent_down,
    latent_gain,
    latent_up,
    output_weight,
    ffn_gain,
    router,
    shared_gate,
    shared_up,
    shared_down,
    expert_gate,
    expert_up,
    expert_down,
    cotangent,
):
    core = lax.axis_index("c")
    spot = lax.axis_index("y")
    at = jnp.stack([lax.axis_index("x"), lax.axis_index("z"), core, spot]).astype(jnp.int32)
    expert = (lax.axis_index("x") * 4 + lax.axis_index("z") * 2 + core) * 4 + spot
    rows = tokens_in.shape[0]
    width = tokens_in.shape[1]
    experts_count = router.shape[1]
    capacity = 16
    every = ("x", "z", "c", "y")

    gain_col = attn_gain.astype(F32)[:, None]
    heads = query_weight.reshape(32, 2, 2, 2, HEAD)
    query_plain = heads[..., :NOPE].reshape(32, 2, 512)
    query_turn = heads[..., NOPE:].reshape(32, 2, 2, 2, 2, 32).transpose(0, 1, 2, 4, 3, 5)
    query_pack = jnp.concatenate([query_plain, query_turn.reshape(32, 2, 256)], axis=2)
    query_pack = query_pack.transpose(1, 0, 2)
    down_pack = jnp.concatenate(
        [latent_down[:, :544], latent_down[:, 512:], latent_down[:, 544:]], axis=1
    )
    up_pack = latent_up.reshape(8, 2, 4, 256).transpose(1, 0, 2, 3)
    up_scaled = (up_pack.astype(F32) * latent_gain.astype(F32)[None, :, None, None]).astype(BF16)
    shared_pack = jnp.concatenate(
        [
            shared_gate.reshape(32, 2, 704),
            shared_up.reshape(32, 2, 704),
            shared_down.reshape(2, 704, 32).transpose(2, 0, 1),
        ],
        axis=2,
    )
    both = jnp.concatenate([router, ffn_gain[:, None]], axis=1)
    pack = jnp.concatenate(
        [
            (query_pack.astype(F32) * gain_col).astype(BF16),
            jnp.broadcast_to((down_pack.astype(F32) * gain_col).astype(BF16), (2, 32, 640)),
            output_weight.reshape(2, 512, 32).transpose(0, 2, 1),
            up_scaled.reshape(2, 32, 256),
            shared_pack.transpose(1, 0, 2),
            jnp.broadcast_to(jnp.pad(both, ((0, 0), (0, 63))), (2, 32, 128)),
        ],
        axis=2,
    )
    weights = gather_rows(pack, at)
    in_all = weights[:, :1408]
    out_all = weights[:, 1408:1920]
    up_all = weights[:, 1920:2176].reshape(LATENT, 1024)
    gate_up_all = weights[:, 2176:3584]
    down_all = weights[:, 3584:4288]
    router_all = weights[:, 4288:4352]

    named = jnp.any(
        routes.T[None, :, :] == jnp.arange(experts_count, dtype=jnp.int32)[:, None, None], axis=1
    )
    before = jnp.arange(rows)[:, None] < jnp.arange(rows)[None, :]
    place = dot(named.astype(BF16), before.astype(BF16))
    slots = (
        named[:, None, :] & (place[:, None, :] == jnp.arange(capacity, dtype=F32)[None, :, None])
    ).astype(BF16)
    slots = slots.reshape(experts_count * capacity, rows)

    def to_experts(values):
        sent = dot(slots, values).astype(BF16).reshape(experts_count, capacity, width)
        got = lax.all_to_all(sent, every, split_axis=0, concat_axis=0, tiled=True)
        return got.reshape(-1, width)

    def return_rows(values):
        sent = values.reshape(experts_count, capacity, width)
        got = lax.all_to_all(sent, every, split_axis=0, concat_axis=0, tiled=True)
        return got.reshape(-1, width)

    cot_sent, in_all = lax.optimization_barrier((cotangent, in_all))
    expert_cot = to_experts(cot_sent)

    docs = jnp.concatenate([documents, shift(documents, "c", 1)])
    positions = jax.vmap(doc_positions)(docs)
    local_pos = lax.dynamic_slice_in_dim(positions, spot * rows, rows, axis=1).reshape(-1)
    steps = jnp.arange(ROPE // 2, dtype=F32)
    angles = local_pos.astype(F32)[:, None] * (10000.0 ** (-steps / (ROPE // 2)))[None, :]
    cosine = jnp.tile(jnp.cos(angles), (1, 4))
    sine = jnp.sin(angles)
    sine = jnp.concatenate([-sine, -sine, sine, sine], axis=1)
    doc = jnp.where(spot // 2 == core, docs[0], docs[1])
    doc_row, doc_col = doc[None, :], doc[:, None]

    tokens_other = shift(tokens_in, "c", 1)
    sent = [(rows, MSG)] * 4
    two = 2 * rows
    *sent, normed_low, latent_low, latent_normed, latent_inverse = call(
        project_kernel,
        sent + [(two, width), (two, LATENT), (two, LATENT), (two, 128)],
        [BF16] * 6 + [F32, F32],
        at,
        tokens_in,
        tokens_other,
        in_all,
        up_all,
        cosine,
        sine,
        scratch=[
            pltpu.VMEM((two, 768), BF16),
            pltpu.VMEM((two, 1024), BF16),
            pltpu.VMEM((two, 128), BF16),
        ],
        flops=1_800_000_000,
        many=True,
    )
    received = to_ring(sent)
    received[0], expert_cot = lax.optimization_barrier((received[0], expert_cot))
    msg, *mixed = call(
        forward_kernel,
        [(4, rows, MSG)] + [(rows, 256)] * 4,
        [BF16] * 5,
        at,
        *received,
        doc_row,
        doc_col,
        scratch=[pltpu.VMEM((4, rows, 256), BF16)],
        flops=500_000_000,
        many=True,
    )
    attended, out_own, out_other = call(
        output_kernel,
        [(two, 512), (rows, width), (rows, width)],
        [BF16, F32, BF16],
        at,
        *to_ring(mixed),
        out_all,
        flops=600_000_000,
        many=True,
    )
    tokens_f = tokens_in.astype(F32)
    resid = tokens_f + half_sum(core_sum(out_own, out_other))

    pointer = jnp.broadcast_to(jnp.arange(64)[None, :] == 0, (8, 64)).astype(BF16)
    gain_two = dot(pointer, weights[:, 4352:], 1, 1)[:1]
    inverse_two = rms(resid)
    normed_two = resid * inverse_two
    ffn_in = (normed_two * gain_two).astype(BF16)
    expert_rows = to_experts(ffn_in)

    ffn_other = shift(ffn_in, "c", 1)
    cot_other = shift(cotangent, "c", 1)
    ffn_two = jnp.concatenate([ffn_in, ffn_other])
    cot_two = jnp.concatenate([cotangent, cot_other])
    shared_lin = dot(ffn_two, gate_up_all)
    shared_up_lin = shared_lin[:, 704:]
    shared_silu, shared_slope = silu_parts(shared_lin[:, :704])
    shared_act = (shared_silu * shared_up_lin).astype(BF16)
    shared_dact = dot(cot_two, down_all)
    shared_dlin = jnp.concatenate(
        [shared_dact * shared_up_lin * shared_slope, shared_dact * shared_silu], axis=1
    ).astype(BF16)
    shared_out = dot(shared_act, down_all, 1, 1)
    shared_out = core_sum(shared_out[:rows], shared_out[rows:].astype(BF16))
    shared_back = dot(shared_dlin, gate_up_all, 1, 1)
    shared_back = core_sum(shared_back[:rows], shared_back[rows:].astype(BF16))
    shared_grads = call(
        shared_grads_kernel,
        (8, 4, 2, 32, 2112),
        BF16,
        at,
        ffn_in,
        ffn_other,
        shared_dlin,
        cotangent,
        cot_other,
        shared_act,
        flops=2_200_000_000,
    )
    shared_sum = lax.psum_scatter(
        shared_grads.reshape(width, -1), ("x", "z", "y"), scatter_dimension=0, tiled=True
    ).reshape(2, 32, -1)

    gate_w, up_w, down_w = expert_gate[0], expert_up[0], expert_down[0]
    plain_grad = dot(expert_cot, down_w, 1, 1)
    expert_rows, shared_back, shared_out, plain_grad, shared_grads = lax.optimization_barrier(
        (expert_rows, shared_back, shared_out, plain_grad, shared_grads)
    )
    probs = jax.nn.softmax(dot(expert_rows, router_all), axis=1)
    mine = (jnp.arange(experts_count, dtype=jnp.int32) == expert)[None, :].astype(F32)
    gate = jnp.sum(probs * mine, axis=1, keepdims=True)
    gate_lin = dot(expert_rows, gate_w)
    up_lin = dot(expert_rows, up_w)
    silu, slope = silu_parts(gate_lin)
    act = silu * up_lin
    act_low = (gate * act).astype(BF16)
    inner = jnp.sum(act * plain_grad, axis=1, keepdims=True)
    act_grad = gate * plain_grad
    gate_grad = (act_grad * up_lin * slope).astype(BF16)
    up_grad = (act_grad * silu).astype(BF16)
    logit_grad = (inner * gate * (mine - probs)).astype(BF16)
    row_grad = (
        dot(gate_grad, gate_w, 1, 1) + dot(up_grad, up_w, 1, 1) + dot(logit_grad, router_all, 1, 1)
    ).astype(BF16)
    back_rows = return_rows(row_grad)
    piece = dot(act_low, down_w).astype(BF16)
    expert_down_grad = dot(act_low, expert_cot, 0, 0)[None]
    expert_gate_grad = dot(expert_rows, gate_grad, 0, 0)[None]
    expert_up_grad = dot(expert_rows, up_grad, 0, 0)[None]
    router_grad = dot(expert_rows, logit_grad, 0, 0)
    back_rows, piece, expert_down_grad, expert_gate_grad, expert_up_grad, router_grad = (
        lax.optimization_barrier(
            (back_rows, piece, expert_down_grad, expert_gate_grad, expert_up_grad, router_grad)
        )
    )
    routed_back = dot(slots, back_rows, 0, 0)
    cot_f = cotangent.astype(F32)
    ffn_grad = half_sum(shared_back + routed_back)
    resid_grad = cot_f + norm_back(ffn_grad * gain_two, normed_two, inverse_two)
    first_lane = jnp.broadcast_to(jnp.arange(64)[None, :] == 0, (rows, 64)).astype(BF16)
    ffn_gain_part = dot((ffn_grad * normed_two).astype(BF16), first_lane, 0, 0)

    resid_low = resid_grad.astype(BF16)
    resid_other = shift(resid_low, "c", 1)
    heads_grad = call(
        heads_kernel,
        [(rows, 256)] * 4,
        [BF16] * 4,
        at,
        resid_low,
        resid_other,
        out_all,
        scratch=[pltpu.VMEM((two, 512), BF16)],
        flops=600_000_000,
        many=True,
    )
    heads_got = to_ring(heads_grad)
    piece, heads_got[0] = lax.optimization_barrier((piece, heads_got[0]))
    back = call(
        backward_kernel,
        [(rows, MSG)] * 4,
        [BF16] * 4,
        at,
        msg,
        *heads_got,
        doc_row,
        doc_col,
        scratch=[
            pltpu.VMEM((4, rows, 256), BF16),
            pltpu.VMEM((4, rows, MSG), BF16),
            pltpu.VMEM((512, 256), F32),
            pltpu.VMEM((512, 128), F32),
        ],
        flops=1_500_000_000,
        many=True,
    )
    lin_grad, kv_grad, in_own, in_other = call(
        return_kernel,
        [(two, 1408), (two, 1024), (rows, width), (rows, width)],
        [BF16, BF16, F32, BF16],
        at,
        *to_ring(back),
        in_all,
        up_all,
        cosine,
        sine,
        latent_normed,
        latent_inverse,
        scratch=[pltpu.VMEM((512, 128), F32)],
        flops=1_800_000_000,
        many=True,
    )
    up_part = dot(latent_low, kv_grad, 0, 0).astype(BF16).reshape(width, 256)
    tail = jnp.concatenate([router_grad, ffn_gain_part], axis=1).astype(BF16)
    pieces = call(
        grads_kernel,
        [(4, 32, 2304)] * 16,
        [BF16] * 16,
        at,
        normed_low,
        lin_grad,
        resid_low,
        resid_other,
        attended,
        up_part,
        tail,
        scratch=[pltpu.VMEM((8, 32, 2304), BF16)],
        flops=2_200_000_000,
        many=True,
    )
    pairs = [pieces[2 * i : 2 * i + 2] for i in range(8)]
    attn_sum = scatter_rows(pairs[:4], pairs[4:])

    attn_in_grad = half_sum(core_sum(in_own, in_other))
    inverse_one = rms(tokens_f)
    input_grad = resid_grad + norm_back(attn_in_grad, tokens_f * inverse_one, inverse_one)
    routed_out = dot(slots, return_rows(piece), 0, 0)
    layer_out = (resid + half_sum(shared_out + routed_out)).astype(BF16)

    shared_sum = lax.all_to_all(shared_sum, "c", split_axis=0, concat_axis=0, tiled=True)
    shared_sum = shared_sum.astype(F32)
    query_sum = attn_sum[..., :768]
    up_sum = attn_sum[..., 1920:2176]
    down_sum = attn_sum[0, :, 768:1408] + attn_sum[1, :, 768:1408]
    down_sum = jnp.concatenate(
        [
            down_sum[:, :512],
            down_sum[:, 512:544] + down_sum[:, 544:576],
            down_sum[:, 576:608] + down_sum[:, 608:],
        ],
        axis=1,
    )
    attn_gain_part = jnp.sum(query_pack.astype(F32) * query_sum, axis=(0, 2)) + jnp.sum(
        latent_down.astype(F32) * down_sum, axis=1
    )
    latent_gain_part = jnp.sum(up_pack.reshape(2, 32, 256).astype(F32) * up_sum, axis=(0, 2))
    tail_sum = attn_sum[0, :, 2176:] + attn_sum[1, :, 2176:]
    small = jnp.concatenate(
        [down_sum, tail_sum[:, :64], attn_gain_part[:, None], latent_gain_part[:, None]], axis=1
    )
    small = small + shift(small, "t", 1)
    attn_gain_grad = small[:, 640]
    latent_gain_grad = jnp.sum(small[:, 641].reshape(8, 4), axis=1)
    latent_down_grad = gain_col * small[:, :576]
    router_out = small[:, 576:640]
    query_plain = query_sum[..., :512].reshape(2, 32, 2, 2, NOPE)
    query_turn = query_sum[..., 512:].reshape(2, 32, 2, 2, 2, 32).transpose(0, 1, 2, 4, 3, 5)
    query_turn = query_turn.reshape(2, 32, 2, 2, ROPE)
    query_out = jnp.concatenate([query_plain, query_turn], axis=4).transpose(1, 0, 2, 3, 4)
    query_out = gain_col * query_out.reshape(32, 2 * 4 * HEAD)
    up_out = up_sum.reshape(2, 8, 4, 256).transpose(1, 0, 2, 3).reshape(8, 2048)
    up_out = latent_gain.astype(F32)[:, None] * up_out
    out_out = attn_sum[..., 1408:1920].transpose(0, 2, 1).reshape(1024, 32)
    ffn_gain_grad = tail_sum[:, 64]
    shared_rows = shared_sum.transpose(1, 0, 2)
    return (
        layer_out,
        input_grad,
        attn_gain_grad,
        query_out,
        latent_down_grad,
        latent_gain_grad,
        up_out,
        out_out,
        ffn_gain_grad,
        router_out,
        shared_rows[..., :704].reshape(32, 1408),
        shared_rows[..., 704:1408].reshape(32, 1408),
        shared_sum[..., 1408:2112].transpose(0, 2, 1).reshape(1408, 32),
        expert_gate_grad,
        expert_up_grad,
        expert_down_grad,
    )


def solution(mesh):
    fine = Mesh(mesh.devices.reshape(4, 2, 2, 4, 2), ("x", "z", "c", "y", "t"))
    fsdp = ("x", "z", "c")
    every = ("x", "z", "c", "y")
    in_specs = (
        P(every, None),
        P(fsdp, None),
        P(every, None),
        P(every),
        P(every, "t"),
        P(every, None),
        P(every),
        P(every, "t"),
        P("t", every),
        P(every),
        P(every, None),
        P(every, "t"),
        P(every, "t"),
        P("t", every),
        P(every, None, "t"),
        P(every, None, "t"),
        P(every, "t", None),
        P(every, None),
    )
    out_specs = (
        P(every, None),
        P(every, None),
        P(every),
        P(every, "t"),
        P(every, None),
        P(every),
        P(every, "t"),
        P("t", every),
        P(every),
        P(every, None),
        P(every, "t"),
        P(every, "t"),
        P("t", every),
        P(every, None, "t"),
        P(every, None, "t"),
        P(every, "t", None),
    )
    return jax.shard_map(shards, mesh=fine, in_specs=in_specs, out_specs=out_specs, check_vma=False)
```

```python
import functools

import jax
import jax.numpy as jnp
import numpy as np
from jax import lax
from jax.experimental import pallas as pl
from jax.experimental.pallas import tpu as pltpu
from jax.sharding import Mesh
from jax.sharding import PartitionSpec as P

NOPE = 128
ROPE = 64
VDIM = 128
LATENT = 512
HEAD = NOPE + ROPE
EPS = 1e-06
SCALE = HEAD ** (-0.5)
F32 = jnp.float32
BF16 = jnp.bfloat16


def dot(left, right, left_dim=1, right_dim=0):
    return lax.dot_general(
        left, right, (((left_dim,), (right_dim,)), ((), ())), preferred_element_type=F32
    )


def shift(values, axis, step):
    size = lax.axis_size(axis)
    return lax.ppermute(values, axis, [(j, (j + step) % size) for j in range(size)])


def diagonal(values):
    return lax.ppermute(values, ("z", "c"), [(0, 3), (1, 2), (2, 1), (3, 0)])


def pick(buffer, index):
    return lax.dynamic_index_in_dim(buffer, index, 0, keepdims=False)


def in_order(own, other, index):
    return jnp.stack([jnp.where(index == 0, own, other), jnp.where(index == 0, other, own)])


def pack_kernel(
    at, query, down, up, out, gate, upper, lower, router, attn_gain, latent_gain, ffn_gain, *refs
):
    keep, send, *quarters, packs, shared_packs = refs
    scale = attn_gain[...].astype(F32)
    lat_scale = latent_gain[...].astype(F32)
    heads = query[...].astype(F32) * scale
    lows = down[...].astype(F32) * scale
    rotated = lows[:, 512:]
    ups = up[...].astype(F32) * lat_scale
    outs, gates, uppers, lowers = (ref[...].astype(F32) for ref in (out, gate, upper, lower))
    for half in range(2):
        first = half * 4 * HEAD
        plain = [heads[:, first + i * HEAD : first + i * HEAD + NOPE] for i in range(4)]
        turned = []
        for pair in range(2):
            for side in range(2):
                for i in (2 * pair, 2 * pair + 1):
                    start = first + i * HEAD + NOPE + 32 * side
                    turned.append(heads[:, start : start + 32])
        blocks = plain + [jnp.concatenate(turned, axis=1), lows[:, :512]]
        blocks.append(
            jnp.concatenate([rotated[:, :32], rotated[:, :32], rotated[:, 32:], rotated[:, 32:]], axis=1)
        )
        blocks.append(outs[:, half * 512 : half * 512 + 512])
        start = half * 1024
        blocks.append(
            jnp.concatenate([ups[:, start + j * 256 : start + j * 256 + 256] for j in range(4)], axis=0)
        )
        gain = jnp.broadcast_to(ffn_gain[...].astype(F32), (32, 64))
        blocks.append(jnp.concatenate([router[...].astype(F32), gain], axis=1))
        for side in range(2):
            index = half * 2 + side
            span = slice(index * 352, index * 352 + 352)
            parts = [gates[:, span], uppers[:, span], jnp.zeros((32, 64), F32)]
            parts += [lowers[:, span], jnp.zeros((32, 32), F32)]
            shared_packs[index] = jnp.concatenate(parts, axis=1).astype(BF16)
        at_lane = 0
        for block in blocks:
            size = block.shape[1]
            packs[half, :, at_lane : at_lane + size] = block.astype(BF16)
            at_lane += size
    keep[...] = packs[at[2]]
    send[...] = packs[1 - at[2]]
    core, side = at[2], at[1]
    places = (core * 2 + side, (1 - core) * 2 + side, core * 2 + 1 - side, (1 - core) * 2 + 1 - side)
    for ref, place in zip(quarters, places, strict=True):
        ref[...] = shared_packs[place]


LANES = 2304
QUARTER = 1152
DOWN = 768


def quad_exchange(parts):
    z, core = lax.axis_index("z"), lax.axis_index("c")
    stay, across, beside, corner = parts
    across, beside, corner = shift(across, "c", 1), shift(beside, "z", 1), diagonal(corner)
    return in_order(in_order(stay, across, core), in_order(beside, corner, core), z)


def quad_blocks(own):
    beside = shift(own, "z", 1)
    return [own, shift(own, "c", 1), beside, shift(beside, "c", 1)]


def quad_sum(own, across, beside, corner):
    own = own + shift(across, "c", 1).astype(F32)
    beside = beside + shift(corner, "c", 1).astype(F32)
    return own + shift(beside.astype(BF16), "z", 1).astype(F32)


def gather_rows(keep, send, at):
    across, beside, corner = shift(send, "c", 1), shift(keep, "z", 1), diagonal(send)
    first = [line_up(at, 0, keep, "x"), line_up(at, 0, beside, "x")]
    second = [line_up(at, 3, across, "y"), line_up(at, 3, corner, "y")]
    near = [
        [(shift(line, axis, 1), shift(line, axis, -1)) for line in lines]
        for lines, axis in ((first, "y"), (second, "x"))
    ]
    far = [
        (shift(pair[0][0], axis, 1), shift(pair[1][1], axis, -1))
        for pair, axis in zip(near, ("y", "x"), strict=True)
    ]
    pieces = []
    for lines, pair, last in zip((first, second), near, far, strict=True):
        for level in range(2):
            pieces += [lines[level], pair[level][0], pair[level][1], last[level]]
    return pieces


PLACES = (0, 3, 1, 2)


def fetch(at, pieces, lane, target, sems):
    size = target.shape[-1]
    copies = []
    for index, piece in enumerate(pieces):
        level = at[1] if index % 8 < 4 else 1 - at[1]
        step = PLACES[index % 4]
        if index < 8:
            place = target.at[:, level, at[2], lax.rem(at[3] + step, 4)]
        else:
            place = target.at[lax.rem(at[0] + step, 4), level, 1 - at[2]]
        copies.append(pltpu.make_async_copy(piece.at[:, :, pl.ds(lane, size)], place, sems.at[index]))
    for copy in copies:
        copy.start()
    return copies


def line_kernel(index, at, *refs):
    for step in range(4):
        refs[4][lax.rem(at[index] + 4 - step, 4)] = refs[step][...]


def line_up(at, index, block, axis):
    blocks = [block] + [shift(block, axis, step) for step in (1, 2, 3)]
    return call(
        functools.partial(line_kernel, index), (4,) + block.shape, BF16, at, *blocks
    )


def add_low(*values):
    return sum(value.astype(F32) for value in values).astype(BF16)


def ring_kernel(index, at, a0, a1, a2, b0, b1, b2, o0, o1, o2, o3, low, high):
    low[...] = (a0[...].astype(F32) + a1[...].astype(F32) + a2[...].astype(F32)).astype(BF16)
    high[...] = (b0[...].astype(F32) + b1[...].astype(F32) + b2[...].astype(F32)).astype(BF16)
    for step, out in enumerate((o0, o1, o2, o3)):
        place = lax.rem(at[index] + step, 4)
        out[0] = low[place]
        out[1] = high[place]


def ring_sum(parts, axis, at, index):
    low = shift(parts[2][0], axis, 1)
    high = shift(parts[2][1], axis, -1)
    right_high = shift(parts[1][1], axis, 1)
    left_low = shift(parts[3][0], axis, -1)
    right_low = shift(add_low(parts[1][0], low), axis, 1)
    left_high = shift(add_low(parts[3][1], high), axis, -1)
    shape = parts[0][0].shape
    return call(
        functools.partial(ring_kernel, index),
        [(2,) + shape[1:]] * 4,
        [BF16] * 4,
        at,
        parts[0][0],
        left_low,
        right_low,
        parts[0][1],
        right_high,
        left_high,
        scratch=[pltpu.VMEM(shape, BF16)] * 2,
        many=True,
    )


def sum_kernel(at, p0, p1, p2, p3, low, high):
    for level, out in enumerate((low, high)):
        total = p0[level].astype(F32) + p1[level].astype(F32)
        out[...] = (total + p2[level].astype(F32) + p3[level].astype(F32)).astype(BF16)


def direct_sum(pieces, axis, at):
    got = [pieces[0]] + [shift(pieces[step], axis, step) for step in (1, 2, 3)]
    shape = pieces[0].shape[1:]
    return call(sum_kernel, [shape] * 2, [BF16] * 2, at, *got, many=True)


def scatter_rows(one, two, at):
    one, two = ring_sum(one, "y", at, 0), ring_sum(two, "x", at, 3)
    one, two = direct_sum(one, "x", at), direct_sum(two, "y", at)
    return one[0], shift(one[1], "z", 1), shift(two[0], "c", 1), diagonal(two[1])


def to_ring(pieces):
    return [pieces[0]] + [shift(pieces[step], "y", step) for step in (1, 2, 3)]


def half_sum(partial):
    low = partial.astype(BF16)
    return low.astype(F32) + shift(low, "t", 1).astype(F32)


def core_sum(own, other):
    return own + shift(other, "c", 1).astype(F32)


def call(kernel, shapes, dtypes, at, *operands, scratch=(), flops=1_000_000, many=False, far=0, out_far=False):
    if not many:
        shapes, dtypes = [shapes], [dtypes]
    out_shape = [jax.ShapeDtypeStruct(s, d) for s, d in zip(shapes, dtypes, strict=True)]
    moved = sum(o.size * o.dtype.itemsize for o in operands)
    moved += sum(int(np.prod(s)) * jnp.dtype(d).itemsize for s, d in zip(shapes, dtypes, strict=True))
    outs = pl.pallas_call(
        kernel,
        out_shape=out_shape,
        in_specs=[pl.BlockSpec(memory_space=pltpu.SMEM)]
        + [pl.BlockSpec(memory_space=pl.ANY)] * far
        + [pl.BlockSpec(memory_space=pltpu.VMEM)] * (len(operands) - far),
        out_specs=[pl.BlockSpec(memory_space=pl.ANY if out_far else pltpu.VMEM)] * len(out_shape),
        scratch_shapes=scratch,
        compiler_params=pltpu.CompilerParams(vmem_limit_bytes=56 * 1024 * 1024),
        cost_estimate=pl.CostEstimate(flops=flops, bytes_accessed=moved, transcendentals=0),
    )(at, *operands)
    return outs if many else outs[0]


MSG = 1024
QR = 256
KV = 384
KR = 896


def rows_at(index):
    return pl.ds(pl.multiple_of(index * 128, 128), 128)


def lanes_at(index, size, base=0):
    return pl.ds(pl.multiple_of(base + index * size, 128), size)


def owner(at, place):
    return jnp.bitwise_xor(lax.shift_right_logical(place, 1), at[2]), jnp.bitwise_and(place, 1)


def ahead(at, step):
    return lax.rem(at[3] + step, 4)


def behind(at, step):
    return lax.rem(at[3] + 4 - step, 4)


def turn(values, cosine, sine):
    return values * cosine + pltpu.roll(values, 64, 1) * sine


def project_kernel(at, *refs):
    pieces = refs[:16]
    own, other, cosine, sine, m0, m1, m2, m3, normed, low, plain, inverse = refs[16:28]
    weights, out_weights, up, tail, query, keys, key, raw, sems = refs[28:]
    copies = fetch(at, pieces, 0, weights, sems.at[0])
    later = fetch(at, pieces, 1920, raw, sems.at[1])
    last = fetch(at, pieces, 1408, out_weights, sems.at[2])
    last += fetch(at, pieces, 2176, tail, sems.at[3])
    for index, block in enumerate((own, other)):
        values = block[...].astype(F32)
        scale = lax.rsqrt(jnp.mean(values * values, axis=1, keepdims=True) + EPS)
        normed[index * 128 : index * 128 + 128] = (values * scale).astype(BF16)
    for copy in copies:
        copy.wait()
    lin = dot(normed[...], weights[...].reshape(2048, 1408))
    cos, sin = cosine[...], sine[...]
    query[:, :512] = lin[:, :512].astype(BF16)
    for pair in range(2):
        span = slice(512 + pair * 128, 640 + pair * 128)
        query[:, span] = turn(lin[:, span], cos, sin).astype(BF16)
    key[...] = turn(lin[:, 1280:], cos, sin).astype(BF16)
    latent = lin[:, 768:1280]
    scale = lax.rsqrt(jnp.mean(latent * latent, axis=1, keepdims=True) + EPS)
    latent = latent * scale
    plain[...] = latent
    low[...] = latent.astype(BF16)
    inverse[...] = jnp.broadcast_to(scale, inverse.shape)
    for copy in later:
        copy.wait()
    ups = raw[...].astype(F32).reshape(64, 4, 8, 256)
    for head in range(4):
        span = slice(head * 256, head * 256 + 256)
        up[:, span] = ups[:, head].reshape(512, 256).astype(BF16)
    keys[...] = dot(low[...], up[...]).astype(BF16)
    for step, out in enumerate((m0, m1, m2, m3)):
        block, pair = owner(at, ahead(at, step))
        rows = rows_at(block)
        out[:, :QR] = query[rows, lanes_at(pair, 256)]
        out[:, QR:KV] = query[rows, lanes_at(pair, 128, 512)]
        out[:, KV:KR] = keys[rows, lanes_at(pair, 512)]
        out[:, KR:] = key[rows, :]
    for copy in last:
        copy.wait()


def head_lanes(rows, head):
    lane = lax.broadcasted_iota(jnp.int32, (rows, 128), 1)
    return jnp.where(((lane >> 5) & 1) == head, 1.0, 0.0).astype(F32)


def head_keys(msg_ref, head):
    rotated = msg_ref[:, :, KR:].reshape(512, 128).astype(F32) * head_lanes(512, head)
    plain = msg_ref[:, :, KV + head * 256 : KV + head * 256 + 128].reshape(512, 128)
    return jnp.concatenate([plain, rotated.astype(BF16)], axis=1)


def head_values(msg_ref, head):
    return msg_ref[:, :, KV + head * 256 + 128 : KV + head * 256 + 256].reshape(512, 128)


def block_probs(query, keys, row_ref, col_ref, block):
    count = (block + 1) * 128
    scores = dot(query, keys[:count], 1, 1) * SCALE
    rows = lax.broadcasted_iota(jnp.int32, (128, count), 0) + block * 128
    cols = lax.broadcasted_iota(jnp.int32, (128, count), 1)
    same = col_ref[block * 128 : count, :] == row_ref[:, :count]
    scores = jnp.where(same & (cols <= rows), scores, -1e30)
    powers = jnp.exp(scores - jnp.max(scores, axis=1, keepdims=True))
    return powers / jnp.sum(powers, axis=1, keepdims=True)


def block_query(msg_ref, head, block):
    return jnp.concatenate(
        [msg_ref[block, :, head * 128 : head * 128 + 128], msg_ref[block, :, QR:KV]], axis=1
    )


def forward_kernel(at, m0, m1, m2, m3, row_ref, col_ref, msg_ref, o0, o1, o2, o3, mixed):
    for step, piece in enumerate((m0, m1, m2, m3)):
        msg_ref[behind(at, step)] = piece[...]
    for head in range(2):
        keys = head_keys(msg_ref, head)
        values = head_values(msg_ref, head)
        for block in range(4):
            query = block_query(msg_ref, head, block)
            probs = block_probs(query, keys, row_ref, col_ref, block)
            part = dot(probs.astype(BF16), values[: (block + 1) * 128])
            mixed[block, :, head * 128 : head * 128 + 128] = part.astype(BF16)
    for step, out in enumerate((o0, o1, o2, o3)):
        out[...] = mixed[ahead(at, step)]


def output_kernel(at, p0, p1, p2, p3, weights, attended, own, other):
    for step, piece in enumerate((p0, p1, p2, p3)):
        block, pair = owner(at, behind(at, step))
        attended[rows_at(block), lanes_at(pair, 256)] = piece[...]
    own[...] = dot(attended[:128], weights[...], 1, 1)
    other[...] = dot(attended[128:], weights[...], 1, 1).astype(BF16)


def heads_kernel(at, own, other, weights, h0, h1, h2, h3, grad):
    grad[:128] = dot(own[...], weights[...]).astype(BF16)
    grad[128:] = dot(other[...], weights[...]).astype(BF16)
    for step, out in enumerate((h0, h1, h2, h3)):
        block, pair = owner(at, ahead(at, step))
        out[...] = grad[rows_at(block), lanes_at(pair, 256)]


def backward_kernel(
    at, msg_ref, g0, g1, g2, g3, row_ref, col_ref, o0, o1, o2, o3, grad_ref, out_ref, key_acc, value_acc
):
    for step, piece in enumerate((g0, g1, g2, g3)):
        grad_ref[behind(at, step)] = piece[...]
    for head in range(2):
        keys = head_keys(msg_ref, head)
        values = head_values(msg_ref, head)
        key_acc[...] = jnp.zeros_like(key_acc)
        value_acc[...] = jnp.zeros_like(value_acc)
        lanes = head_lanes(128, head)
        for block in range(4):
            count = (block + 1) * 128
            query = block_query(msg_ref, head, block)
            probs = block_probs(query, keys, row_ref, col_ref, block)
            grad = grad_ref[block, :, head * 128 : head * 128 + 128]
            probs_grad = dot(grad, values[:count], 1, 1)
            inner = jnp.sum(probs * probs_grad, axis=1, keepdims=True)
            score_grad = (probs * (probs_grad - inner) * SCALE).astype(BF16)
            query_grad = dot(score_grad, keys[:count])
            out_ref[block, :, head * 128 : head * 128 + 128] = query_grad[:, :128].astype(BF16)
            turned = query_grad[:, 128:]
            if head == 1:
                turned = turned + out_ref[block, :, QR:KV].astype(F32)
            out_ref[block, :, QR:KV] = turned.astype(BF16)
            key_acc[:count] += dot(score_grad, query, 0, 0)
            value_acc[:count] += dot(probs.astype(BF16), grad, 0, 0)
        base = KV + head * 256
        for block in range(4):
            span = slice(block * 128, block * 128 + 128)
            out_ref[block, :, base : base + 128] = key_acc[span, :128].astype(BF16)
            out_ref[block, :, base + 128 : base + 256] = value_acc[span, :].astype(BF16)
            turned = key_acc[span, 128:] * lanes
            if head == 1:
                turned = turned + out_ref[block, :, KR:].astype(F32)
            out_ref[block, :, KR:] = turned.astype(BF16)
    for step, out in enumerate((o0, o1, o2, o3)):
        out[...] = out_ref[ahead(at, step)]


def return_kernel(
    at, b0, b1, b2, b3, weights, up, cosine, sine, plain, inverse, lin_grad, kv_grad, own, other, key
):
    for step, piece in enumerate((b0, b1, b2, b3)):
        block, pair = owner(at, behind(at, step))
        rows = rows_at(block)
        lin_grad[rows, lanes_at(pair, 256)] = piece[:, :QR]
        turned = turn(piece[:, QR:KV].astype(F32), cosine[rows, :], -sine[rows, :])
        lin_grad[rows, lanes_at(pair, 128, 512)] = turned.astype(BF16)
        kv_grad[rows, lanes_at(pair, 512)] = piece[:, KV:KR]
        key[rows_at(block + 2 * pair), :] = piece[:, KR:].astype(F32)
    turned = turn(key[:256] + key[256:], cosine[...], -sine[...])
    lin_grad[:, 1280:] = turned.astype(BF16)
    grad = dot(kv_grad[...], up[...], 1, 1)
    latent = plain[...]
    grad = inverse[:, :1] * (grad - latent * jnp.mean(grad * latent, axis=1, keepdims=True))
    lin_grad[:, 768:1280] = grad.astype(BF16)
    own[...] = dot(lin_grad[:128], weights[...], 1, 1)
    other[...] = dot(lin_grad[128:], weights[...], 1, 1).astype(BF16)


def grads_kernel(at, normed, lin_grad, own, other, attended, low, kv_grad, tail, *refs):
    one, two, rows, ups = refs[:8], refs[8:16], refs[16], refs[17]
    for head in range(4):
        span = slice(head * 256, head * 256 + 256)
        ups[:, head] = dot(low[...], kv_grad[:, span], 0, 0).reshape(64, 8, 256)
    for step in range(4):
        column = lax.rem(at[0] + step, 4)
        for side in range(2):
            level = at[1] if side == 0 else 1 - at[1]
            chunk = column * 2 + level
            span = pl.ds(pl.multiple_of(chunk * 256, 256), 256)
            part = dot(normed[:, span], lin_grad[...], 0, 0).astype(BF16)
            rows[:, :, :1408] = part.reshape(8, 32, 1408)
            part = dot(own[:, span], attended[:128], 0, 0) + dot(other[:, span], attended[128:], 0, 0)
            rows[:, :, 1408:1920] = part.astype(BF16).reshape(8, 32, 512)
            rows[:, :, 1920:2176] = ups[pl.ds(chunk * 8, 8)].reshape(8, 32, 256).astype(BF16)
            rows[:, :, 2176:] = tail[span, :].reshape(8, 32, 128)
            for place in range(4):
                one[place * 2 + side][column] = rows[at[2] * 4 + ahead(at, place)]
            two[step * 2 + side][...] = rows[pl.ds((1 - at[2]) * 4, 4)]


def shared_kernel(at, gathered, *refs):
    ffn_blocks, cot_blocks, outs, backs, grads = refs[:4], refs[4:8], refs[8:12], refs[12:16], refs[16]
    weights, ffn, cot, lin_grad, act, sems = refs[17:]
    copies = []
    for z in range(2):
        for core in range(2):
            copies.append(
                pltpu.make_async_copy(
                    gathered.at[:, :, z, core], weights.at[:, z, core], sems.at[2 * z + core]
                )
            )
    for copy in copies:
        copy.start()
    for i in range(4):
        ffn[i * 128 : i * 128 + 128] = ffn_blocks[i][...]
        cot[i * 128 : i * 128 + 128] = cot_blocks[i][...]
    for copy in copies:
        copy.wait()
    gate_up = weights[:, :, :, :, :, :704].reshape(2048, 704)
    down = weights[:, :, :, :, :, DOWN : DOWN + 352].reshape(2048, 352)
    lin = dot(ffn[...], gate_up)
    act_grad = dot(cot[...], down)
    up_lin = lin[:, 352:]
    silu, slope = silu_parts(lin[:, :352])
    act[...] = (silu * up_lin).astype(BF16)
    both = jnp.concatenate([act_grad * up_lin * slope, act_grad * silu], axis=1)
    lin_grad[...] = both.astype(BF16)
    back = dot(lin_grad[...], gate_up, 1, 1)
    out = dot(act[...], down, 1, 1)
    for i in range(4):
        span = slice(i * 128, i * 128 + 128)
        backs[i][...] = back[span].astype(backs[i].dtype)
        outs[i][...] = out[span].astype(outs[i].dtype)
    for block in range(8):
        span = slice(block * 256, block * 256 + 256)
        part = dot(ffn[:, span], lin_grad[...], 0, 0).astype(BF16).reshape(2, 4, 32, 704)
        low = dot(cot[:, span], act[...], 0, 0).astype(BF16).reshape(2, 4, 32, 352)
        for core in range(2):
            grads[block // 2, :, block % 2, core, :, :704] = part[core]
            grads[block // 2, :, block % 2, core, :, DOWN : DOWN + 352] = low[core]
            grads[block // 2, :, block % 2, core, :, 704:DOWN] = jnp.zeros((4, 32, 64), BF16)
            grads[block // 2, :, block % 2, core, :, DOWN + 352 :] = jnp.zeros((4, 32, 32), BF16)


def finish_kernel(at, p0, p1, p2, p3, query, down, up, attn_gain, latent_gain, *outs):
    query_out, up_out, out_out, small, ffn_gain_out = outs
    own = p0[...].astype(F32) + p1[...].astype(F32)
    other = p2[...].astype(F32) + p3[...].astype(F32)
    first = at[2] == 0
    halves = [jnp.where(first, own, other), jnp.where(first, other, own)]
    heads, lifts = [], []
    for half in halves:
        for head in range(4):
            pair, place = head // 2, head % 2
            heads.append(half[:, head * 128 : head * 128 + 128])
            for side in range(2):
                start = 512 + pair * 128 + side * 64 + place * 32
                heads.append(half[:, start : start + 32])
        lifts += [half[8 * j : 8 * j + 8, 1920:2176] for j in range(4)]
    grads = jnp.concatenate(heads, axis=1)
    query_out[...] = grads * attn_gain[...].astype(F32)
    part = jnp.sum(grads * query[...].astype(F32), axis=1, keepdims=True)
    lift = jnp.concatenate(lifts, axis=1)
    up_out[...] = lift * latent_gain[...].astype(F32)
    lift_part = jnp.sum(lift * up[...].astype(F32), axis=1, keepdims=True)
    out_out[:, :512] = halves[0][:, 1408:1920]
    out_out[:, 512:] = halves[1][:, 1408:1920]
    both = own + other
    small[:, :512] = both[:, 768:1280]
    turned = jnp.concatenate(
        [
            both[:, 1280:1312] + both[:, 1312:1344],
            both[:, 1344:1376] + both[:, 1376:1408],
            both[:, 2176:2240],
        ],
        axis=1,
    )
    small[:, 512:640] = turned
    part += jnp.sum(down[:, :512].astype(F32) * both[:, 768:1280], axis=1, keepdims=True)
    part += jnp.sum(down[:, 512:].astype(F32) * turned[:, :64], axis=1, keepdims=True)
    small[:, 640:768] = jnp.broadcast_to(part, (32, 128))
    small[:, 768:] = jnp.zeros((32, 128), F32)
    small[:8, 768:] = jnp.broadcast_to(lift_part, (8, 128))
    ffn_gain_out[...] = both[:, 2240:2241]


def shared_finish_kernel(at, stay, across, beside, corner, gate, up, down):
    core, side = at[2] == 0, at[1] == 0
    own = [ref[...].astype(F32) for ref in (stay, beside)]
    other = [ref[...].astype(F32) for ref in (across, corner)]
    own = [jnp.where(side, own[0], own[1]), jnp.where(side, own[1], own[0])]
    other = [jnp.where(side, other[0], other[1]), jnp.where(side, other[1], other[0])]
    parts = [jnp.where(core, a, b) for a, b in zip(own, other, strict=True)]
    parts += [jnp.where(core, b, a) for a, b in zip(own, other, strict=True)]
    gate[...] = jnp.concatenate([part[:, :352] for part in parts], axis=1)
    up[...] = jnp.concatenate([part[:, 352:704] for part in parts], axis=1)
    down[...] = jnp.concatenate([part[:, DOWN : DOWN + 352] for part in parts], axis=1)


def doc_positions(doc_row):
    places = jnp.arange(doc_row.shape[0], dtype=jnp.int32)
    starts = jnp.concatenate([jnp.ones((1,), bool), doc_row[1:] != doc_row[:-1]])
    begins = lax.cummax(jnp.where(starts, places, 0), axis=0)
    return places - begins


def norm_back(scaled, normed, inverse):
    return inverse * (scaled - normed * jnp.mean(scaled * normed, axis=1, keepdims=True))


def silu_parts(lin):
    sig = jax.nn.sigmoid(lin)
    return lin * sig, sig * (1.0 + lin * (1.0 - sig))


def rms(values):
    return lax.rsqrt(jnp.mean(values * values, axis=1, keepdims=True) + EPS)


def shards(
    tokens_in,
    documents,
    routes,
    attn_gain,
    query_weight,
    latent_down,
    latent_gain,
    latent_up,
    output_weight,
    ffn_gain,
    router,
    shared_gate,
    shared_up,
    shared_down,
    expert_gate,
    expert_up,
    expert_down,
    cotangent,
):
    core = lax.axis_index("c")
    spot = lax.axis_index("y")
    at = jnp.stack([lax.axis_index("x"), lax.axis_index("z"), core, spot]).astype(jnp.int32)
    expert = (lax.axis_index("x") * 4 + lax.axis_index("z") * 2 + core) * 4 + spot
    rows = tokens_in.shape[0]
    width = tokens_in.shape[1]
    experts_count = router.shape[1]
    capacity = 16
    every = ("x", "z", "c", "y")

    keep, send, *quarters = call(
        pack_kernel,
        [(32, LANES)] * 2 + [(32, QUARTER)] * 4,
        [BF16] * 6,
        at,
        query_weight,
        latent_down,
        latent_up,
        output_weight.T,
        shared_gate,
        shared_up,
        shared_down.T,
        router,
        attn_gain[:, None],
        latent_gain[:, None],
        ffn_gain[:, None],
        scratch=[pltpu.VMEM((2, 32, LANES), BF16), pltpu.VMEM((4, 32, QUARTER), BF16)],
        many=True,
    )
    pieces = gather_rows(keep, send, at)
    shared_rows = quad_exchange(quarters).reshape(128, QUARTER)
    cot_four = quad_blocks(cotangent)

    named = jnp.any(
        routes.T[None, :, :] == jnp.arange(experts_count, dtype=jnp.int32)[:, None, None], axis=1
    )
    before = jnp.arange(rows)[:, None] < jnp.arange(rows)[None, :]
    place = dot(named.astype(BF16), before.astype(BF16))
    slots = (
        named[:, None, :] & (place[:, None, :] == jnp.arange(capacity, dtype=F32)[None, :, None])
    ).astype(BF16)
    slots = slots.reshape(experts_count * capacity, rows)

    def exchange_rows(values):
        sent = values.reshape(experts_count, capacity, width)
        got = lax.all_to_all(sent, every, split_axis=0, concat_axis=0, tiled=True)
        return got.reshape(-1, width)

    docs = jnp.concatenate([documents, shift(documents, "c", 1)])
    positions = jax.vmap(doc_positions)(docs)
    local_pos = lax.dynamic_slice_in_dim(positions, spot * rows, rows, axis=1).reshape(-1)
    steps = jnp.arange(ROPE // 2, dtype=F32)
    angles = local_pos.astype(F32)[:, None] * (10000.0 ** (-steps / (ROPE // 2)))[None, :]
    cosine = jnp.tile(jnp.cos(angles), (1, 4))
    sine = jnp.sin(angles)
    sine = jnp.concatenate([-sine, -sine, sine, sine], axis=1)
    doc = jnp.where(spot // 2 == core, docs[0], docs[1])
    doc_row, doc_col = doc[None, :], doc[:, None]

    tokens_other = shift(tokens_in, "c", 1)
    cot_sent = dot(slots, cotangent).astype(BF16)
    cot_sent, pieces, shared_rows, cot_four, cosine, sine, doc_row, doc_col, tokens_other = (
        lax.optimization_barrier(
            (cot_sent, pieces, shared_rows, cot_four, cosine, sine, doc_row, doc_col, tokens_other)
        )
    )
    expert_cot = exchange_rows(cot_sent)
    shared_all = lax.all_gather(shared_rows, ("x", "y"), axis=0, tiled=True)
    shared_all = shared_all.reshape(4, 4, 2, 2, 32, QUARTER)
    sent = [(rows, MSG)] * 4
    two = 2 * rows
    six = (4, 2, 2, 4, 32)
    outs = call(
        project_kernel,
        sent
        + [(two, width), (two, LATENT), (two, LATENT), (two, 128)]
        + [six + (1408,), six + (512,), (LATENT, 1024), six + (128,)],
        [BF16] * 6 + [F32, F32] + [BF16] * 4,
        at,
        *pieces,
        tokens_in,
        tokens_other,
        cosine,
        sine,
        scratch=[
            pltpu.VMEM((two, 768), BF16),
            pltpu.VMEM((two, 1024), BF16),
            pltpu.VMEM((two, 128), BF16),
            pltpu.VMEM(six + (256,), BF16),
            pltpu.SemaphoreType.DMA((4, 16)),
        ],
        flops=1_800_000_000,
        many=True,
        far=16,
    )
    sent, normed_low, latent_low, latent_normed, latent_inverse = outs[:4], *outs[4:8]
    in_all, out_all = outs[8].reshape(width, 1408), outs[9].reshape(width, 512)
    up_all, tail_all = outs[10], outs[11].reshape(width, 128)
    received = to_ring(sent)
    received, expert_cot = lax.optimization_barrier((received, expert_cot))
    msg, *mixed = call(
        forward_kernel,
        [(4, rows, MSG)] + [(rows, 256)] * 4,
        [BF16] * 5,
        at,
        *received,
        doc_row,
        doc_col,
        scratch=[pltpu.VMEM((4, rows, 256), BF16)],
        flops=500_000_000,
        many=True,
    )
    attended, out_own, out_other = call(
        output_kernel,
        [(two, 512), (rows, width), (rows, width)],
        [BF16, F32, BF16],
        at,
        *to_ring(mixed),
        out_all,
        flops=600_000_000,
        many=True,
    )
    tokens_f = tokens_in.astype(F32)
    resid = tokens_f + half_sum(core_sum(out_own, out_other))

    pointer = jnp.broadcast_to(jnp.arange(128)[None, :] == 64, (8, 128)).astype(BF16)
    gain_two = dot(pointer, tail_all, 1, 1)[:1]
    router_all = tail_all[:, :64]
    inverse_two = rms(resid)
    normed_two = resid * inverse_two
    ffn_in = (normed_two * gain_two).astype(BF16)
    ffn_sent = dot(slots, ffn_in).astype(BF16)
    ffn_four, ffn_sent = lax.optimization_barrier((quad_blocks(ffn_in), ffn_sent))
    expert_rows = exchange_rows(ffn_sent)

    *shared_parts, shared_grads = call(
        shared_kernel,
        [(rows, width)] * 8 + [(4, 4, 2, 2, 32, QUARTER)],
        [F32, BF16, F32, BF16] * 2 + [BF16],
        at,
        shared_all,
        *ffn_four,
        *cot_four,
        scratch=[
            pltpu.VMEM((4, 2, 2, 4, 32, QUARTER), BF16),
            pltpu.VMEM((4 * rows, width), BF16),
            pltpu.VMEM((4 * rows, width), BF16),
            pltpu.VMEM((4 * rows, 704), BF16),
            pltpu.VMEM((4 * rows, 352), BF16),
            pltpu.SemaphoreType.DMA((4,)),
        ],
        flops=7_000_000_000,
        many=True,
        far=1,
    )
    shared_back = quad_sum(*shared_parts[4:])
    shared_sum = lax.psum_scatter(
        shared_grads.reshape(width, QUARTER), ("x", "y"), scatter_dimension=0, tiled=True
    ).reshape(2, 2, 32, QUARTER)
    own_rows, far_rows = pick(shared_sum, at[1]), pick(shared_sum, 1 - at[1])
    stay, beside = pick(own_rows, core), shift(pick(far_rows, core), "z", 1)
    across, corner = shift(pick(own_rows, 1 - core), "c", 1), diagonal(pick(far_rows, 1 - core))
    shared_gate_grad, shared_up_grad, shared_down_grad = call(
        shared_finish_kernel,
        [(32, 1408)] * 3,
        [F32] * 3,
        at,
        stay,
        across,
        beside,
        corner,
        many=True,
    )
    gate_w, up_w, down_w = expert_gate[0], expert_up[0], expert_down[0]
    plain_grad = dot(expert_cot, down_w, 1, 1)
    expert_rows, plain_grad, shared_parts, shared_grads = lax.optimization_barrier(
        (expert_rows, plain_grad, shared_parts, shared_grads)
    )
    probs = jax.nn.softmax(dot(expert_rows, router_all), axis=1)
    mine = (jnp.arange(experts_count, dtype=jnp.int32) == expert)[None, :].astype(F32)
    gate = jnp.sum(probs * mine, axis=1, keepdims=True)
    gate_lin = dot(expert_rows, gate_w)
    up_lin = dot(expert_rows, up_w)
    silu, slope = silu_parts(gate_lin)
    act = silu * up_lin
    act_low = (gate * act).astype(BF16)
    inner = jnp.sum(act * plain_grad, axis=1, keepdims=True)
    act_grad = gate * plain_grad
    gate_grad = (act_grad * up_lin * slope).astype(BF16)
    up_grad = (act_grad * silu).astype(BF16)
    logit_grad = (inner * gate * (mine - probs)).astype(BF16)
    row_grad = (
        dot(gate_grad, gate_w, 1, 1) + dot(up_grad, up_w, 1, 1) + dot(logit_grad, router_all, 1, 1)
    ).astype(BF16)
    back_rows = exchange_rows(row_grad)
    piece = dot(act_low, down_w).astype(BF16)
    expert_down_grad = dot(act_low, expert_cot, 0, 0)[None]
    expert_gate_grad = dot(expert_rows, gate_grad, 0, 0)[None]
    expert_up_grad = dot(expert_rows, up_grad, 0, 0)[None]
    router_grad = dot(expert_rows, logit_grad, 0, 0)
    back_rows, piece, expert_down_grad, expert_gate_grad, expert_up_grad, router_grad, shared_back = (
        lax.optimization_barrier(
            (back_rows, piece, expert_down_grad, expert_gate_grad, expert_up_grad, router_grad, shared_back)
        )
    )
    routed_back = dot(slots, back_rows, 0, 0)
    cot_f = cotangent.astype(F32)
    ffn_grad = half_sum(shared_back + routed_back)
    resid_grad = cot_f + norm_back(ffn_grad * gain_two, normed_two, inverse_two)
    first_lane = jnp.broadcast_to(jnp.arange(64)[None, :] == 0, (rows, 64)).astype(BF16)
    ffn_gain_part = dot((ffn_grad * normed_two).astype(BF16), first_lane, 0, 0)

    resid_low = resid_grad.astype(BF16)
    resid_other = shift(resid_low, "c", 1)
    heads_grad = call(
        heads_kernel,
        [(rows, 256)] * 4,
        [BF16] * 4,
        at,
        resid_low,
        resid_other,
        out_all,
        scratch=[pltpu.VMEM((two, 512), BF16)],
        flops=600_000_000,
        many=True,
    )
    heads_got = to_ring(heads_grad)
    heads_got, shared_gate_grad, shared_up_grad, shared_down_grad = lax.optimization_barrier(
        (heads_got, shared_gate_grad, shared_up_grad, shared_down_grad)
    )
    back = call(
        backward_kernel,
        [(rows, MSG)] * 4,
        [BF16] * 4,
        at,
        msg,
        *heads_got,
        doc_row,
        doc_col,
        scratch=[
            pltpu.VMEM((4, rows, 256), BF16),
            pltpu.VMEM((4, rows, MSG), BF16),
            pltpu.VMEM((512, 256), F32),
            pltpu.VMEM((512, 128), F32),
        ],
        flops=1_500_000_000,
        many=True,
    )
    returned, piece = lax.optimization_barrier((to_ring(back), piece))
    piece_rows = exchange_rows(piece)
    lin_grad, kv_grad, in_own, in_other = call(
        return_kernel,
        [(two, 1408), (two, 1024), (rows, width), (rows, width)],
        [BF16, BF16, F32, BF16],
        at,
        *returned,
        in_all,
        up_all,
        cosine,
        sine,
        latent_normed,
        latent_inverse,
        scratch=[pltpu.VMEM((512, 128), F32)],
        flops=1_800_000_000,
        many=True,
    )
    tail = jnp.concatenate([router_grad, ffn_gain_part], axis=1).astype(BF16)
    blocks = call(
        grads_kernel,
        [(4, 32, 2304)] * 16,
        [BF16] * 16,
        at,
        normed_low,
        lin_grad,
        resid_low,
        resid_other,
        attended,
        latent_low,
        kv_grad,
        tail,
        scratch=[pltpu.VMEM((8, 32, 2304), BF16), pltpu.VMEM((64, 4, 8, 256), F32)],
        flops=2_200_000_000,
        many=True,
    )
    blocks = list(blocks)
    blocks[4], blocks[5], blocks[12], blocks[13], piece_rows = lax.optimization_barrier(
        (blocks[4], blocks[5], blocks[12], blocks[13], piece_rows)
    )
    pairs = [blocks[2 * i : 2 * i + 2] for i in range(8)]
    attn_sum = scatter_rows(pairs[:4], pairs[4:], at)

    attn_in_grad = half_sum(core_sum(in_own, in_other))
    inverse_one = rms(tokens_f)
    input_grad = resid_grad + norm_back(attn_in_grad, tokens_f * inverse_one, inverse_one)
    routed_out = dot(slots, piece_rows, 0, 0)
    shared_out = quad_sum(*shared_parts[:4])
    layer_out = (resid + half_sum(shared_out + routed_out)).astype(BF16)

    query_out, up_out, out_out, small, ffn_gain_grad = call(
        finish_kernel,
        [(32, 1536), (8, 2048), (32, 1024), (32, 896), (32, 1)],
        [F32] * 5,
        at,
        *attn_sum,
        query_weight,
        latent_down,
        latent_up,
        attn_gain[:, None],
        latent_gain[:, None],
        many=True,
    )
    small = small + shift(small, "t", 1)
    return (
        layer_out,
        input_grad,
        small[:, 640],
        query_out,
        attn_gain.astype(F32)[:, None] * small[:, :576],
        small[:8, 768],
        up_out,
        out_out.T,
        ffn_gain_grad[:, 0],
        small[:, 576:640],
        shared_gate_grad,
        shared_up_grad,
        shared_down_grad.T,
        expert_gate_grad,
        expert_up_grad,
        expert_down_grad,
    )


def solution(mesh):
    fine = Mesh(mesh.devices.reshape(4, 2, 2, 4, 2), ("x", "z", "c", "y", "t"))
    fsdp = ("x", "z", "c")
    every = ("x", "z", "c", "y")
    in_specs = (
        P(every, None),
        P(fsdp, None),
        P(every, None),
        P(every),
        P(every, "t"),
        P(every, None),
        P(every),
        P(every, "t"),
        P("t", every),
        P(every),
        P(every, None),
        P(every, "t"),
        P(every, "t"),
        P("t", every),
        P(every, None, "t"),
        P(every, None, "t"),
        P(every, "t", None),
        P(every, None),
    )
    out_specs = (
        P(every, None),
        P(every, None),
        P(every),
        P(every, "t"),
        P(every, None),
        P(every),
        P(every, "t"),
        P("t", every),
        P(every),
        P(every, None),
        P(every, "t"),
        P(every, "t"),
        P("t", every),
        P(every, None, "t"),
        P(every, None, "t"),
        P(every, "t", None),
    )
    return jax.shard_map(shards, mesh=fine, in_specs=in_specs, out_specs=out_specs, check_vma=False)
```

```python
import functools

import jax
import jax.numpy as jnp
import numpy as np
from jax import lax
from jax.experimental import pallas as pl
from jax.experimental.pallas import tpu as pltpu
from jax.sharding import Mesh
from jax.sharding import PartitionSpec as P

NOPE = 128
ROPE = 64
VDIM = 128
LATENT = 512
HEAD = NOPE + ROPE
EPS = 1e-06
SCALE = HEAD ** (-0.5)
F32 = jnp.float32
BF16 = jnp.bfloat16


def dot(left, right, left_dim=1, right_dim=0):
    return lax.dot_general(
        left, right, (((left_dim,), (right_dim,)), ((), ())), preferred_element_type=F32
    )


def shift(values, axis, step):
    size = lax.axis_size(axis)
    return lax.ppermute(values, axis, [(j, (j + step) % size) for j in range(size)])


def diagonal(values):
    return lax.ppermute(values, ("z", "c"), [(0, 3), (1, 2), (2, 1), (3, 0)])


def pick(buffer, index):
    return lax.dynamic_index_in_dim(buffer, index, 0, keepdims=False)


def in_order(own, other, index):
    return jnp.stack([jnp.where(index == 0, own, other), jnp.where(index == 0, other, own)])


def pack_kernel(
    at, query, down, up, out, gate, upper, lower, router, attn_gain, latent_gain, ffn_gain, *refs
):
    keep, send, *quarters, packs, shared_packs = refs
    scale = attn_gain[...].astype(F32)
    lat_scale = latent_gain[...].astype(F32)
    heads = query[...].astype(F32) * scale
    lows = down[...].astype(F32) * scale
    rotated = lows[:, 512:]
    ups = up[...].astype(F32) * lat_scale
    outs, gates, uppers, lowers = (ref[...].astype(F32) for ref in (out, gate, upper, lower))
    for half in range(2):
        first = half * 4 * HEAD
        plain = [heads[:, first + i * HEAD : first + i * HEAD + NOPE] for i in range(4)]
        turned = []
        for pair in range(2):
            for side in range(2):
                for i in (2 * pair, 2 * pair + 1):
                    start = first + i * HEAD + NOPE + 32 * side
                    turned.append(heads[:, start : start + 32])
        blocks = plain + [jnp.concatenate(turned, axis=1), lows[:, :512]]
        blocks.append(
            jnp.concatenate([rotated[:, :32], rotated[:, :32], rotated[:, 32:], rotated[:, 32:]], axis=1)
        )
        blocks.append(outs[:, half * 512 : half * 512 + 512])
        start = half * 1024
        blocks.append(
            jnp.concatenate([ups[:, start + j * 256 : start + j * 256 + 256] for j in range(4)], axis=0)
        )
        gain = jnp.broadcast_to(ffn_gain[...].astype(F32), (32, 64))
        blocks.append(jnp.concatenate([router[...].astype(F32), gain], axis=1))
        for side in range(2):
            index = half * 2 + side
            span = slice(index * 352, index * 352 + 352)
            parts = [gates[:, span], uppers[:, span], jnp.zeros((32, 64), F32)]
            parts += [lowers[:, span], jnp.zeros((32, 32), F32)]
            shared_packs[index] = jnp.concatenate(parts, axis=1).astype(BF16)
        at_lane = 0
        for block in blocks:
            size = block.shape[1]
            packs[half, :, at_lane : at_lane + size] = block.astype(BF16)
            at_lane += size
    keep[...] = packs[at[2]]
    send[...] = packs[1 - at[2]]
    core, side = at[2], at[1]
    places = (core * 2 + side, (1 - core) * 2 + side, core * 2 + 1 - side, (1 - core) * 2 + 1 - side)
    for ref, place in zip(quarters, places, strict=True):
        ref[...] = shared_packs[place]


LANES = 2304
QUARTER = 1152
DOWN = 768


def quad_exchange(parts):
    z, core = lax.axis_index("z"), lax.axis_index("c")
    stay, across, beside, corner = parts
    across, beside, corner = shift(across, "c", 1), shift(beside, "z", 1), diagonal(corner)
    return in_order(in_order(stay, across, core), in_order(beside, corner, core), z)


def quad_blocks(own):
    beside = shift(own, "z", 1)
    return [own, shift(own, "c", 1), beside, shift(beside, "c", 1)]


def gather_rows(keep, send, at):
    across, beside, corner = shift(send, "c", 1), shift(keep, "z", 1), diagonal(send)
    first = [line_up(at, 0, keep, "x"), line_up(at, 0, beside, "x")]
    second = [line_up(at, 3, across, "y"), line_up(at, 3, corner, "y")]
    near = [
        [(shift(line, axis, 1), shift(line, axis, -1)) for line in lines]
        for lines, axis in ((first, "y"), (second, "x"))
    ]
    far = [
        (shift(pair[0][0], axis, 1), shift(pair[1][1], axis, -1))
        for pair, axis in zip(near, ("y", "x"), strict=True)
    ]
    pieces = []
    for lines, pair, last in zip((first, second), near, far, strict=True):
        for level in range(2):
            pieces += [lines[level], pair[level][0], pair[level][1], last[level]]
    return pieces


PLACES = (0, 3, 1, 2)


def fetch(at, pieces, lane, target, sems):
    size = target.shape[-1]
    copies = []
    for index, piece in enumerate(pieces):
        level = at[1] if index % 8 < 4 else 1 - at[1]
        step = PLACES[index % 4]
        if index < 8:
            place = target.at[:, level, at[2], lax.rem(at[3] + step, 4)]
        else:
            place = target.at[lax.rem(at[0] + step, 4), level, 1 - at[2]]
        copies.append(pltpu.make_async_copy(piece.at[:, :, pl.ds(lane, size)], place, sems.at[index]))
    for copy in copies:
        copy.start()
    return copies


def line_kernel(index, at, *refs):
    for step in range(4):
        refs[4][lax.rem(at[index] + 4 - step, 4)] = refs[step][...]


def line_up(at, index, block, axis):
    blocks = [block] + [shift(block, axis, step) for step in (1, 2, 3)]
    return call(
        functools.partial(line_kernel, index), (4,) + block.shape, BF16, at, *blocks
    )


def add_low(*values):
    return sum(value.astype(F32) for value in values).astype(BF16)


def ring_kernel(index, at, own, plus, minus, low_in, high_in, o0, o1, o2, o3, low, high):
    low[...] = (own[0].astype(F32) + minus[1].astype(F32) + low_in[...].astype(F32)).astype(BF16)
    high[...] = (own[1].astype(F32) + plus[1].astype(F32) + high_in[...].astype(F32)).astype(BF16)
    for step, out in enumerate((o0, o1, o2, o3)):
        place = lax.rem(at[index] + step, 4)
        out[0] = low[place]
        out[1] = high[place]


def add_kernel(at, right, left, plus, minus, right_out, left_out):
    right_out[...] = (right[...].astype(F32) + plus[0].astype(F32)).astype(BF16)
    left_out[...] = (left[...].astype(F32) + minus[0].astype(F32)).astype(BF16)


def ring_sums(one, two, at):
    sides = ((one, "y", 0), (two, "x", 3))
    got = [(shift(side[1], axis, 1), shift(side[2], axis, -1)) for side, axis, _ in sides]
    got = lax.optimization_barrier(got)
    shape = one[3].shape
    last = []
    for (side, axis, _), (plus, minus) in zip(sides, got, strict=True):
        right, left = call(
            add_kernel, [shape] * 2, [BF16] * 2, at, side[3], side[4], plus, minus, many=True
        )
        last.append((shift(right, axis, 1), shift(left, axis, -1)))
    last = lax.optimization_barrier(last)
    return [
        call(
            functools.partial(ring_kernel, index),
            [(2,) + shape[1:]] * 4,
            [BF16] * 4,
            at,
            side[0],
            plus,
            minus,
            low,
            high,
            scratch=[pltpu.VMEM(shape, BF16)] * 2,
            many=True,
        )
        for (side, _, index), (plus, minus), (low, high) in zip(sides, got, last, strict=True)
    ]


def sum_kernel(at, p0, p1, p2, p3, low, high):
    for level, out in enumerate((low, high)):
        total = p0[level].astype(F32) + p1[level].astype(F32)
        out[...] = (total + p2[level].astype(F32) + p3[level].astype(F32)).astype(BF16)


def scatter_rows(one, two, at):
    one, two = ring_sums(one, two, at)
    got = [
        [side[0]] + [shift(side[step], axis, step) for step in (1, 2, 3)]
        for side, axis in ((one, "x"), (two, "y"))
    ]
    got = lax.optimization_barrier(got)
    shape = one[0].shape[1:]
    one, two = (call(sum_kernel, [shape] * 2, [BF16] * 2, at, *side, many=True) for side in got)
    return one[0], shift(one[1], "z", 1), shift(two[0], "c", 1), diagonal(two[1])


def to_ring(pieces):
    return [pieces[0]] + [shift(pieces[step], "y", step) for step in (1, 2, 3)]


def half_sum(partial):
    low = partial.astype(BF16)
    return low.astype(F32) + shift(low, "t", 1).astype(F32)


def core_sum(own, other):
    return own + shift(other, "c", 1).astype(F32)


def call(kernel, shapes, dtypes, at, *operands, scratch=(), flops=1_000_000, many=False, far=0, out_far=False):
    if not many:
        shapes, dtypes = [shapes], [dtypes]
    out_shape = [jax.ShapeDtypeStruct(s, d) for s, d in zip(shapes, dtypes, strict=True)]
    moved = sum(o.size * o.dtype.itemsize for o in operands)
    moved += sum(int(np.prod(s)) * jnp.dtype(d).itemsize for s, d in zip(shapes, dtypes, strict=True))
    outs = pl.pallas_call(
        kernel,
        out_shape=out_shape,
        in_specs=[pl.BlockSpec(memory_space=pltpu.SMEM)]
        + [pl.BlockSpec(memory_space=pl.ANY)] * far
        + [pl.BlockSpec(memory_space=pltpu.VMEM)] * (len(operands) - far),
        out_specs=[pl.BlockSpec(memory_space=pl.ANY if out_far else pltpu.VMEM)] * len(out_shape),
        scratch_shapes=scratch,
        compiler_params=pltpu.CompilerParams(vmem_limit_bytes=56 * 1024 * 1024),
        cost_estimate=pl.CostEstimate(flops=flops, bytes_accessed=moved, transcendentals=0),
    )(at, *operands)
    return outs if many else outs[0]


MSG = 1024
QR = 256
KV = 384
KR = 896


def rows_at(index):
    return pl.ds(pl.multiple_of(index * 128, 128), 128)


def lanes_at(index, size, base=0):
    return pl.ds(pl.multiple_of(base + index * size, 128), size)


def owner(at, place):
    return jnp.bitwise_xor(lax.shift_right_logical(place, 1), at[2]), jnp.bitwise_and(place, 1)


def ahead(at, step):
    return lax.rem(at[3] + step, 4)


def behind(at, step):
    return lax.rem(at[3] + 4 - step, 4)


def turn(values, cosine, sine):
    return values * cosine + pltpu.roll(values, 64, 1) * sine


def project_kernel(at, *refs):
    pieces = refs[:16]
    own, other, cosine, sine, m0, m1, m2, m3, normed, low, plain, inverse = refs[16:28]
    weights, out_weights, up, tail, query, keys, key, raw, sems = refs[28:]
    copies = fetch(at, pieces, 0, weights, sems.at[0])
    later = fetch(at, pieces, 1920, raw, sems.at[1])
    last = fetch(at, pieces, 1408, out_weights, sems.at[2])
    last += fetch(at, pieces, 2176, tail, sems.at[3])
    for index, block in enumerate((own, other)):
        values = block[...].astype(F32)
        scale = lax.rsqrt(jnp.mean(values * values, axis=1, keepdims=True) + EPS)
        normed[index * 128 : index * 128 + 128] = (values * scale).astype(BF16)
    for copy in copies:
        copy.wait()
    lin = dot(normed[...], weights[...].reshape(2048, 1408))
    cos, sin = cosine[...], sine[...]
    query[:, :512] = lin[:, :512].astype(BF16)
    for pair in range(2):
        span = slice(512 + pair * 128, 640 + pair * 128)
        query[:, span] = turn(lin[:, span], cos, sin).astype(BF16)
    key[...] = turn(lin[:, 1280:], cos, sin).astype(BF16)
    latent = lin[:, 768:1280]
    scale = lax.rsqrt(jnp.mean(latent * latent, axis=1, keepdims=True) + EPS)
    latent = latent * scale
    plain[...] = latent
    low[...] = latent.astype(BF16)
    inverse[...] = jnp.broadcast_to(scale, inverse.shape)
    for copy in later:
        copy.wait()
    ups = raw[...].astype(F32).reshape(64, 4, 8, 256)
    for head in range(4):
        span = slice(head * 256, head * 256 + 256)
        up[:, span] = ups[:, head].reshape(512, 256).astype(BF16)
    keys[...] = dot(low[...], up[...]).astype(BF16)
    for step, out in enumerate((m0, m1, m2, m3)):
        block, pair = owner(at, ahead(at, step))
        rows = rows_at(block)
        out[:, :QR] = query[rows, lanes_at(pair, 256)]
        out[:, QR:KV] = query[rows, lanes_at(pair, 128, 512)]
        out[:, KV:KR] = keys[rows, lanes_at(pair, 512)]
        out[:, KR:] = key[rows, :]
    for copy in last:
        copy.wait()


def head_lanes(rows, head):
    lane = lax.broadcasted_iota(jnp.int32, (rows, 128), 1)
    return jnp.where(((lane >> 5) & 1) == head, 1.0, 0.0).astype(F32)


def head_keys(msg_ref, head):
    rotated = msg_ref[:, :, KR:].reshape(512, 128).astype(F32) * head_lanes(512, head)
    plain = msg_ref[:, :, KV + head * 256 : KV + head * 256 + 128].reshape(512, 128)
    return jnp.concatenate([plain, rotated.astype(BF16)], axis=1)


def head_values(msg_ref, head):
    return msg_ref[:, :, KV + head * 256 + 128 : KV + head * 256 + 256].reshape(512, 128)


def block_probs(query, keys, row_ref, col_ref, block):
    count = (block + 1) * 128
    scores = dot(query, keys[:count], 1, 1) * SCALE
    rows = lax.broadcasted_iota(jnp.int32, (128, count), 0) + block * 128
    cols = lax.broadcasted_iota(jnp.int32, (128, count), 1)
    same = col_ref[block * 128 : count, :] == row_ref[:, :count]
    scores = jnp.where(same & (cols <= rows), scores, -1e30)
    powers = jnp.exp(scores - jnp.max(scores, axis=1, keepdims=True))
    return powers / jnp.sum(powers, axis=1, keepdims=True)


def block_query(msg_ref, head, block):
    return jnp.concatenate(
        [msg_ref[block, :, head * 128 : head * 128 + 128], msg_ref[block, :, QR:KV]], axis=1
    )


def forward_kernel(at, m0, m1, m2, m3, row_ref, col_ref, msg_ref, o0, o1, o2, o3, mixed):
    for step, piece in enumerate((m0, m1, m2, m3)):
        msg_ref[behind(at, step)] = piece[...]
    for head in range(2):
        keys = head_keys(msg_ref, head)
        values = head_values(msg_ref, head)
        for block in range(4):
            query = block_query(msg_ref, head, block)
            probs = block_probs(query, keys, row_ref, col_ref, block)
            part = dot(probs.astype(BF16), values[: (block + 1) * 128])
            mixed[block, :, head * 128 : head * 128 + 128] = part.astype(BF16)
    for step, out in enumerate((o0, o1, o2, o3)):
        out[...] = mixed[ahead(at, step)]


def output_kernel(at, p0, p1, p2, p3, weights, attended, own, other):
    for step, piece in enumerate((p0, p1, p2, p3)):
        block, pair = owner(at, behind(at, step))
        attended[rows_at(block), lanes_at(pair, 256)] = piece[...]
    own[...] = dot(attended[:128], weights[...], 1, 1)
    other[...] = dot(attended[128:], weights[...], 1, 1).astype(BF16)


def heads_kernel(at, own, other, weights, h0, h1, h2, h3, grad):
    grad[:128] = dot(own[...], weights[...]).astype(BF16)
    grad[128:] = dot(other[...], weights[...]).astype(BF16)
    for step, out in enumerate((h0, h1, h2, h3)):
        block, pair = owner(at, ahead(at, step))
        out[...] = grad[rows_at(block), lanes_at(pair, 256)]


def backward_kernel(
    at, msg_ref, g0, g1, g2, g3, row_ref, col_ref, o0, o1, o2, o3, grad_ref, out_ref, key_acc, value_acc
):
    for step, piece in enumerate((g0, g1, g2, g3)):
        grad_ref[behind(at, step)] = piece[...]
    for head in range(2):
        keys = head_keys(msg_ref, head)
        values = head_values(msg_ref, head)
        key_acc[...] = jnp.zeros_like(key_acc)
        value_acc[...] = jnp.zeros_like(value_acc)
        lanes = head_lanes(128, head)
        for block in range(4):
            count = (block + 1) * 128
            query = block_query(msg_ref, head, block)
            probs = block_probs(query, keys, row_ref, col_ref, block)
            grad = grad_ref[block, :, head * 128 : head * 128 + 128]
            probs_grad = dot(grad, values[:count], 1, 1)
            inner = jnp.sum(probs * probs_grad, axis=1, keepdims=True)
            score_grad = (probs * (probs_grad - inner) * SCALE).astype(BF16)
            query_grad = dot(score_grad, keys[:count])
            out_ref[block, :, head * 128 : head * 128 + 128] = query_grad[:, :128].astype(BF16)
            turned = query_grad[:, 128:]
            if head == 1:
                turned = turned + out_ref[block, :, QR:KV].astype(F32)
            out_ref[block, :, QR:KV] = turned.astype(BF16)
            key_acc[:count] += dot(score_grad, query, 0, 0)
            value_acc[:count] += dot(probs.astype(BF16), grad, 0, 0)
        base = KV + head * 256
        for block in range(4):
            span = slice(block * 128, block * 128 + 128)
            out_ref[block, :, base : base + 128] = key_acc[span, :128].astype(BF16)
            out_ref[block, :, base + 128 : base + 256] = value_acc[span, :].astype(BF16)
            turned = key_acc[span, 128:] * lanes
            if head == 1:
                turned = turned + out_ref[block, :, KR:].astype(F32)
            out_ref[block, :, KR:] = turned.astype(BF16)
    for step, out in enumerate((o0, o1, o2, o3)):
        out[...] = out_ref[ahead(at, step)]


def return_kernel(
    at, b0, b1, b2, b3, weights, up, cosine, sine, plain, inverse, lin_grad, kv_grad, own, other, key
):
    for step, piece in enumerate((b0, b1, b2, b3)):
        block, pair = owner(at, behind(at, step))
        rows = rows_at(block)
        lin_grad[rows, lanes_at(pair, 256)] = piece[:, :QR]
        turned = turn(piece[:, QR:KV].astype(F32), cosine[rows, :], -sine[rows, :])
        lin_grad[rows, lanes_at(pair, 128, 512)] = turned.astype(BF16)
        kv_grad[rows, lanes_at(pair, 512)] = piece[:, KV:KR]
        key[rows_at(block + 2 * pair), :] = piece[:, KR:].astype(F32)
    turned = turn(key[:256] + key[256:], cosine[...], -sine[...])
    lin_grad[:, 1280:] = turned.astype(BF16)
    grad = dot(kv_grad[...], up[...], 1, 1)
    latent = plain[...]
    grad = inverse[:, :1] * (grad - latent * jnp.mean(grad * latent, axis=1, keepdims=True))
    lin_grad[:, 768:1280] = grad.astype(BF16)
    own[...] = dot(lin_grad[:128], weights[...], 1, 1)
    other[...] = dot(lin_grad[128:], weights[...], 1, 1).astype(BF16)


def grads_kernel(at, normed, lin_grad, own, other, attended, low, kv_grad, tail, *refs):
    own_one, plus_one, minus_one, right_one, left_one = refs[:5]
    own_two, plus_two, minus_two, right_two, left_two = refs[5:10]
    rows, ups = refs[10:]

    def store_one(place, side, column, value):
        if place == 0:
            own_one[side, column] = value
        elif place == 2:
            (plus_one, minus_one)[side][0, column] = value
        elif place == 1:
            (right_one.at[column] if side == 0 else plus_one.at[1, column])[...] = value
        else:
            (left_one.at[column] if side == 1 else minus_one.at[1, column])[...] = value

    def store_two(place, side, value):
        if place == 0:
            own_two[side] = value
        elif place == 2:
            (plus_two, minus_two)[side][0] = value
        elif place == 1:
            (right_two if side == 0 else plus_two.at[1])[...] = value
        else:
            (left_two if side == 1 else minus_two.at[1])[...] = value

    for head in range(4):
        span = slice(head * 256, head * 256 + 256)
        ups[:, head] = dot(low[...], kv_grad[:, span], 0, 0).reshape(64, 8, 256)
    for step in range(4):
        column = lax.rem(at[0] + step, 4)
        for side in range(2):
            level = at[1] if side == 0 else 1 - at[1]
            chunk = column * 2 + level
            span = pl.ds(pl.multiple_of(chunk * 256, 256), 256)
            part = dot(normed[:, span], lin_grad[...], 0, 0).astype(BF16)
            rows[:, :, :1408] = part.reshape(8, 32, 1408)
            part = dot(own[:, span], attended[:128], 0, 0) + dot(other[:, span], attended[128:], 0, 0)
            rows[:, :, 1408:1920] = part.astype(BF16).reshape(8, 32, 512)
            rows[:, :, 1920:2176] = ups[pl.ds(chunk * 8, 8)].reshape(8, 32, 256).astype(BF16)
            rows[:, :, 2176:] = tail[span, :].reshape(8, 32, 128)
            for place in range(4):
                store_one(place, side, column, rows[at[2] * 4 + ahead(at, place)])
            store_two(step, side, rows[pl.ds((1 - at[2]) * 4, 4)])


def shared_kernel(at, gathered, *refs):
    ffn_blocks, cot_blocks, kept, sent, grads = refs[:4], refs[4:8], refs[8], refs[9], refs[10]
    weights, ffn, cot, lin_grad, act, sems = refs[11:]
    copies = []
    for z in range(2):
        for core in range(2):
            copies.append(
                pltpu.make_async_copy(
                    gathered.at[:, :, z, core], weights.at[:, z, core], sems.at[2 * z + core]
                )
            )
    for copy in copies:
        copy.start()
    for i in range(4):
        ffn[i * 128 : i * 128 + 128] = ffn_blocks[i][...]
        cot[i * 128 : i * 128 + 128] = cot_blocks[i][...]
    for copy in copies:
        copy.wait()
    gate_up = weights[:, :, :, :, :, :704].reshape(2048, 704)
    down = weights[:, :, :, :, :, DOWN : DOWN + 352].reshape(2048, 352)
    lin = dot(ffn[...], gate_up)
    act_grad = dot(cot[...], down)
    up_lin = lin[:, 352:]
    silu, slope = silu_parts(lin[:, :352])
    act[...] = (silu * up_lin).astype(BF16)
    both = jnp.concatenate([act_grad * up_lin * slope, act_grad * silu], axis=1)
    lin_grad[...] = both.astype(BF16)
    back = dot(lin_grad[...], gate_up, 1, 1)
    out = dot(act[...], down, 1, 1)
    for side in range(2):
        first = side * 256
        for row, values in enumerate((back, out)):
            kept[2 * side + row] = values[first : first + 128]
            sent[2 * side + row] = values[first + 128 : first + 256].astype(BF16)
    for block in range(8):
        span = slice(block * 256, block * 256 + 256)
        part = dot(ffn[:, span], lin_grad[...], 0, 0).astype(BF16).reshape(2, 4, 32, 704)
        low = dot(cot[:, span], act[...], 0, 0).astype(BF16).reshape(2, 4, 32, 352)
        for core in range(2):
            grads[block // 2, :, block % 2, core, :, :704] = part[core]
            grads[block // 2, :, block % 2, core, :, DOWN : DOWN + 352] = low[core]
            grads[block // 2, :, block % 2, core, :, 704:DOWN] = jnp.zeros((4, 32, 64), BF16)
            grads[block // 2, :, block % 2, core, :, DOWN + 352 :] = jnp.zeros((4, 32, 32), BF16)


def finish_kernel(at, p0, p1, p2, p3, query, down, up, attn_gain, latent_gain, *outs):
    query_out, up_out, out_out, small, ffn_gain_out = outs
    own = p0[...].astype(F32) + p1[...].astype(F32)
    other = p2[...].astype(F32) + p3[...].astype(F32)
    first = at[2] == 0
    halves = [jnp.where(first, own, other), jnp.where(first, other, own)]
    heads, lifts = [], []
    for half in halves:
        for head in range(4):
            pair, place = head // 2, head % 2
            heads.append(half[:, head * 128 : head * 128 + 128])
            for side in range(2):
                start = 512 + pair * 128 + side * 64 + place * 32
                heads.append(half[:, start : start + 32])
        lifts += [half[8 * j : 8 * j + 8, 1920:2176] for j in range(4)]
    grads = jnp.concatenate(heads, axis=1)
    query_out[...] = grads * attn_gain[...].astype(F32)
    part = jnp.sum(grads * query[...].astype(F32), axis=1, keepdims=True)
    lift = jnp.concatenate(lifts, axis=1)
    up_out[...] = lift * latent_gain[...].astype(F32)
    lift_part = jnp.sum(lift * up[...].astype(F32), axis=1, keepdims=True)
    out_out[:, :512] = halves[0][:, 1408:1920]
    out_out[:, 512:] = halves[1][:, 1408:1920]
    both = own + other
    small[:, :512] = both[:, 768:1280]
    turned = jnp.concatenate(
        [
            both[:, 1280:1312] + both[:, 1312:1344],
            both[:, 1344:1376] + both[:, 1376:1408],
            both[:, 2176:2240],
        ],
        axis=1,
    )
    small[:, 512:640] = turned
    part += jnp.sum(down[:, :512].astype(F32) * both[:, 768:1280], axis=1, keepdims=True)
    part += jnp.sum(down[:, 512:].astype(F32) * turned[:, :64], axis=1, keepdims=True)
    small[:, 640:768] = jnp.broadcast_to(part, (32, 128))
    small[:, 768:] = jnp.zeros((32, 128), F32)
    small[:8, 768:] = jnp.broadcast_to(lift_part, (8, 128))
    ffn_gain_out[...] = both[:, 2240:2241]


def shared_finish_kernel(at, stay, across, beside, corner, gate, up, down):
    core, side = at[2] == 0, at[1] == 0
    own = [ref[...].astype(F32) for ref in (stay, beside)]
    other = [ref[...].astype(F32) for ref in (across, corner)]
    own = [jnp.where(side, own[0], own[1]), jnp.where(side, own[1], own[0])]
    other = [jnp.where(side, other[0], other[1]), jnp.where(side, other[1], other[0])]
    parts = [jnp.where(core, a, b) for a, b in zip(own, other, strict=True)]
    parts += [jnp.where(core, b, a) for a, b in zip(own, other, strict=True)]
    gate[...] = jnp.concatenate([part[:, :352] for part in parts], axis=1)
    up[...] = jnp.concatenate([part[:, 352:704] for part in parts], axis=1)
    down[...] = jnp.concatenate([part[:, DOWN : DOWN + 352] for part in parts], axis=1)


def doc_positions(doc_row):
    places = jnp.arange(doc_row.shape[0], dtype=jnp.int32)
    starts = jnp.concatenate([jnp.ones((1,), bool), doc_row[1:] != doc_row[:-1]])
    begins = lax.cummax(jnp.where(starts, places, 0), axis=0)
    return places - begins


def norm_back(scaled, normed, inverse):
    return inverse * (scaled - normed * jnp.mean(scaled * normed, axis=1, keepdims=True))


def silu_parts(lin):
    sig = jax.nn.sigmoid(lin)
    return lin * sig, sig * (1.0 + lin * (1.0 - sig))


def rms(values):
    return lax.rsqrt(jnp.mean(values * values, axis=1, keepdims=True) + EPS)


def shards(
    tokens_in,
    documents,
    routes,
    attn_gain,
    query_weight,
    latent_down,
    latent_gain,
    latent_up,
    output_weight,
    ffn_gain,
    router,
    shared_gate,
    shared_up,
    shared_down,
    expert_gate,
    expert_up,
    expert_down,
    cotangent,
):
    core = lax.axis_index("c")
    spot = lax.axis_index("y")
    at = jnp.stack([lax.axis_index("x"), lax.axis_index("z"), core, spot]).astype(jnp.int32)
    expert = (lax.axis_index("x") * 4 + lax.axis_index("z") * 2 + core) * 4 + spot
    rows = tokens_in.shape[0]
    width = tokens_in.shape[1]
    experts_count = router.shape[1]
    capacity = 16
    every = ("x", "z", "c", "y")

    keep, send, *quarters = call(
        pack_kernel,
        [(32, LANES)] * 2 + [(32, QUARTER)] * 4,
        [BF16] * 6,
        at,
        query_weight,
        latent_down,
        latent_up,
        output_weight.T,
        shared_gate,
        shared_up,
        shared_down.T,
        router,
        attn_gain[:, None],
        latent_gain[:, None],
        ffn_gain[:, None],
        scratch=[pltpu.VMEM((2, 32, LANES), BF16), pltpu.VMEM((4, 32, QUARTER), BF16)],
        many=True,
    )
    pieces = gather_rows(keep, send, at)
    shared_rows = quad_exchange(quarters).reshape(128, QUARTER)
    cot_four = quad_blocks(cotangent)

    named = jnp.any(
        routes.T[None, :, :] == jnp.arange(experts_count, dtype=jnp.int32)[:, None, None], axis=1
    )
    before = jnp.arange(rows)[:, None] < jnp.arange(rows)[None, :]
    place = dot(named.astype(BF16), before.astype(BF16))
    slots = (
        named[:, None, :] & (place[:, None, :] == jnp.arange(capacity, dtype=F32)[None, :, None])
    ).astype(BF16)
    slots = slots.reshape(experts_count * capacity, rows)

    def exchange_rows(values):
        sent = values.reshape(experts_count, capacity, -1)
        got = lax.all_to_all(sent, every, split_axis=0, concat_axis=0, tiled=True)
        return got.reshape(experts_count * capacity, -1)

    docs = jnp.concatenate([documents, shift(documents, "c", 1)])
    positions = jax.vmap(doc_positions)(docs)
    local_pos = lax.dynamic_slice_in_dim(positions, spot * rows, rows, axis=1).reshape(-1)
    steps = jnp.arange(ROPE // 2, dtype=F32)
    angles = local_pos.astype(F32)[:, None] * (10000.0 ** (-steps / (ROPE // 2)))[None, :]
    cosine = jnp.tile(jnp.cos(angles), (1, 4))
    sine = jnp.sin(angles)
    sine = jnp.concatenate([-sine, -sine, sine, sine], axis=1)
    doc = jnp.where(spot // 2 == core, docs[0], docs[1])
    doc_row, doc_col = doc[None, :], doc[:, None]

    tokens_other = shift(tokens_in, "c", 1)
    half = lax.axis_index("t")
    cot_sent = lax.dynamic_slice_in_dim(cotangent, half * 1024, 1024, axis=1)
    cot_sent = dot(slots, cot_sent).astype(BF16)
    cot_sent, pieces, shared_rows, cot_four, cosine, sine, doc_row, doc_col, tokens_other = (
        lax.optimization_barrier(
            (cot_sent, pieces, shared_rows, cot_four, cosine, sine, doc_row, doc_col, tokens_other)
        )
    )
    own_cot = exchange_rows(cot_sent)
    shared_all = lax.all_gather(shared_rows, ("x", "y"), axis=0, tiled=True)
    shared_all = shared_all.reshape(4, 4, 2, 2, 32, QUARTER)
    sent = [(rows, MSG)] * 4
    two = 2 * rows
    six = (4, 2, 2, 4, 32)
    outs = call(
        project_kernel,
        sent
        + [(two, width), (two, LATENT), (two, LATENT), (two, 128)]
        + [six + (1408,), six + (512,), (LATENT, 1024), six + (128,)],
        [BF16] * 6 + [F32, F32] + [BF16] * 4,
        at,
        *pieces,
        tokens_in,
        tokens_other,
        cosine,
        sine,
        scratch=[
            pltpu.VMEM((two, 768), BF16),
            pltpu.VMEM((two, 1024), BF16),
            pltpu.VMEM((two, 128), BF16),
            pltpu.VMEM(six + (256,), BF16),
            pltpu.SemaphoreType.DMA((4, 16)),
        ],
        flops=1_800_000_000,
        many=True,
        far=16,
    )
    sent, normed_low, latent_low, latent_normed, latent_inverse = outs[:4], *outs[4:8]
    in_all, out_all = outs[8].reshape(width, 1408), outs[9].reshape(width, 512)
    up_all, tail_all = outs[10], outs[11].reshape(width, 128)
    sent, own_cot = lax.optimization_barrier((sent, own_cot))
    other_cot = shift(own_cot, "t", 1)
    received = to_ring(sent)
    msg, *mixed = call(
        forward_kernel,
        [(4, rows, MSG)] + [(rows, 256)] * 4,
        [BF16] * 5,
        at,
        *received,
        doc_row,
        doc_col,
        scratch=[pltpu.VMEM((4, rows, 256), BF16)],
        flops=500_000_000,
        many=True,
    )
    mixed, other_cot = lax.optimization_barrier((to_ring(mixed), other_cot))
    attended, out_own, out_other = call(
        output_kernel,
        [(two, 512), (rows, width), (rows, width)],
        [BF16, F32, BF16],
        at,
        *mixed,
        out_all,
        flops=600_000_000,
        many=True,
    )
    tokens_f = tokens_in.astype(F32)
    resid = tokens_f + half_sum(core_sum(out_own, out_other))

    pointer = jnp.broadcast_to(jnp.arange(128)[None, :] == 64, (8, 128)).astype(BF16)
    gain_two = dot(pointer, tail_all, 1, 1)[:1]
    router_all = tail_all[:, :64]
    inverse_two = rms(resid)
    normed_two = resid * inverse_two
    ffn_in = (normed_two * gain_two).astype(BF16)
    ffn_sent = dot(slots, ffn_in).astype(BF16)
    ffn_four, ffn_sent = lax.optimization_barrier((quad_blocks(ffn_in), ffn_sent))
    expert_rows = exchange_rows(ffn_sent)

    kept, sent, shared_grads = call(
        shared_kernel,
        [(4, rows, width)] * 2 + [(4, 4, 2, 2, 32, QUARTER)],
        [F32, BF16, BF16],
        at,
        shared_all,
        *ffn_four,
        *cot_four,
        scratch=[
            pltpu.VMEM((4, 2, 2, 4, 32, QUARTER), BF16),
            pltpu.VMEM((4 * rows, width), BF16),
            pltpu.VMEM((4 * rows, width), BF16),
            pltpu.VMEM((4 * rows, 704), BF16),
            pltpu.VMEM((4 * rows, 352), BF16),
            pltpu.SemaphoreType.DMA((4,)),
        ],
        flops=7_000_000_000,
        many=True,
        far=1,
    )
    kept = kept + shift(sent, "c", 1).astype(F32)
    shared_sum = lax.psum_scatter(
        shared_grads.reshape(width, QUARTER), ("x", "y"), scatter_dimension=0, tiled=True
    ).reshape(2, 2, 32, QUARTER)
    gate_w, up_w, down_w = expert_gate[0], expert_up[0], expert_down[0]
    first_cot = jnp.where(half == 0, own_cot, other_cot)
    last_cot = jnp.where(half == 0, other_cot, own_cot)
    plain_grad = dot(first_cot, down_w[:, :1024], 1, 1) + dot(last_cot, down_w[:, 1024:], 1, 1)
    shared_back = kept[0] + shift(kept[2].astype(BF16), "z", 1).astype(F32)
    expert_rows, plain_grad, kept, shared_grads = lax.optimization_barrier(
        (expert_rows, plain_grad, kept, shared_grads)
    )
    probs = jax.nn.softmax(dot(expert_rows, router_all), axis=1)
    mine = (jnp.arange(experts_count, dtype=jnp.int32) == expert)[None, :].astype(F32)
    gate = jnp.sum(probs * mine, axis=1, keepdims=True)
    gate_lin = dot(expert_rows, gate_w)
    up_lin = dot(expert_rows, up_w)
    silu, slope = silu_parts(gate_lin)
    act = silu * up_lin
    act_low = (gate * act).astype(BF16)
    inner = jnp.sum(act * plain_grad, axis=1, keepdims=True)
    act_grad = gate * plain_grad
    gate_grad = (act_grad * up_lin * slope).astype(BF16)
    up_grad = (act_grad * silu).astype(BF16)
    logit_grad = (inner * gate * (mine - probs)).astype(BF16)
    row_grad = (
        dot(gate_grad, gate_w, 1, 1) + dot(up_grad, up_w, 1, 1) + dot(logit_grad, router_all, 1, 1)
    ).astype(BF16)
    back_rows = exchange_rows(row_grad)
    piece = dot(act_low, down_w).astype(BF16)
    expert_down_grad = jnp.concatenate(
        [dot(act_low, first_cot, 0, 0), dot(act_low, last_cot, 0, 0)], axis=1
    )[None]
    expert_gate_grad = dot(expert_rows, gate_grad, 0, 0)[None]
    expert_up_grad = dot(expert_rows, up_grad, 0, 0)[None]
    router_grad = dot(expert_rows, logit_grad, 0, 0)
    piece_own = lax.dynamic_slice_in_dim(piece, half * 1024, 1024, axis=1)
    piece_sent = lax.dynamic_slice_in_dim(piece, 1024 - half * 1024, 1024, axis=1)
    done = (back_rows, piece_own, piece_sent, expert_down_grad, expert_gate_grad, expert_up_grad, router_grad)
    done, shared_back = lax.optimization_barrier((done, shared_back))
    back_rows, piece_own, piece_sent, expert_down_grad, expert_gate_grad, expert_up_grad, router_grad = done
    routed_back = dot(slots, back_rows, 0, 0)
    cot_f = cotangent.astype(F32)
    ffn_grad = half_sum(shared_back + routed_back)
    ffn_grad, piece_sent = lax.optimization_barrier((ffn_grad, piece_sent))
    piece = add_low(piece_own, shift(piece_sent, "t", 1))
    resid_grad = cot_f + norm_back(ffn_grad * gain_two, normed_two, inverse_two)
    first_lane = jnp.broadcast_to(jnp.arange(64)[None, :] == 0, (rows, 64)).astype(BF16)
    ffn_gain_part = dot((ffn_grad * normed_two).astype(BF16), first_lane, 0, 0)

    resid_low = resid_grad.astype(BF16)
    resid_other = shift(resid_low, "c", 1)
    heads_grad = call(
        heads_kernel,
        [(rows, 256)] * 4,
        [BF16] * 4,
        at,
        resid_low,
        resid_other,
        out_all,
        scratch=[pltpu.VMEM((two, 512), BF16)],
        flops=600_000_000,
        many=True,
    )
    heads_got, shared_sum = lax.optimization_barrier((to_ring(heads_grad), shared_sum))
    own_rows, far_rows = pick(shared_sum, at[1]), pick(shared_sum, 1 - at[1])
    stay, beside = pick(own_rows, core), shift(pick(far_rows, core), "z", 1)
    across, corner = shift(pick(own_rows, 1 - core), "c", 1), diagonal(pick(far_rows, 1 - core))
    shared_gate_grad, shared_up_grad, shared_down_grad = call(
        shared_finish_kernel,
        [(32, 1408)] * 3,
        [F32] * 3,
        at,
        stay,
        across,
        beside,
        corner,
        many=True,
    )
    back = call(
        backward_kernel,
        [(rows, MSG)] * 4,
        [BF16] * 4,
        at,
        msg,
        *heads_got,
        doc_row,
        doc_col,
        scratch=[
            pltpu.VMEM((4, rows, 256), BF16),
            pltpu.VMEM((4, rows, MSG), BF16),
            pltpu.VMEM((512, 256), F32),
            pltpu.VMEM((512, 128), F32),
        ],
        flops=1_500_000_000,
        many=True,
    )
    returned, piece = lax.optimization_barrier((to_ring(back), piece))
    piece_rows = exchange_rows(piece)
    lin_grad, kv_grad, in_own, in_other = call(
        return_kernel,
        [(two, 1408), (two, 1024), (rows, width), (rows, width)],
        [BF16, BF16, F32, BF16],
        at,
        *returned,
        in_all,
        up_all,
        cosine,
        sine,
        latent_normed,
        latent_inverse,
        scratch=[pltpu.VMEM((512, 128), F32)],
        flops=1_800_000_000,
        many=True,
    )
    tail = jnp.concatenate([router_grad, ffn_gain_part], axis=1).astype(BF16)
    blocks = call(
        grads_kernel,
        ([(2, 4, 32, LANES)] * 3 + [(4, 32, LANES)] * 2) * 2,
        [BF16] * 10,
        at,
        normed_low,
        lin_grad,
        resid_low,
        resid_other,
        attended,
        latent_low,
        kv_grad,
        tail,
        scratch=[pltpu.VMEM((8, 32, 2304), BF16), pltpu.VMEM((64, 4, 8, 256), F32)],
        flops=2_200_000_000,
        many=True,
    )
    blocks, piece_rows, kept = lax.optimization_barrier((blocks, piece_rows, kept))
    attn_sum = scatter_rows(blocks[:5], blocks[5:], at)

    attn_in_grad = half_sum(core_sum(in_own, in_other))
    inverse_one = rms(tokens_f)
    input_grad = resid_grad + norm_back(attn_in_grad, tokens_f * inverse_one, inverse_one)
    routed_out = dot(slots, piece_rows, 0, 0)
    shared_out = half_sum(kept[1] + shift(kept[3].astype(BF16), "z", 1).astype(F32))
    routed_out = routed_out.astype(BF16)
    routed_other = shift(routed_out, "t", 1)
    routed_out = jnp.concatenate(
        [jnp.where(half == 0, routed_out, routed_other), jnp.where(half == 0, routed_other, routed_out)],
        axis=1,
    )
    layer_out = (resid + (shared_out + routed_out.astype(F32))).astype(BF16)

    query_out, up_out, out_out, small, ffn_gain_grad = call(
        finish_kernel,
        [(32, 1536), (8, 2048), (32, 1024), (32, 896), (32, 1)],
        [F32] * 5,
        at,
        *attn_sum,
        query_weight,
        latent_down,
        latent_up,
        attn_gain[:, None],
        latent_gain[:, None],
        many=True,
    )
    small = small + shift(small, "t", 1)
    return (
        layer_out,
        input_grad,
        small[:, 640],
        query_out,
        attn_gain.astype(F32)[:, None] * small[:, :576],
        small[:8, 768],
        up_out,
        out_out.T,
        ffn_gain_grad[:, 0],
        small[:, 576:640],
        shared_gate_grad,
        shared_up_grad,
        shared_down_grad.T,
        expert_gate_grad,
        expert_up_grad,
        expert_down_grad,
    )


def solution(mesh):
    fine = Mesh(mesh.devices.reshape(4, 2, 2, 4, 2), ("x", "z", "c", "y", "t"))
    fsdp = ("x", "z", "c")
    every = ("x", "z", "c", "y")
    in_specs = (
        P(every, None),
        P(fsdp, None),
        P(every, None),
        P(every),
        P(every, "t"),
        P(every, None),
        P(every),
        P(every, "t"),
        P("t", every),
        P(every),
        P(every, None),
        P(every, "t"),
        P(every, "t"),
        P("t", every),
        P(every, None, "t"),
        P(every, None, "t"),
        P(every, "t", None),
        P(every, None),
    )
    out_specs = (
        P(every, None),
        P(every, None),
        P(every),
        P(every, "t"),
        P(every, None),
        P(every),
        P(every, "t"),
        P("t", every),
        P(every),
        P(every, None),
        P(every, "t"),
        P(every, "t"),
        P("t", every),
        P(every, None, "t"),
        P(every, None, "t"),
        P(every, "t", None),
    )
    return jax.shard_map(shards, mesh=fine, in_specs=in_specs, out_specs=out_specs, check_vma=False)
```

```python
import functools

import jax
import jax.numpy as jnp
import numpy as np
from jax import lax
from jax.experimental import pallas as pl
from jax.experimental.pallas import tpu as pltpu
from jax.sharding import Mesh
from jax.sharding import PartitionSpec as P

NOPE = 128
ROPE = 64
VDIM = 128
LATENT = 512
HEAD = NOPE + ROPE
EPS = 1e-06
SCALE = HEAD ** (-0.5)
F32 = jnp.float32
BF16 = jnp.bfloat16


def dot(left, right, left_dim=1, right_dim=0):
    return lax.dot_general(
        left, right, (((left_dim,), (right_dim,)), ((), ())), preferred_element_type=F32
    )


def shift(values, axis, step):
    size = lax.axis_size(axis)
    return lax.ppermute(values, axis, [(j, (j + step) % size) for j in range(size)])


def diagonal(values):
    return lax.ppermute(values, ("z", "c"), [(0, 3), (1, 2), (2, 1), (3, 0)])


def pick(buffer, index):
    return lax.dynamic_index_in_dim(buffer, index, 0, keepdims=False)


def in_order(own, other, index):
    return jnp.stack([jnp.where(index == 0, own, other), jnp.where(index == 0, other, own)])


def pack_kernel(
    at, query, down, up, out, gate, upper, lower, router, attn_gain, latent_gain, ffn_gain, *refs
):
    *targets, packs, shared_packs = refs
    scale = attn_gain[...].astype(F32)
    lat_scale = latent_gain[...].astype(F32)
    heads = query[...].astype(F32) * scale
    lows = down[...].astype(F32) * scale
    rotated = lows[:, 512:]
    ups = up[...].astype(F32) * lat_scale
    outs, gates, uppers, lowers = (ref[...].astype(F32) for ref in (out, gate, upper, lower))
    for half in range(2):
        first = half * 4 * HEAD
        plain = [heads[:, first + i * HEAD : first + i * HEAD + NOPE] for i in range(4)]
        turned = []
        for pair in range(2):
            for side in range(2):
                for i in (2 * pair, 2 * pair + 1):
                    start = first + i * HEAD + NOPE + 32 * side
                    turned.append(heads[:, start : start + 32])
        blocks = plain + [jnp.concatenate(turned, axis=1), lows[:, :512]]
        blocks.append(
            jnp.concatenate([rotated[:, :32], rotated[:, :32], rotated[:, 32:], rotated[:, 32:]], axis=1)
        )
        blocks.append(outs[:, half * 512 : half * 512 + 512])
        start = half * 1024
        blocks.append(
            jnp.concatenate([ups[:, start + j * 256 : start + j * 256 + 256] for j in range(4)], axis=0)
        )
        gain = jnp.broadcast_to(ffn_gain[...].astype(F32), (32, 64))
        blocks.append(jnp.concatenate([router[...].astype(F32), gain], axis=1))
        for side in range(2):
            index = half * 2 + side
            span = slice(index * 352, index * 352 + 352)
            parts = [gates[:, span], uppers[:, span], jnp.zeros((32, 64), F32)]
            parts += [lowers[:, span], jnp.zeros((32, 32), F32)]
            shared_packs[index] = jnp.concatenate(parts, axis=1).astype(BF16)
        at_lane = 0
        for block in blocks:
            size = block.shape[1]
            packs[half, :, at_lane : at_lane + size] = block.astype(BF16)
            at_lane += size
    core, side = at[2], at[1]
    places = (core * 2 + side, (1 - core) * 2 + side, core * 2 + 1 - side, (1 - core) * 2 + 1 - side)
    for index, (ref, place) in enumerate(zip(targets, places, strict=True)):
        ref[:, :LANES] = packs[core if index % 2 == 0 else 1 - core]
        ref[:, LANES:] = shared_packs[place]


LANES = 2304
QUARTER = 1152
DOWN = 768


def quad_order(parts):
    z, core = lax.axis_index("z"), lax.axis_index("c")
    stay, across, beside, corner = parts
    return in_order(in_order(stay, across, core), in_order(beside, corner, core), z)


def quad_blocks(own):
    beside = shift(own, "z", 1)
    return [own, shift(own, "c", 1), beside, shift(beside, "c", 1)]


def gather_lines(packs, at):
    stay, across, beside, corner = packs
    got = [stay, shift(across, "c", 1), shift(beside, "z", 1), diagonal(corner)]
    stay, across, beside, corner = (block[:, :LANES] for block in got)
    lines = [
        line_up(at, 0, jnp.stack([stay, beside]), "x"),
        line_up(at, 3, jnp.stack([across, corner]), "y"),
    ]
    return lines, [block[:, LANES:] for block in got]


PLACES = ((0, 0, 0), (0, 1, 0), (1, 0, 3), (1, 1, 3), (2, 0, 1), (2, 1, 1), (3, 0, 2), (4, 1, 2))


def fetch(at, pieces, lane, target, sems):
    span = pl.ds(lane, target.shape[-1])
    copies = []
    for side in range(2):
        for index, side_level, step in PLACES:
            piece = pieces[side * 5 + index]
            level = at[1] if side_level == 0 else 1 - at[1]
            if side == 0:
                place = target.at[:, level, at[2], lax.rem(at[3] + step, 4)]
            else:
                place = target.at[lax.rem(at[0] + step, 4), level, 1 - at[2]]
            source = piece.at[side_level, :, :, span] if index < 3 else piece.at[:, :, span]
            copies.append(pltpu.make_async_copy(source, place, sems.at[len(copies)]))
    for copy in copies:
        copy.start()
    return copies


def line_kernel(index, at, *refs):
    for step in range(4):
        place = lax.rem(at[index] + 4 - step, 4)
        refs[4][0, place] = refs[step][0]
        refs[4][1, place] = refs[step][1]


def line_up(at, index, block, axis):
    blocks = [block] + [shift(block, axis, step) for step in (1, 2, 3)]
    shape = (2, 4) + block.shape[1:]
    return call(functools.partial(line_kernel, index), shape, BF16, at, *blocks)


def add_low(*values):
    return sum(value.astype(F32) for value in values).astype(BF16)


def ring_kernel(index, at, own, plus, minus, low_in, high_in, o0, o1, o2, o3, low, high):
    low[...] = (own[0].astype(F32) + minus[1].astype(F32) + low_in[...].astype(F32)).astype(BF16)
    high[...] = (own[1].astype(F32) + plus[1].astype(F32) + high_in[...].astype(F32)).astype(BF16)
    for step, out in enumerate((o0, o1, o2, o3)):
        place = lax.rem(at[index] + step, 4)
        out[0] = low[place]
        out[1] = high[place]


def add_kernel(at, right, left, plus, minus, right_out, left_out):
    right_out[...] = (right[...].astype(F32) + plus[0].astype(F32)).astype(BF16)
    left_out[...] = (left[...].astype(F32) + minus[0].astype(F32)).astype(BF16)


def ring_sums(one, two, at):
    sides = ((one, "y", 0), (two, "x", 3))
    got = [(shift(side[1], axis, 1), shift(side[2], axis, -1)) for side, axis, _ in sides]
    got = lax.optimization_barrier(got)
    shape = one[3].shape
    last = []
    for (side, axis, _), (plus, minus) in zip(sides, got, strict=True):
        right, left = call(
            add_kernel, [shape] * 2, [BF16] * 2, at, side[3], side[4], plus, minus, many=True
        )
        last.append((shift(right, axis, 1), shift(left, axis, -1)))
    last = lax.optimization_barrier(last)
    return [
        call(
            functools.partial(ring_kernel, index),
            [(2,) + shape[1:]] * 4,
            [BF16] * 4,
            at,
            side[0],
            plus,
            minus,
            low,
            high,
            scratch=[pltpu.VMEM(shape, BF16)] * 2,
            many=True,
        )
        for (side, _, index), (plus, minus), (low, high) in zip(sides, got, last, strict=True)
    ]


def sum_kernel(at, p0, p1, p2, p3, low, high):
    for level, out in enumerate((low, high)):
        total = p0[level].astype(F32) + p1[level].astype(F32)
        out[...] = (total + p2[level].astype(F32) + p3[level].astype(F32)).astype(BF16)


def scatter_rows(one, two, at):
    one, two = ring_sums(one, two, at)
    got = [
        [side[0]] + [shift(side[step], axis, step) for step in (1, 2, 3)]
        for side, axis in ((one, "x"), (two, "y"))
    ]
    got = lax.optimization_barrier(got)
    shape = one[0].shape[1:]
    one, two = (call(sum_kernel, [shape] * 2, [BF16] * 2, at, *side, many=True) for side in got)
    return one[0], shift(one[1], "z", 1), shift(two[0], "c", 1), diagonal(two[1])


def to_ring(pieces):
    return [pieces[0]] + [shift(pieces[step], "y", step) for step in (1, 2, 3)]


def half_sum(partial):
    low = partial.astype(BF16)
    return low.astype(F32) + shift(low, "t", 1).astype(F32)


def core_sum(own, other):
    return own + shift(other, "c", 1).astype(F32)


def call(kernel, shapes, dtypes, at, *operands, scratch=(), flops=1_000_000, many=False, far=0, out_far=False):
    if not many:
        shapes, dtypes = [shapes], [dtypes]
    out_shape = [jax.ShapeDtypeStruct(s, d) for s, d in zip(shapes, dtypes, strict=True)]
    moved = sum(o.size * o.dtype.itemsize for o in operands)
    moved += sum(int(np.prod(s)) * jnp.dtype(d).itemsize for s, d in zip(shapes, dtypes, strict=True))
    outs = pl.pallas_call(
        kernel,
        out_shape=out_shape,
        in_specs=[pl.BlockSpec(memory_space=pltpu.SMEM)]
        + [pl.BlockSpec(memory_space=pl.ANY)] * far
        + [pl.BlockSpec(memory_space=pltpu.VMEM)] * (len(operands) - far),
        out_specs=[pl.BlockSpec(memory_space=pl.ANY if out_far else pltpu.VMEM)] * len(out_shape),
        scratch_shapes=scratch,
        compiler_params=pltpu.CompilerParams(vmem_limit_bytes=56 * 1024 * 1024),
        cost_estimate=pl.CostEstimate(flops=flops, bytes_accessed=moved, transcendentals=0),
    )(at, *operands)
    return outs if many else outs[0]


MSG = 1024
QR = 256
KV = 384
KR = 896


def rows_at(index):
    return pl.ds(pl.multiple_of(index * 128, 128), 128)


def lanes_at(index, size, base=0):
    return pl.ds(pl.multiple_of(base + index * size, 128), size)


def owner(at, place):
    return jnp.bitwise_xor(lax.shift_right_logical(place, 1), at[2]), jnp.bitwise_and(place, 1)


def ahead(at, step):
    return lax.rem(at[3] + step, 4)


def behind(at, step):
    return lax.rem(at[3] + 4 - step, 4)


def turn(values, cosine, sine):
    return values * cosine + pltpu.roll(values, 64, 1) * sine


def project_kernel(at, *refs):
    pieces = refs[:10]
    own, other, cosine, sine, m0, m1, m2, m3, normed, low, plain, inverse = refs[10:22]
    weights, out_weights, up, tail, query, keys, key, raw, sems = refs[22:]
    copies = fetch(at, pieces, 0, weights, sems.at[0])
    later = fetch(at, pieces, 1920, raw, sems.at[1])
    last = fetch(at, pieces, 1408, out_weights, sems.at[2])
    last += fetch(at, pieces, 2176, tail, sems.at[3])
    for index, block in enumerate((own, other)):
        values = block[...].astype(F32)
        scale = lax.rsqrt(jnp.mean(values * values, axis=1, keepdims=True) + EPS)
        normed[index * 128 : index * 128 + 128] = (values * scale).astype(BF16)
    for copy in copies:
        copy.wait()
    lin = dot(normed[...], weights[...].reshape(2048, 1408))
    cos, sin = cosine[...], sine[...]
    query[:, :512] = lin[:, :512].astype(BF16)
    for pair in range(2):
        span = slice(512 + pair * 128, 640 + pair * 128)
        query[:, span] = turn(lin[:, span], cos, sin).astype(BF16)
    key[...] = turn(lin[:, 1280:], cos, sin).astype(BF16)
    latent = lin[:, 768:1280]
    scale = lax.rsqrt(jnp.mean(latent * latent, axis=1, keepdims=True) + EPS)
    latent = latent * scale
    plain[...] = latent
    low[...] = latent.astype(BF16)
    inverse[...] = jnp.broadcast_to(scale, inverse.shape)
    for copy in later:
        copy.wait()
    ups = raw[...].astype(F32).reshape(64, 4, 8, 256)
    for head in range(4):
        span = slice(head * 256, head * 256 + 256)
        up[:, span] = ups[:, head].reshape(512, 256).astype(BF16)
    keys[...] = dot(low[...], up[...]).astype(BF16)
    for step, out in enumerate((m0, m1, m2, m3)):
        block, pair = owner(at, ahead(at, step))
        rows = rows_at(block)
        out[:, :QR] = query[rows, lanes_at(pair, 256)]
        out[:, QR:KV] = query[rows, lanes_at(pair, 128, 512)]
        out[:, KV:KR] = keys[rows, lanes_at(pair, 512)]
        out[:, KR:] = key[rows, :]
    for copy in last:
        copy.wait()


def head_lanes(rows, head):
    lane = lax.broadcasted_iota(jnp.int32, (rows, 128), 1)
    return jnp.where(((lane >> 5) & 1) == head, 1.0, 0.0).astype(F32)


def head_keys(msg_ref, head):
    rotated = msg_ref[:, :, KR:].reshape(512, 128).astype(F32) * head_lanes(512, head)
    plain = msg_ref[:, :, KV + head * 256 : KV + head * 256 + 128].reshape(512, 128)
    return jnp.concatenate([plain, rotated.astype(BF16)], axis=1)


def head_values(msg_ref, head):
    return msg_ref[:, :, KV + head * 256 + 128 : KV + head * 256 + 256].reshape(512, 128)


def block_probs(query, keys, row_ref, col_ref, block):
    count = (block + 1) * 128
    scores = dot(query, keys[:count], 1, 1) * SCALE
    rows = lax.broadcasted_iota(jnp.int32, (128, count), 0) + block * 128
    cols = lax.broadcasted_iota(jnp.int32, (128, count), 1)
    same = col_ref[block * 128 : count, :] == row_ref[:, :count]
    scores = jnp.where(same & (cols <= rows), scores, -1e30)
    powers = jnp.exp(scores - jnp.max(scores, axis=1, keepdims=True))
    return powers / jnp.sum(powers, axis=1, keepdims=True)


def block_query(msg_ref, head, block):
    return jnp.concatenate(
        [msg_ref[block, :, head * 128 : head * 128 + 128], msg_ref[block, :, QR:KV]], axis=1
    )


def forward_kernel(at, m0, m1, m2, m3, row_ref, col_ref, msg_ref, o0, o1, o2, o3, mixed):
    for step, piece in enumerate((m0, m1, m2, m3)):
        msg_ref[behind(at, step)] = piece[...]
    for head in range(2):
        keys = head_keys(msg_ref, head)
        values = head_values(msg_ref, head)
        for block in range(4):
            query = block_query(msg_ref, head, block)
            probs = block_probs(query, keys, row_ref, col_ref, block)
            part = dot(probs.astype(BF16), values[: (block + 1) * 128])
            mixed[block, :, head * 128 : head * 128 + 128] = part.astype(BF16)
    for step, out in enumerate((o0, o1, o2, o3)):
        out[...] = mixed[ahead(at, step)]


def output_kernel(at, p0, p1, p2, p3, weights, attended, own, other):
    for step, piece in enumerate((p0, p1, p2, p3)):
        block, pair = owner(at, behind(at, step))
        attended[rows_at(block), lanes_at(pair, 256)] = piece[...]
    own[...] = dot(attended[:128], weights[...], 1, 1)
    other[...] = dot(attended[128:], weights[...], 1, 1).astype(BF16)


def heads_kernel(at, own, other, weights, h0, h1, h2, h3, grad):
    grad[:128] = dot(own[...], weights[...]).astype(BF16)
    grad[128:] = dot(other[...], weights[...]).astype(BF16)
    for step, out in enumerate((h0, h1, h2, h3)):
        block, pair = owner(at, ahead(at, step))
        out[...] = grad[rows_at(block), lanes_at(pair, 256)]


def backward_kernel(
    at, msg_ref, g0, g1, g2, g3, row_ref, col_ref, o0, o1, o2, o3, grad_ref, out_ref, key_acc, value_acc
):
    for step, piece in enumerate((g0, g1, g2, g3)):
        grad_ref[behind(at, step)] = piece[...]
    for head in range(2):
        keys = head_keys(msg_ref, head)
        values = head_values(msg_ref, head)
        key_acc[...] = jnp.zeros_like(key_acc)
        value_acc[...] = jnp.zeros_like(value_acc)
        lanes = head_lanes(128, head)
        for block in range(4):
            count = (block + 1) * 128
            query = block_query(msg_ref, head, block)
            probs = block_probs(query, keys, row_ref, col_ref, block)
            grad = grad_ref[block, :, head * 128 : head * 128 + 128]
            probs_grad = dot(grad, values[:count], 1, 1)
            inner = jnp.sum(probs * probs_grad, axis=1, keepdims=True)
            score_grad = (probs * (probs_grad - inner) * SCALE).astype(BF16)
            query_grad = dot(score_grad, keys[:count])
            out_ref[block, :, head * 128 : head * 128 + 128] = query_grad[:, :128].astype(BF16)
            turned = query_grad[:, 128:]
            if head == 1:
                turned = turned + out_ref[block, :, QR:KV].astype(F32)
            out_ref[block, :, QR:KV] = turned.astype(BF16)
            key_acc[:count] += dot(score_grad, query, 0, 0)
            value_acc[:count] += dot(probs.astype(BF16), grad, 0, 0)
        base = KV + head * 256
        for block in range(4):
            span = slice(block * 128, block * 128 + 128)
            out_ref[block, :, base : base + 128] = key_acc[span, :128].astype(BF16)
            out_ref[block, :, base + 128 : base + 256] = value_acc[span, :].astype(BF16)
            turned = key_acc[span, 128:] * lanes
            if head == 1:
                turned = turned + out_ref[block, :, KR:].astype(F32)
            out_ref[block, :, KR:] = turned.astype(BF16)
    for step, out in enumerate((o0, o1, o2, o3)):
        out[...] = out_ref[ahead(at, step)]


def return_kernel(
    at, b0, b1, b2, b3, weights, up, cosine, sine, plain, inverse, lin_grad, kv_grad, own, other, key
):
    for step, piece in enumerate((b0, b1, b2, b3)):
        block, pair = owner(at, behind(at, step))
        rows = rows_at(block)
        lin_grad[rows, lanes_at(pair, 256)] = piece[:, :QR]
        turned = turn(piece[:, QR:KV].astype(F32), cosine[rows, :], -sine[rows, :])
        lin_grad[rows, lanes_at(pair, 128, 512)] = turned.astype(BF16)
        kv_grad[rows, lanes_at(pair, 512)] = piece[:, KV:KR]
        key[rows_at(block + 2 * pair), :] = piece[:, KR:].astype(F32)
    turned = turn(key[:256] + key[256:], cosine[...], -sine[...])
    lin_grad[:, 1280:] = turned.astype(BF16)
    grad = dot(kv_grad[...], up[...], 1, 1)
    latent = plain[...]
    grad = inverse[:, :1] * (grad - latent * jnp.mean(grad * latent, axis=1, keepdims=True))
    lin_grad[:, 768:1280] = grad.astype(BF16)
    own[...] = dot(lin_grad[:128], weights[...], 1, 1)
    other[...] = dot(lin_grad[128:], weights[...], 1, 1).astype(BF16)


def grads_kernel(at, normed, lin_grad, own, other, attended, low, kv_grad, tail, *refs):
    own_one, plus_one, minus_one, right_one, left_one = refs[:5]
    own_two, plus_two, minus_two, right_two, left_two = refs[5:10]
    rows, ups = refs[10:]

    def store_one(place, side, column, value):
        if place == 0:
            own_one[side, column] = value
        elif place == 2:
            (plus_one, minus_one)[side][0, column] = value
        elif place == 1:
            (right_one.at[column] if side == 0 else plus_one.at[1, column])[...] = value
        else:
            (left_one.at[column] if side == 1 else minus_one.at[1, column])[...] = value

    def store_two(place, side, value):
        if place == 0:
            own_two[side] = value
        elif place == 2:
            (plus_two, minus_two)[side][0] = value
        elif place == 1:
            (right_two if side == 0 else plus_two.at[1])[...] = value
        else:
            (left_two if side == 1 else minus_two.at[1])[...] = value

    for head in range(4):
        span = slice(head * 256, head * 256 + 256)
        ups[:, head] = dot(low[...], kv_grad[:, span], 0, 0).reshape(64, 8, 256)
    for step in range(4):
        column = lax.rem(at[0] + step, 4)
        for side in range(2):
            level = at[1] if side == 0 else 1 - at[1]
            chunk = column * 2 + level
            span = pl.ds(pl.multiple_of(chunk * 256, 256), 256)
            part = dot(normed[:, span], lin_grad[...], 0, 0).astype(BF16)
            rows[:, :, :1408] = part.reshape(8, 32, 1408)
            part = dot(own[:, span], attended[:128], 0, 0) + dot(other[:, span], attended[128:], 0, 0)
            rows[:, :, 1408:1920] = part.astype(BF16).reshape(8, 32, 512)
            rows[:, :, 1920:2176] = ups[pl.ds(chunk * 8, 8)].reshape(8, 32, 256).astype(BF16)
            rows[:, :, 2176:] = tail[span, :].reshape(8, 32, 128)
            for place in range(4):
                store_one(place, side, column, rows[at[2] * 4 + ahead(at, place)])
            store_two(step, side, rows[pl.ds((1 - at[2]) * 4, 4)])


def shared_kernel(at, gathered, *refs):
    ffn_blocks, cot_blocks, kept, sent, grads = refs[:4], refs[4:8], refs[8], refs[9], refs[10]
    weights, ffn, cot, lin_grad, act, sems = refs[11:]
    copies = []
    for z in range(2):
        for core in range(2):
            copies.append(
                pltpu.make_async_copy(
                    gathered.at[:, :, z, core], weights.at[:, z, core], sems.at[2 * z + core]
                )
            )
    for copy in copies:
        copy.start()
    for i in range(4):
        ffn[i * 128 : i * 128 + 128] = ffn_blocks[i][...]
        cot[i * 128 : i * 128 + 128] = cot_blocks[i][...]
    for copy in copies:
        copy.wait()
    gate_up = weights[:, :, :, :, :, :704].reshape(2048, 704)
    down = weights[:, :, :, :, :, DOWN : DOWN + 352].reshape(2048, 352)
    lin = dot(ffn[...], gate_up)
    act_grad = dot(cot[...], down)
    up_lin = lin[:, 352:]
    silu, slope = silu_parts(lin[:, :352])
    act[...] = (silu * up_lin).astype(BF16)
    both = jnp.concatenate([act_grad * up_lin * slope, act_grad * silu], axis=1)
    lin_grad[...] = both.astype(BF16)
    back = dot(lin_grad[...], gate_up, 1, 1)
    out = dot(act[...], down, 1, 1)
    for side in range(2):
        first = side * 256
        for row, values in enumerate((back, out)):
            kept[2 * side + row] = values[first : first + 128]
            sent[2 * side + row] = values[first + 128 : first + 256].astype(BF16)
    for block in range(8):
        span = slice(block * 256, block * 256 + 256)
        part = dot(ffn[:, span], lin_grad[...], 0, 0).astype(BF16).reshape(2, 4, 32, 704)
        low = dot(cot[:, span], act[...], 0, 0).astype(BF16).reshape(2, 4, 32, 352)
        for core in range(2):
            grads[block // 2, :, block % 2, core, :, :704] = part[core]
            grads[block // 2, :, block % 2, core, :, DOWN : DOWN + 352] = low[core]
            grads[block // 2, :, block % 2, core, :, 704:DOWN] = jnp.zeros((4, 32, 64), BF16)
            grads[block // 2, :, block % 2, core, :, DOWN + 352 :] = jnp.zeros((4, 32, 32), BF16)


def finish_kernel(at, p0, p1, p2, p3, query, down, up, attn_gain, latent_gain, *outs):
    query_out, up_out, out_out, small, ffn_gain_out = outs
    own = p0[...].astype(F32) + p1[...].astype(F32)
    other = p2[...].astype(F32) + p3[...].astype(F32)
    first = at[2] == 0
    halves = [jnp.where(first, own, other), jnp.where(first, other, own)]
    heads, lifts = [], []
    for half in halves:
        for head in range(4):
            pair, place = head // 2, head % 2
            heads.append(half[:, head * 128 : head * 128 + 128])
            for side in range(2):
                start = 512 + pair * 128 + side * 64 + place * 32
                heads.append(half[:, start : start + 32])
        lifts += [half[8 * j : 8 * j + 8, 1920:2176] for j in range(4)]
    grads = jnp.concatenate(heads, axis=1)
    query_out[...] = grads * attn_gain[...].astype(F32)
    part = jnp.sum(grads * query[...].astype(F32), axis=1, keepdims=True)
    lift = jnp.concatenate(lifts, axis=1)
    up_out[...] = lift * latent_gain[...].astype(F32)
    lift_part = jnp.sum(lift * up[...].astype(F32), axis=1, keepdims=True)
    out_out[:, :512] = halves[0][:, 1408:1920]
    out_out[:, 512:] = halves[1][:, 1408:1920]
    both = own + other
    small[:, :512] = both[:, 768:1280]
    turned = jnp.concatenate(
        [
            both[:, 1280:1312] + both[:, 1312:1344],
            both[:, 1344:1376] + both[:, 1376:1408],
            both[:, 2176:2240],
        ],
        axis=1,
    )
    small[:, 512:640] = turned
    part += jnp.sum(down[:, :512].astype(F32) * both[:, 768:1280], axis=1, keepdims=True)
    part += jnp.sum(down[:, 512:].astype(F32) * turned[:, :64], axis=1, keepdims=True)
    small[:, 640:768] = jnp.broadcast_to(part, (32, 128))
    small[:, 768:] = jnp.zeros((32, 128), F32)
    small[:8, 768:] = jnp.broadcast_to(lift_part, (8, 128))
    ffn_gain_out[...] = both[:, 2240:2241]


def shared_finish_kernel(at, stay, across, beside, corner, gate, up, down):
    core, side = at[2] == 0, at[1] == 0
    own = [ref[...].astype(F32) for ref in (stay, beside)]
    other = [ref[...].astype(F32) for ref in (across, corner)]
    own = [jnp.where(side, own[0], own[1]), jnp.where(side, own[1], own[0])]
    other = [jnp.where(side, other[0], other[1]), jnp.where(side, other[1], other[0])]
    parts = [jnp.where(core, a, b) for a, b in zip(own, other, strict=True)]
    parts += [jnp.where(core, b, a) for a, b in zip(own, other, strict=True)]
    gate[...] = jnp.concatenate([part[:, :352] for part in parts], axis=1)
    up[...] = jnp.concatenate([part[:, 352:704] for part in parts], axis=1)
    down[...] = jnp.concatenate([part[:, DOWN : DOWN + 352] for part in parts], axis=1)


def doc_positions(doc_row):
    places = jnp.arange(doc_row.shape[0], dtype=jnp.int32)
    starts = jnp.concatenate([jnp.ones((1,), bool), doc_row[1:] != doc_row[:-1]])
    begins = lax.cummax(jnp.where(starts, places, 0), axis=0)
    return places - begins


def norm_back(scaled, normed, inverse):
    return inverse * (scaled - normed * jnp.mean(scaled * normed, axis=1, keepdims=True))


def silu_parts(lin):
    sig = jax.nn.sigmoid(lin)
    return lin * sig, sig * (1.0 + lin * (1.0 - sig))


def rms(values):
    return lax.rsqrt(jnp.mean(values * values, axis=1, keepdims=True) + EPS)


def shards(
    tokens_in,
    documents,
    routes,
    attn_gain,
    query_weight,
    latent_down,
    latent_gain,
    latent_up,
    output_weight,
    ffn_gain,
    router,
    shared_gate,
    shared_up,
    shared_down,
    expert_gate,
    expert_up,
    expert_down,
    cotangent,
):
    core = lax.axis_index("c")
    spot = lax.axis_index("y")
    at = jnp.stack([lax.axis_index("x"), lax.axis_index("z"), core, spot]).astype(jnp.int32)
    expert = (lax.axis_index("x") * 4 + lax.axis_index("z") * 2 + core) * 4 + spot
    rows = tokens_in.shape[0]
    width = tokens_in.shape[1]
    experts_count = router.shape[1]
    capacity = 16
    every = ("x", "z", "c", "y")

    packs = call(
        pack_kernel,
        [(32, LANES + QUARTER)] * 4,
        [BF16] * 4,
        at,
        query_weight,
        latent_down,
        latent_up,
        output_weight.T,
        shared_gate,
        shared_up,
        shared_down.T,
        router,
        attn_gain[:, None],
        latent_gain[:, None],
        ffn_gain[:, None],
        scratch=[pltpu.VMEM((2, 32, LANES), BF16), pltpu.VMEM((4, 32, QUARTER), BF16)],
        many=True,
    )
    docs = jnp.concatenate([documents, shift(documents, "c", 1)])
    lines, quarters = gather_lines(packs, at)
    lines, quarters, docs, routes, cot_early, tokens_early = lax.optimization_barrier(
        (lines, quarters, docs, routes, cotangent, tokens_in)
    )
    near = [(shift(line, axis, 1), shift(line, axis, -1)) for line, axis in zip(lines, ("y", "x"), strict=True)]

    named = jnp.any(
        routes.T[None, :, :] == jnp.arange(experts_count, dtype=jnp.int32)[:, None, None], axis=1
    )
    before = jnp.arange(rows)[:, None] < jnp.arange(rows)[None, :]
    place = dot(named.astype(BF16), before.astype(BF16))
    slots = (
        named[:, None, :] & (place[:, None, :] == jnp.arange(capacity, dtype=F32)[None, :, None])
    ).astype(BF16)
    slots = slots.reshape(experts_count * capacity, rows)

    def exchange_rows(values):
        sent = values.reshape(experts_count, capacity, -1)
        got = lax.all_to_all(sent, every, split_axis=0, concat_axis=0, tiled=True)
        return got.reshape(experts_count * capacity, -1)

    half = lax.axis_index("t")
    cot_sent = lax.dynamic_slice_in_dim(cot_early, half * 1024, 1024, axis=1)
    cot_sent = dot(slots, cot_sent).astype(BF16)
    positions = jax.vmap(doc_positions)(docs)
    local_pos = lax.dynamic_slice_in_dim(positions, spot * rows, rows, axis=1).reshape(-1)
    steps = jnp.arange(ROPE // 2, dtype=F32)
    angles = local_pos.astype(F32)[:, None] * (10000.0 ** (-steps / (ROPE // 2)))[None, :]
    cosine = jnp.tile(jnp.cos(angles), (1, 4))
    sine = jnp.sin(angles)
    sine = jnp.concatenate([-sine, -sine, sine, sine], axis=1)
    doc = jnp.where(spot // 2 == core, docs[0], docs[1])
    doc_row, doc_col = doc[None, :], doc[:, None]

    beside = shift(cot_early, "z", 1)
    across = shift(jnp.concatenate([cot_early, tokens_early]), "c", 1)
    cot_four = [cotangent, across[:rows], beside, shift(beside, "c", 1)]
    tokens_other = across[rows:]
    shared_rows = quad_order(quarters).reshape(128, QUARTER)
    near, cot_sent, slots, cosine, sine, doc_row, doc_col, shared_rows, cot_four, tokens_other = (
        lax.optimization_barrier(
            (near, cot_sent, slots, cosine, sine, doc_row, doc_col, shared_rows, cot_four, tokens_other)
        )
    )
    pieces = []
    for line, (left, right), axis in zip(lines, near, ("y", "x"), strict=True):
        pieces += [line, left, right, shift(left[0], axis, 1), shift(right[1], axis, -1)]
    cot_sent, pieces = lax.optimization_barrier((cot_sent, pieces))
    own_cot = exchange_rows(cot_sent)
    shared_all = lax.all_gather(shared_rows, ("x", "y"), axis=0, tiled=True)
    shared_all = shared_all.reshape(4, 4, 2, 2, 32, QUARTER)
    sent = [(rows, MSG)] * 4
    two = 2 * rows
    six = (4, 2, 2, 4, 32)
    outs = call(
        project_kernel,
        sent
        + [(two, width), (two, LATENT), (two, LATENT), (two, 128)]
        + [six + (1408,), six + (512,), (LATENT, 1024), six + (128,)],
        [BF16] * 6 + [F32, F32] + [BF16] * 4,
        at,
        *pieces,
        tokens_in,
        tokens_other,
        cosine,
        sine,
        scratch=[
            pltpu.VMEM((two, 768), BF16),
            pltpu.VMEM((two, 1024), BF16),
            pltpu.VMEM((two, 128), BF16),
            pltpu.VMEM(six + (256,), BF16),
            pltpu.SemaphoreType.DMA((4, 16)),
        ],
        flops=1_800_000_000,
        many=True,
        far=10,
    )
    sent, normed_low, latent_low, latent_normed, latent_inverse = outs[:4], *outs[4:8]
    in_all, out_all = outs[8].reshape(width, 1408), outs[9].reshape(width, 512)
    up_all, tail_all = outs[10], outs[11].reshape(width, 128)
    sent, own_cot = lax.optimization_barrier((sent, own_cot))
    other_cot = shift(own_cot, "t", 1)
    received = to_ring(sent)
    msg, *mixed = call(
        forward_kernel,
        [(4, rows, MSG)] + [(rows, 256)] * 4,
        [BF16] * 5,
        at,
        *received,
        doc_row,
        doc_col,
        scratch=[pltpu.VMEM((4, rows, 256), BF16)],
        flops=500_000_000,
        many=True,
    )
    mixed, other_cot = lax.optimization_barrier((to_ring(mixed), other_cot))
    attended, out_own, out_other = call(
        output_kernel,
        [(two, 512), (rows, width), (rows, width)],
        [BF16, F32, BF16],
        at,
        *mixed,
        out_all,
        flops=600_000_000,
        many=True,
    )
    tokens_f = tokens_in.astype(F32)
    resid = tokens_f + half_sum(core_sum(out_own, out_other))

    pointer = jnp.broadcast_to(jnp.arange(128)[None, :] == 64, (8, 128)).astype(BF16)
    gain_two = dot(pointer, tail_all, 1, 1)[:1]
    router_all = tail_all[:, :64]
    inverse_two = rms(resid)
    normed_two = resid * inverse_two
    ffn_in = (normed_two * gain_two).astype(BF16)
    ffn_sent = dot(slots, ffn_in).astype(BF16)
    ffn_four, ffn_sent = lax.optimization_barrier((quad_blocks(ffn_in), ffn_sent))
    expert_rows = exchange_rows(ffn_sent)

    kept, sent, shared_grads = call(
        shared_kernel,
        [(4, rows, width)] * 2 + [(4, 4, 2, 2, 32, QUARTER)],
        [F32, BF16, BF16],
        at,
        shared_all,
        *ffn_four,
        *cot_four,
        scratch=[
            pltpu.VMEM((4, 2, 2, 4, 32, QUARTER), BF16),
            pltpu.VMEM((4 * rows, width), BF16),
            pltpu.VMEM((4 * rows, width), BF16),
            pltpu.VMEM((4 * rows, 704), BF16),
            pltpu.VMEM((4 * rows, 352), BF16),
            pltpu.SemaphoreType.DMA((4,)),
        ],
        flops=7_000_000_000,
        many=True,
        far=1,
    )
    kept = kept + shift(sent, "c", 1).astype(F32)
    shared_sum = lax.psum_scatter(
        shared_grads.reshape(width, QUARTER), ("x", "y"), scatter_dimension=0, tiled=True
    ).reshape(2, 2, 32, QUARTER)
    gate_w, up_w, down_w = expert_gate[0], expert_up[0], expert_down[0]
    first_cot = jnp.where(half == 0, own_cot, other_cot)
    last_cot = jnp.where(half == 0, other_cot, own_cot)
    plain_grad = dot(first_cot, down_w[:, :1024], 1, 1) + dot(last_cot, down_w[:, 1024:], 1, 1)
    shared_back = kept[0] + shift(kept[2].astype(BF16), "z", 1).astype(F32)
    expert_rows, plain_grad, kept, shared_grads = lax.optimization_barrier(
        (expert_rows, plain_grad, kept, shared_grads)
    )
    probs = jax.nn.softmax(dot(expert_rows, router_all), axis=1)
    mine = (jnp.arange(experts_count, dtype=jnp.int32) == expert)[None, :].astype(F32)
    gate = jnp.sum(probs * mine, axis=1, keepdims=True)
    gate_lin = dot(expert_rows, gate_w)
    up_lin = dot(expert_rows, up_w)
    silu, slope = silu_parts(gate_lin)
    act = silu * up_lin
    act_low = (gate * act).astype(BF16)
    inner = jnp.sum(act * plain_grad, axis=1, keepdims=True)
    act_grad = gate * plain_grad
    gate_grad = (act_grad * up_lin * slope).astype(BF16)
    up_grad = (act_grad * silu).astype(BF16)
    logit_grad = (inner * gate * (mine - probs)).astype(BF16)
    row_grad = (
        dot(gate_grad, gate_w, 1, 1) + dot(up_grad, up_w, 1, 1) + dot(logit_grad, router_all, 1, 1)
    ).astype(BF16)
    back_rows = exchange_rows(row_grad)
    piece = dot(act_low, down_w).astype(BF16)
    expert_down_grad = jnp.concatenate(
        [dot(act_low, first_cot, 0, 0), dot(act_low, last_cot, 0, 0)], axis=1
    )[None]
    expert_gate_grad = dot(expert_rows, gate_grad, 0, 0)[None]
    expert_up_grad = dot(expert_rows, up_grad, 0, 0)[None]
    router_grad = dot(expert_rows, logit_grad, 0, 0)
    piece_own = lax.dynamic_slice_in_dim(piece, half * 1024, 1024, axis=1)
    piece_sent = lax.dynamic_slice_in_dim(piece, 1024 - half * 1024, 1024, axis=1)
    done = (back_rows, piece_own, piece_sent, expert_down_grad, expert_gate_grad, expert_up_grad, router_grad)
    done, shared_back = lax.optimization_barrier((done, shared_back))
    back_rows, piece_own, piece_sent, expert_down_grad, expert_gate_grad, expert_up_grad, router_grad = done
    routed_back = dot(slots, back_rows, 0, 0)
    cot_f = cotangent.astype(F32)
    ffn_grad = half_sum(shared_back + routed_back)
    ffn_grad, piece_sent = lax.optimization_barrier((ffn_grad, piece_sent))
    piece = add_low(piece_own, shift(piece_sent, "t", 1))
    resid_grad = cot_f + norm_back(ffn_grad * gain_two, normed_two, inverse_two)
    first_lane = jnp.broadcast_to(jnp.arange(64)[None, :] == 0, (rows, 64)).astype(BF16)
    ffn_gain_part = dot((ffn_grad * normed_two).astype(BF16), first_lane, 0, 0)

    resid_low = resid_grad.astype(BF16)
    resid_other = shift(resid_low, "c", 1)
    heads_grad = call(
        heads_kernel,
        [(rows, 256)] * 4,
        [BF16] * 4,
        at,
        resid_low,
        resid_other,
        out_all,
        scratch=[pltpu.VMEM((two, 512), BF16)],
        flops=600_000_000,
        many=True,
    )
    heads_got, shared_sum = lax.optimization_barrier((to_ring(heads_grad), shared_sum))
    own_rows, far_rows = pick(shared_sum, at[1]), pick(shared_sum, 1 - at[1])
    stay, beside = pick(own_rows, core), shift(pick(far_rows, core), "z", 1)
    across, corner = shift(pick(own_rows, 1 - core), "c", 1), diagonal(pick(far_rows, 1 - core))
    shared_gate_grad, shared_up_grad, shared_down_grad = call(
        shared_finish_kernel,
        [(32, 1408)] * 3,
        [F32] * 3,
        at,
        stay,
        across,
        beside,
        corner,
        many=True,
    )
    back = call(
        backward_kernel,
        [(rows, MSG)] * 4,
        [BF16] * 4,
        at,
        msg,
        *heads_got,
        doc_row,
        doc_col,
        scratch=[
            pltpu.VMEM((4, rows, 256), BF16),
            pltpu.VMEM((4, rows, MSG), BF16),
            pltpu.VMEM((512, 256), F32),
            pltpu.VMEM((512, 128), F32),
        ],
        flops=1_500_000_000,
        many=True,
    )
    returned, piece = lax.optimization_barrier((to_ring(back), piece))
    piece_rows = exchange_rows(piece)
    lin_grad, kv_grad, in_own, in_other = call(
        return_kernel,
        [(two, 1408), (two, 1024), (rows, width), (rows, width)],
        [BF16, BF16, F32, BF16],
        at,
        *returned,
        in_all,
        up_all,
        cosine,
        sine,
        latent_normed,
        latent_inverse,
        scratch=[pltpu.VMEM((512, 128), F32)],
        flops=1_800_000_000,
        many=True,
    )
    tail = jnp.concatenate([router_grad, ffn_gain_part], axis=1).astype(BF16)
    blocks = call(
        grads_kernel,
        ([(2, 4, 32, LANES)] * 3 + [(4, 32, LANES)] * 2) * 2,
        [BF16] * 10,
        at,
        normed_low,
        lin_grad,
        resid_low,
        resid_other,
        attended,
        latent_low,
        kv_grad,
        tail,
        scratch=[pltpu.VMEM((8, 32, 2304), BF16), pltpu.VMEM((64, 4, 8, 256), F32)],
        flops=2_200_000_000,
        many=True,
    )
    blocks, piece_rows, kept = lax.optimization_barrier((blocks, piece_rows, kept))
    attn_sum = scatter_rows(blocks[:5], blocks[5:], at)

    attn_in_grad = half_sum(core_sum(in_own, in_other))
    inverse_one = rms(tokens_f)
    input_grad = resid_grad + norm_back(attn_in_grad, tokens_f * inverse_one, inverse_one)
    routed_out = dot(slots, piece_rows, 0, 0)
    shared_out = half_sum(kept[1] + shift(kept[3].astype(BF16), "z", 1).astype(F32))
    routed_out = routed_out.astype(BF16)
    routed_other = shift(routed_out, "t", 1)
    routed_out = jnp.concatenate(
        [jnp.where(half == 0, routed_out, routed_other), jnp.where(half == 0, routed_other, routed_out)],
        axis=1,
    )
    layer_out = (resid + (shared_out + routed_out.astype(F32))).astype(BF16)

    query_out, up_out, out_out, small, ffn_gain_grad = call(
        finish_kernel,
        [(32, 1536), (8, 2048), (32, 1024), (32, 896), (32, 1)],
        [F32] * 5,
        at,
        *attn_sum,
        query_weight,
        latent_down,
        latent_up,
        attn_gain[:, None],
        latent_gain[:, None],
        many=True,
    )
    small = small + shift(small, "t", 1)
    return (
        layer_out,
        input_grad,
        small[:, 640],
        query_out,
        attn_gain.astype(F32)[:, None] * small[:, :576],
        small[:8, 768],
        up_out,
        out_out.T,
        ffn_gain_grad[:, 0],
        small[:, 576:640],
        shared_gate_grad,
        shared_up_grad,
        shared_down_grad.T,
        expert_gate_grad,
        expert_up_grad,
        expert_down_grad,
    )


def solution(mesh):
    fine = Mesh(mesh.devices.reshape(4, 2, 2, 4, 2), ("x", "z", "c", "y", "t"))
    fsdp = ("x", "z", "c")
    every = ("x", "z", "c", "y")
    in_specs = (
        P(every, None),
        P(fsdp, None),
        P(every, None),
        P(every),
        P(every, "t"),
        P(every, None),
        P(every),
        P(every, "t"),
        P("t", every),
        P(every),
        P(every, None),
        P(every, "t"),
        P(every, "t"),
        P("t", every),
        P(every, None, "t"),
        P(every, None, "t"),
        P(every, "t", None),
        P(every, None),
    )
    out_specs = (
        P(every, None),
        P(every, None),
        P(every),
        P(every, "t"),
        P(every, None),
        P(every),
        P(every, "t"),
        P("t", every),
        P(every),
        P(every, None),
        P(every, "t"),
        P(every, "t"),
        P("t", every),
        P(every, None, "t"),
        P(every, None, "t"),
        P(every, "t", None),
    )
    return jax.shard_map(shards, mesh=fine, in_specs=in_specs, out_specs=out_specs, check_vma=False)
```
